32 devices in a mesh: dp: 2 (over y), ctx: 4 (over z), tensor: 4 (over x, core).
Axes of the slice: x: 2, y: 2, z: 4, core: 2. Of those that a mesh axis runs over, the one named last changes fastest.
Arguments:
- tokens: bfloat16 [4, 1024, 2048], P('dp', 'ctx'), may hold values from -6 to 6
- out_grad: bfloat16 [4, 1024, 2048], P('dp', 'ctx'), may hold values from -6 to 6
- doc_lengths: int32 [4, 8], P('dp'), may hold values from 1 to 1017, as said below
- adapter_ids: int32 [4], P('dp'), may hold values from 0 to 7
- mixer_gain: float32 [2, 2048], replicated, may hold values from 0.5 to 1.5
- ffn_gain: float32 [2, 2048], replicated, may hold values from 0.5 to 1.5
- ssm_in: bfloat16 [2, 2048, 2, 3072], P(None, ('dp', 'ctx'), None, 'tensor'), may hold values from -0.125 to 0.125
- step_proj: bfloat16 [2, 2048, 48], P(None, ('dp', 'ctx'), 'tensor'), may hold values from -0.125 to 0.125
- query_proj: bfloat16 [2, 2048, 1024], P(None, ('dp', 'ctx'), 'tensor'), may hold values from -0.125 to 0.125
- state_proj: bfloat16 [2, 2048, 2, 256], P(None, ('dp', 'ctx')), may hold values from -0.125 to 0.125
- keyval_proj: bfloat16 [2, 2048, 2, 256], P(None, ('dp', 'ctx')), may hold values from -0.125 to 0.125
- conv_inner: float32 [2, 4, 3072], P(None, None, 'tensor'), may hold values from -3 to 3
- conv_state: float32 [2, 4, 2, 256], replicated, may hold values from -3 to 3
- decay_log: float32 [2, 48], P(None, 'tensor'), may hold values from -4 to -0.7
- step_bias: float32 [2, 48], P(None, 'tensor'), may hold values from -2.5 to -2
- skip_gain: float32 [2, 48], P(None, 'tensor'), may hold values from -4 to 4
- ssm_out: bfloat16 [2, 3072, 2048], P(None, 'tensor', ('dp', 'ctx')), may hold values from -0.0546875 to 0.0546875
- attn_out: bfloat16 [2, 1024, 2048], P(None, 'tensor', ('dp', 'ctx')), may hold values from -2.5 to 2.5
- gate_up: bfloat16 [2, 2048, 2, 4096], P(None, ('dp', 'ctx'), None, 'tensor'), may hold values from -0.125 to 0.125
- down_proj: bfloat16 [2, 4096, 2048], P(None, 'tensor', ('dp', 'ctx')), may hold values from -0.09375 to 0.09375
- mixer_shrink: bfloat16 [2, 8, 2048, 16], replicated, may hold values from -0.125 to 0.125
- inner_expand: bfloat16 [2, 8, 16, 2, 3072], P(None, None, None, None, 'tensor'), may hold values from -0.75 to 0.75
- step_expand: bfloat16 [2, 8, 16, 48], P(None, None, None, 'tensor'), may hold values from -0.75 to 0.75
- query_expand: bfloat16 [2, 8, 16, 1024], P(None, None, None, 'tensor'), may hold values from -0.75 to 0.75
- state_expand: bfloat16 [2, 8, 16, 2, 256], replicated, may hold values from -0.75 to 0.75
- keyval_expand: bfloat16 [2, 8, 16, 2, 256], replicated, may hold values from -0.75 to 0.75
- ssmout_shrink: bfloat16 [2, 8, 3072, 16], P(None, None, 'tensor'), may hold values from -0.109375 to 0.109375
- attnout_shrink: bfloat16 [2, 8, 1024, 16], P(None, None, 'tensor'), may hold values from -2.5 to 2.5
- mixer_expand: bfloat16 [2, 8, 16, 2048], replicated, may hold values from -0.75 to 0.75
- ffn_shrink: bfloat16 [2, 8, 2048, 16], replicated, may hold values from -0.125 to 0.125
- gateup_expand: bfloat16 [2, 8, 16, 2, 4096], P(None, None, None, None, 'tensor'), may hold values from -0.75 to 0.75
- down_shrink: bfloat16 [2, 8, 4096, 16], P(None, None, 'tensor'), may hold values from -0.09375 to 0.09375
- down_expand: bfloat16 [2, 8, 16, 2048], replicated, may hold values from -0.75 to 0.75
Outputs:
- output: bfloat16 [4, 1024, 2048], P('dp', 'ctx')
- input_grad: float32 [4, 1024, 2048], P('dp', 'ctx')
- mixshrink_grad: float32 [2, 8, 2048, 16], replicated
- innerexpand_grad: float32 [2, 8, 16, 2, 3072], P(None, None, None, None, 'tensor')
- stepexpand_grad: float32 [2, 8, 16, 48], P(None, None, None, 'tensor')
- queryexpand_grad: float32 [2, 8, 16, 1024], P(None, None, None, 'tensor')
- stateexpand_grad: float32 [2, 8, 16, 2, 256], replicated
- keyvalexpand_grad: float32 [2, 8, 16, 2, 256], replicated
- ssmshrink_grad: float32 [2, 8, 3072, 16], P(None, None, 'tensor')
- attnshrink_grad: float32 [2, 8, 1024, 16], P(None, None, 'tensor')
- mixexpand_grad: float32 [2, 8, 16, 2048], replicated
- ffnshrink_grad: float32 [2, 8, 2048, 16], replicated
- gateexpand_grad: float32 [2, 8, 16, 2, 4096], P(None, None, None, None, 'tensor')
- downshrink_grad: float32 [2, 8, 4096, 16], P(None, None, 'tensor')
- downexpand_grad: float32 [2, 8, 16, 2048], replicated
The draws below stay inside these ranges and needn't reach their ends.
Inputs may be any that keep to these rules, and one draw needn't show every extreme that they name: `doc_lengths`: each row sums to 1024. One document of each sequence, at a place drawn from the seed, starts before position 256 and ends after position 768; every other document holds at most 36 tokens. In the first sequence every document but that one holds exactly 1 token.
All inputs are finite; a program needn't handle non-finite values.
Results may differ from the reference program's by a relative error of at most 0.033.
Values may be sent and summed in bfloat16 or wider, within the bound.
No kernel may reach another device: no remote copies, remote signals or barrier semaphores. Data moves between devices by JAX's collectives and lax.ppermute only.
A program may use at most 384 MiB of HBM per device.

```python
import jax
import jax.numpy as jnp
from jax import lax

D = 2048
MH = 48
MP = 64
NST = 256
QH = 8
KVH = 2
HD = 128
FF = 4096
NAD = 8
RANK = 16
CONV = 4
L = 2
LEN = 1024
DOCS = 8
DSSM = 3072
SHORT = 36
SEQS = 4


def draw_doc_lengths(key, part):
    key = jax.random.fold_in(key, 11)
    first, second = jax.random.split(key)
    shorts = jax.random.randint(first, (SEQS, DOCS), 1, SHORT + 1)
    shorts = jnp.where(jnp.arange(SEQS)[:, None] == 0, 1, shorts)
    place = jax.random.randint(second, (SEQS,), 0, DOCS)
    chosen = jnp.arange(DOCS)[None, :] == place[:, None]
    others = jnp.sum(jnp.where(chosen, 0, shorts), axis=1, keepdims=True)
    return jnp.where(chosen, LEN - others, shorts).astype(jnp.int32)


def draw_skip_gain(key, part):
    key = jax.random.fold_in(key, 13)
    first = jax.random.fold_in(key, 0)
    return jax.random.uniform(first, (L, MH), jnp.float32, -4.0, 4.0)


def set_ends(entries, key, least, largest):
    dims = entries.shape
    index_at = [jax.random.randint(jax.random.fold_in(key, axis), (), 0, dims[axis]) for axis in range(len(dims))]
    entries = entries.at[tuple(index_at)].set(least)
    longest = dims.index(max(dims))
    index_at[longest] = (index_at[longest] + 1) % dims[longest]
    return entries.at[tuple(index_at)].set(largest)


def steps_of(own_key, extent, shards, smallest, high):
    def one(position, parts):
        steps = jax.random.uniform(jax.random.fold_in(jax.random.fold_in(own_key, 6), position), (parts,), jnp.float32, smallest / len(shards), high / len(shards))
        return jnp.repeat(jnp.exp(steps), extent[position] // parts).reshape((-1,) + (1,) * (len(extent) - position - 1))

    factor_of = one(*shards[0])
    for cut in shards[1:]:
        factor_of = factor_of * one(*cut)
    return factor_of


def scatter_about(stream_key, extent, scale, limit, cuts=(), kind=jnp.bfloat16):
    level = steps_of(stream_key, extent, cuts, -0.22, 0.18) if cuts else 1.0
    values = jax.random.normal(stream_key, extent, jnp.float32) * scale * level
    return jnp.minimum(jnp.maximum(values, -limit), limit).astype(kind)


def setup_inputs(seed: int = 0) -> dict:
    arg_keys = jax.random.split(jax.random.key(seed), 34)
    return {
        "tokens": scatter_about(arg_keys[0], (SEQS, LEN, D), 1.0, 6.0, ((0, 2), (1, 4))),
        "out_grad": scatter_about(arg_keys[1], (SEQS, LEN, D), 1.0, 6.0, ((0, 2), (1, 4))),
        "doc_lengths": draw_doc_lengths(jax.random.fold_in(arg_keys[33], 71), 0),
        "adapter_ids": set_ends(jax.random.randint(arg_keys[3], (SEQS,), 0, NAD), jax.random.fold_in(arg_keys[3], 1), 0, NAD - 1).astype(jnp.int32),
        "mixer_gain": jnp.clip(1.0 + 0.1 * jax.random.normal(arg_keys[4], (L, D), jnp.float32), 0.5, 1.5),
        "ffn_gain": jnp.clip(1.0 + 0.1 * jax.random.normal(arg_keys[5], (L, D), jnp.float32), 0.5, 1.5),
        "ssm_in": scatter_about(arg_keys[6], (L, D, 2, DSSM), D ** -0.5, 0.125, ((1, 8), (3, 4))),
        "step_proj": scatter_about(arg_keys[7], (L, D, MH), D ** -0.5, 0.125, ((1, 8), (2, 4))),
        "query_proj": scatter_about(arg_keys[8], (L, D, QH * HD), D ** -0.5, 0.125, ((1, 8), (2, 4))),
        "state_proj": scatter_about(arg_keys[9], (L, D, 2, NST), D ** -0.5, 0.125, ((1, 8),)),
        "keyval_proj": scatter_about(arg_keys[10], (L, D, 2, KVH * HD), D ** -0.5, 0.125, ((1, 8),)),
        "conv_inner": scatter_about(arg_keys[11], (L, CONV, DSSM), CONV ** -0.5, 3.0, ((2, 4),), jnp.float32),
        "conv_state": scatter_about(arg_keys[12], (L, CONV, 2, NST), CONV ** -0.5, 3.0, (), jnp.float32),
        "decay_log": jnp.clip(-4.0 + 3.3 * jax.random.uniform(arg_keys[13], (L, MH), jnp.float32) ** steps_of(arg_keys[13], (L, MH), ((1, 4),), -0.2, 0.2), -4.0, -0.7),
        "step_bias": jnp.clip(-2.5 + 0.5 * jax.random.uniform(arg_keys[14], (L, MH), jnp.float32) ** steps_of(arg_keys[14], (L, MH), ((1, 4),), -0.2, 0.2), -2.5, -2.0),
        "skip_gain": draw_skip_gain(jax.random.fold_in(arg_keys[33], 71), 0),
        "ssm_out": scatter_about(arg_keys[16], (L, DSSM, D), (4 * DSSM) ** -0.5, 0.0546875, ((1, 4), (2, 8))),
        "attn_out": scatter_about(arg_keys[17], (L, QH * HD, D), (QH * HD // 256 + 1) ** -0.5, 2.5, ((1, 4), (2, 8))),
        "gate_up": scatter_about(arg_keys[18], (L, D, 2, FF), D ** -0.5, 0.125, ((1, 8), (3, 4))),
        "down_proj": scatter_about(arg_keys[19], (L, FF, D), FF ** -0.5, 0.09375, ((1, 4), (2, 8))),
        "mixer_shrink": scatter_about(arg_keys[20], (L, NAD, D, RANK), D ** -0.5, 0.125),
        "inner_expand": scatter_about(arg_keys[21], (L, NAD, RANK, 2, DSSM), 64 ** -0.5, 0.75, ((4, 4),)),
        "step_expand": scatter_about(arg_keys[22], (L, NAD, RANK, MH), 64 ** -0.5, 0.75, ((3, 4),)),
        "query_expand": scatter_about(arg_keys[23], (L, NAD, RANK, QH * HD), 64 ** -0.5, 0.75, ((3, 4),)),
        "state_expand": scatter_about(arg_keys[24], (L, NAD, RANK, 2, NST), 64 ** -0.5, 0.75),
        "keyval_expand": scatter_about(arg_keys[25], (L, NAD, RANK, 2, KVH * HD), 64 ** -0.5, 0.75),
        "ssmout_shrink": scatter_about(arg_keys[26], (L, NAD, DSSM, RANK), DSSM ** -0.5, 0.109375, ((2, 4),)),
        "attnout_shrink": scatter_about(arg_keys[27], (L, NAD, QH * HD, RANK), (QH * HD // 256 + 1) ** -0.5, 2.5, ((2, 4),)),
        "mixer_expand": scatter_about(arg_keys[28], (L, NAD, RANK, D), 64 ** -0.5, 0.75),
        "ffn_shrink": scatter_about(arg_keys[29], (L, NAD, D, RANK), D ** -0.5, 0.125),
        "gateup_expand": scatter_about(arg_keys[30], (L, NAD, RANK, 2, FF), 64 ** -0.5, 0.75, ((4, 4),)),
        "down_shrink": scatter_about(arg_keys[31], (L, NAD, FF, RANK), FF ** -0.5, 0.09375, ((2, 4),)),
        "down_expand": scatter_about(arg_keys[32], (L, NAD, RANK, D), 64 ** -0.5, 0.75),
    }


EPS = 1e-05
ROPE_BASE = 10000.0
HIGHEST = lax.Precision.HIGHEST

@jax.custom_vjp
def low(v):
    return lax.optimization_barrier(v.astype(jnp.bfloat16)).astype(jnp.float32)

@jax.custom_vjp
def low_back(v):
    return v

def low_keep(v):
    return (low(v), None)

def low_pass(kept, grad):
    return (grad,)

def back_keep(v):
    return (v, None)

def back_low(kept, grad):
    return (low(grad),)
low.defvjp(low_keep, low_pass)
low_back.defvjp(back_keep, back_low)

def matmul(left, right):
    return jnp.dot(left, right, precision=HIGHEST, preferred_element_type=jnp.float32)

def rms_norm(stream, gain):
    return stream * lax.rsqrt(lax.optimization_barrier(jnp.mean(stream * stream, axis=-1, keepdims=True)) + EPS) * gain

def segment_of(positions, lengths):
    ends = jnp.cumsum(lengths)
    inside = lax.optimization_barrier(jnp.sum((positions[:, None] >= ends[None, :]).astype(jnp.int32), axis=1))
    return jnp.where(positions < 0, -1, inside).astype(jnp.int32)

def rotary(values, positions):
    half = values.shape[-1] // 2
    freqs = ROPE_BASE ** (-jnp.arange(half, dtype=jnp.float32) / half)
    angles = positions.astype(jnp.float32)[:, None] * freqs[None, :]
    cosine = jnp.cos(angles)[:, None, :]
    sine = jnp.sin(angles)[:, None, :]
    first = values[..., :half]
    second = values[..., half:]
    return jnp.concatenate([first * cosine - second * sine, second * cosine + first * sine], axis=-1)

def causal_conv(extended, seg_ext, taps):
    reach = taps.shape[0] - 1
    count = extended.shape[1] - reach
    seg_here = seg_ext[:, reach:]
    total = jnp.zeros((extended.shape[0], count, extended.shape[2]), jnp.float32)
    for offset in range(taps.shape[0]):
        start = reach - offset
        same = (seg_ext[:, start:start + count] == seg_here).astype(jnp.float32)
        total = total + taps[offset] * extended[:, start:start + count, :] * same[..., None]
    return jax.nn.silu(total)

def span_masks(segs, seg_before):
    count = segs.shape[1]
    causal = jnp.tril(jnp.ones((count, count), dtype=bool))
    allowed = (segs[:, :, None] == segs[:, None, :]) & causal[None]
    carry_in = (segs == seg_before[:, None]).astype(jnp.float32)
    tail = (segs == segs[:, -1:]).astype(jnp.float32)
    return (allowed, carry_in, tail)

def span_summary(inner, state_b, step, rate, carry_in, tail):
    cum = jnp.cumsum(-rate * step, axis=1)
    weight = jnp.exp(cum[:, -1:, :] - cum) * tail[..., None]
    weighted = inner * (step * weight)[..., None]
    local = jnp.einsum('sjn,sjhp->shnp', state_b, weighted, precision=HIGHEST)
    total = jnp.exp(cum[:, -1, :]) * carry_in[:, -1:]
    return (total, local)

def span_output(inner, state_b, state_c, step, state_in, rate, skip, allowed, carry_in):
    cum = jnp.cumsum(-rate * step, axis=1)
    diff = cum[:, :, None, :] - cum[:, None, :, :]
    keep = allowed[..., None]
    decay = jnp.where(keep, jnp.exp(jnp.where(keep, diff, 0.0)), 0.0)
    scores = jnp.einsum('sin,sjn->sij', state_c, state_b, precision=HIGHEST)
    mixing = scores[..., None] * decay
    direct = jnp.einsum('sijh,sjhp->sihp', mixing, inner * step[..., None], precision=HIGHEST)
    prior = jnp.einsum('sin,shnp->sihp', state_c, state_in, precision=HIGHEST)
    prior = prior * (jnp.exp(cum) * carry_in[..., None])[..., None]
    return direct + prior + skip[:, None] * inner

def ssm_sequence(inner, state_b, state_c, step, segs, rate, skip):
    block = min(128, LEN)
    blocks = LEN // block
    before = jnp.concatenate([jnp.full((1,), -1, jnp.int32), segs[:-1]])
    items = (inner.reshape(blocks, block, MH, MP), state_b.reshape(blocks, block, NST), state_c.reshape(blocks, block, NST), step.reshape(blocks, block, MH), segs.reshape(blocks, block), before.reshape(blocks, block)[:, 0])

    def advance(state, item):
        inner_b, b_part, c_part, step_b, seg_b, first_before = item
        allowed, carry_in, tail = span_masks(seg_b[None], first_before[None])
        out = span_output(inner_b[None], b_part[None], c_part[None], step_b[None], state[None], rate, skip, allowed, carry_in)
        total, local = span_summary(inner_b[None], b_part[None], step_b[None], rate, carry_in, tail)
        return (total[0][:, None, None] * state + local[0], out[0])
    _, outs = lax.scan(jax.checkpoint(advance), jnp.zeros((MH, NST, MP), jnp.float32), items)
    return outs.reshape(LEN, MH, MP)

def attention(query_rot, key_rot, value_low, segs, positions):
    group = QH // KVH
    keys = jnp.repeat(key_rot, group, axis=1)
    values = jnp.repeat(value_low, group, axis=1)
    scores = low_back(jnp.einsum('qhd,khd->hqk', query_rot, keys, precision=HIGHEST) * HD ** (-0.5))
    allowed = (positions[:, None] >= positions[None, :]) & (segs[:, None] == segs[None, :])
    masked = jnp.where(allowed[None], scores, -1e+30)
    weights = low(jax.nn.softmax(masked, axis=-1))
    return jnp.einsum('hqk,khd->qhd', weights, values, precision=HIGHEST).reshape(LEN, QH * HD)

def layer_forward(stream, segs, positions, aid, frozen, train, layer):
    mixer_gain, ffn_gain, ssm_in, step_proj, query_proj, state_proj, keyval_proj, conv_inner, conv_state, decay_log, step_bias, skip_gain, ssm_out, attn_out, gate_up, down_proj = frozen
    mixer_shrink, inner_expand, step_expand, query_expand, state_expand, keyval_expand, ssmout_shrink, attnout_shrink, mixer_expand, ffn_shrink, gateup_expand, down_shrink, down_expand = train

    def select(table):
        return table[layer][aid]
    normed = low(rms_norm(stream, mixer_gain[layer]))
    rank_in = low_back(low(matmul(normed, select(mixer_shrink))))
    inner_raw = low_back(matmul(normed, ssm_in[layer].reshape(D, 2 * DSSM)) + matmul(rank_in, select(inner_expand).reshape(RANK, 2 * DSSM)))
    gate_z = inner_raw[:, :DSSM]
    inner_x = inner_raw[:, DSSM:]
    step_raw = low_back(matmul(normed, step_proj[layer]) + matmul(rank_in, select(step_expand)))
    query = low_back(matmul(normed, query_proj[layer]) + matmul(rank_in, select(query_expand)))
    states = low_back(matmul(normed, state_proj[layer].reshape(D, 2 * NST)) + matmul(rank_in, select(state_expand).reshape(RANK, 2 * NST)))
    keyval = low_back(matmul(normed, keyval_proj[layer].reshape(D, 2 * KVH * HD)) + matmul(rank_in, select(keyval_expand).reshape(RANK, 2 * KVH * HD)))
    conv_in = jnp.concatenate([inner_x, states], axis=-1)
    taps = jnp.concatenate([conv_inner[layer], conv_state[layer].reshape(CONV, 2 * NST)], axis=-1)
    extended = jnp.concatenate([jnp.zeros((CONV - 1, conv_in.shape[1]), jnp.float32), conv_in], axis=0)[None]
    seg_ext = jnp.concatenate([jnp.full((CONV - 1,), -1, jnp.int32), segs])[None]
    conv_out = causal_conv(extended, seg_ext, taps)[0]
    inner = conv_out[:, :DSSM].reshape(LEN, MH, MP)
    state_b = conv_out[:, DSSM:DSSM + NST]
    state_c = conv_out[:, DSSM + NST:]
    step = jax.nn.softplus(step_raw + step_bias[layer])
    ssm = ssm_sequence(inner, state_b, state_c, step, segs, jnp.exp(decay_log[layer]), skip_gain[layer])
    gated = low_back(low(ssm.reshape(LEN, DSSM) * jax.nn.silu(gate_z)))
    query_rot = low(rotary(query.reshape(LEN, QH, HD), positions))
    key_rot = low(rotary(keyval[:, :KVH * HD].reshape(LEN, KVH, HD), positions))
    value_low = low(keyval[:, KVH * HD:].reshape(LEN, KVH, HD))
    attended = low_back(low(jax.checkpoint(attention)(query_rot, key_rot, value_low, segs, positions)))
    out_rank = low_back(low(matmul(gated, select(ssmout_shrink)) + matmul(attended, select(attnout_shrink))))
    mixed = low_back(matmul(gated, ssm_out[layer]) + matmul(attended, attn_out[layer]) + matmul(out_rank, select(mixer_expand)))
    stream = stream + mixed
    normed_two = low(rms_norm(stream, ffn_gain[layer]))
    rank_ffn = low_back(low(matmul(normed_two, select(ffn_shrink))))
    pair_expand = select(gateup_expand)
    gate_val = low_back(matmul(normed_two, gate_up[layer][:, 0]) + matmul(rank_ffn, pair_expand[:, 0]))
    up_val = low_back(matmul(normed_two, gate_up[layer][:, 1]) + matmul(rank_ffn, pair_expand[:, 1]))
    hidden = low(jax.nn.silu(gate_val) * up_val)
    down_rank = low_back(low(matmul(hidden, select(down_shrink))))
    down_val = low_back(matmul(hidden, down_proj[layer]) + matmul(down_rank, select(down_expand)))
    return stream + down_val

def reference(tokens, out_grad, doc_lengths, adapter_ids, mixer_gain, ffn_gain, ssm_in, step_proj, query_proj, state_proj, keyval_proj, conv_inner, conv_state, decay_log, step_bias, skip_gain, ssm_out, attn_out, gate_up, down_proj, mixer_shrink, inner_expand, step_expand, query_expand, state_expand, keyval_expand, ssmout_shrink, attnout_shrink, mixer_expand, ffn_shrink, gateup_expand, down_shrink, down_expand):
    frozen = tuple((w.astype(jnp.float32) for w in (mixer_gain, ffn_gain, ssm_in, step_proj, query_proj, state_proj, keyval_proj, conv_inner, conv_state, decay_log, step_bias, skip_gain, ssm_out, attn_out, gate_up, down_proj)))
    train = tuple((w.astype(jnp.float32) for w in (mixer_shrink, inner_expand, step_expand, query_expand, state_expand, keyval_expand, ssmout_shrink, attnout_shrink, mixer_expand, ffn_shrink, gateup_expand, down_shrink, down_expand)))
    positions = jnp.arange(LEN, dtype=jnp.int32)

    def forward(stream, tables):

        def one_sequence(item):
            seq_stream, lengths, aid = item
            segs = segment_of(positions, lengths)
            for layer in range(L):
                seq_stream = layer_forward(seq_stream, segs, positions, aid, frozen, tables, layer)
            return seq_stream
        return lax.map(one_sequence, (stream, doc_lengths, adapter_ids))
    result, pullback = jax.vjp(forward, tokens.astype(jnp.float32), train)
    grad_in, grads = pullback(out_grad.astype(jnp.float32))
    return (result.astype(jnp.bfloat16), grad_in, grads[0], grads[1], grads[2], grads[3], grads[4], grads[5], grads[6], grads[7], grads[8], grads[9], grads[10], grads[11], grads[12])
```

```python
import functools

import jax
import jax.numpy as jnp
from jax import lax
from jax.experimental import pallas as pl
from jax.experimental.pallas import tpu as pltpu
from jax.sharding import Mesh
from jax.sharding import PartitionSpec as P

HD = 128
CONV = 4
EPS = 1e-05
ROPE_BASE = 10000.0
HIGHEST = lax.Precision.HIGHEST
BF = jnp.bfloat16
F32 = jnp.float32
TOK = ("ta", "zl", "tb")
ROWS = 512
COST = 1000
VMEM = 56 * 1024 * 1024


def dot(a, b, **kw):
    return jnp.dot(a, b, preferred_element_type=F32, **kw)


def dot_nt(a, b):
    return lax.dot_general(a, b, (((1,), (1,)), ((), ())), preferred_element_type=F32)


def dot_tn(a, b):
    return lax.dot_general(a, b, (((0,), (0,)), ((), ())), preferred_element_type=F32)


def sigmoid(v):
    return 1.0 / (1.0 + jnp.exp(-v))


def swap(value, axis):
    return lax.ppermute(value, axis, [(0, 1), (1, 0)])


def rms_norm(stream, gain):
    return stream * lax.rsqrt(jnp.mean(stream * stream, axis=-1, keepdims=True) + EPS) * gain


def norm_back(stream, gain, upstream):
    scale = lax.rsqrt(jnp.mean(stream * stream, axis=-1, keepdims=True) + EPS)
    weighted = upstream * gain
    inner = jnp.mean(stream * weighted, axis=-1, keepdims=True)
    return scale * weighted - stream * (scale * scale * scale * inner)


def segment_of(positions, lengths):
    ends = jnp.cumsum(lengths)
    inside = jnp.sum((positions[:, None] >= ends[None, :]).astype(jnp.int32), axis=1)
    return jnp.where(positions < 0, -1, inside)


def gather_tokens(own):
    return lax.all_gather(own, TOK, axis=0, tiled=True)


def scatter_stages(keep, send, *tokens):
    b, half = keep.shape[0] // 4, keep.shape[1] // 2
    recv = swap(later(send, *tokens), "tb")
    tokens = yield [recv]

    def pair(rows, cols):
        return keep[rows, cols].astype(F32) + recv[rows, cols].astype(F32)

    first, second = slice(0, half), slice(half, 2 * half)

    def odd(cols, k):
        return jnp.concatenate([pair(slice(k * b, k * b + b), cols), pair(slice((k + 2) * b, (k + 3) * b), cols)], axis=0)

    got_a = swap(later(pair(slice(2 * b, 4 * b), first).astype(BF), *tokens), "ta")
    got_b = swap(later(odd(second, 1).astype(BF), *tokens), "zl")
    tokens = yield [got_a, got_b]
    sum_a = pair(slice(0, 2 * b), first) + got_a.astype(F32)
    sum_b = odd(second, 0) + got_b.astype(F32)
    last_a = swap(later(sum_a[b:].astype(BF), *tokens), "zl")
    last_b = swap(later(sum_b[b:].astype(BF), *tokens), "ta")
    yield [last_a, last_b]
    return jnp.concatenate([sum_a[:b] + last_a.astype(F32), sum_b[:b] + last_b.astype(F32)], axis=1)


def scatter_tokens(keep, send):
    return Stages(scatter_stages(keep, send)).finish()


class Stages:
    def __init__(self, chain):
        self.chain, self.begun, self.result = chain, False, None

    def start(self, *tokens):
        try:
            if self.begun:
                return self.chain.send(tokens)
            self.begun = True
            return next(self.chain)
        except StopIteration as end:
            self.result = end.value
            return None

    def finish(self):
        while self.start() is not None:
            pass
        return self.result


def later(value, *tokens):
    return tied(value, *tokens)[0] if tokens else value


def tied(*values):
    return lax.optimization_barrier(values)


def blocks_of(me_ref, parts, rows):
    out, j = [], 0
    for part in parts:
        for k in range(part.shape[0] // rows):
            at = pl.multiple_of((j ^ me_ref[0]) * rows, rows)
            out.append((part.at[pl.ds(k * rows, rows), :], pl.ds(at, rows)))
            j += 1
    return out


def weight_copies(me_ref, parts, held, sem):
    rows = held.shape[0] // sem.shape[0]
    return [
        pltpu.make_async_copy(block, held.at[at, :], sem.at[j]) for j, (block, at) in enumerate(blocks_of(me_ref, parts, rows))
    ]


def load_weight(me_ref, parts, held, sem):
    copies = weight_copies(me_ref, parts, held, sem)
    for copy in copies:
        copy.start()
    for copy in copies:
        copy.wait()


def load_ffn(me_ref, gates, ups, downs, held, dheld, sem):
    half = dheld.shape[1]
    copies = weight_copies(me_ref, gates, held.at[:, pl.ds(0, half)], sem.at[0])
    copies += weight_copies(me_ref, ups, held.at[:, pl.ds(half, half)], sem.at[1])
    copies += weight_copies(me_ref, downs, dheld, sem.at[2])
    for copy in copies:
        copy.start()
    for copy in copies:
        copy.wait()


def load_mixer(me_ref, parts, far_kv, far_bc, held, sem):
    rows = held.shape[0] // sem.shape[1]
    states = far_bc.shape[1]
    inner = (held.shape[1] - 3 * HD - 2 * states) // 2
    core = me_ref[3]

    def key(which):
        return pl.ds(pl.multiple_of(2 * inner + HD + which * HD, HD), HD)

    def state(which):
        return pl.ds(pl.multiple_of(2 * inner + 3 * HD + which * states, HD), states)

    first, second, third = (blocks_of(me_ref, part, rows) for part in parts)
    copies = []
    for j, ((one, at), (two, _), (three, _)) in enumerate(zip(first, second, third)):
        here = pl.ds(j * rows, rows)
        for k, (source, cols) in enumerate(
            (
                (one.at[:, pl.ds(0, inner)], pl.ds(0, inner)),
                (one.at[:, pl.ds(inner, HD)], pl.ds(2 * inner, HD)),
                (two.at[:, pl.ds(0, inner)], pl.ds(inner, inner)),
                (two.at[:, pl.ds(inner, HD)], key(core)),
                (three, state(core)),
                (far_kv.at[here, :], key(1 - core)),
                (far_bc.at[here, :], state(1 - core)),
            )
        ):
            copies.append(pltpu.make_async_copy(source, held.at[at, cols], sem.at[k, j]))
    for copy in copies:
        copy.start()
    for copy in copies:
        copy.wait()


def emit(me_ref, keep_ref, send_ref, cols, value):
    b = value.shape[0] // 4
    low = value.astype(BF)
    for z in range(2):
        one, two = low[2 * z * b : (2 * z + 1) * b], low[(2 * z + 1) * b : (2 * z + 2) * b]
        at = pl.ds(pl.multiple_of((z ^ me_ref[2]) * b, b), b)
        first = jnp.full(one.shape, me_ref[3]) == 0
        keep_ref[at, cols] = jnp.where(first, one, two)
        send_ref[at, cols] = jnp.where(first, two, one)


def in_kernel(me_ref, h_ref, shrink_ref, expand_ref, cos_ref, sin_ref, stepw_ref, far_kv, far_bc, *rest):
    parts, rest = (rest[0:2], rest[2:4], rest[4:6]), rest[6:]
    zx_ref, bc_ref, qkv_ref, step_ref, rank_ref, held, sem = rest
    inner = zx_ref.shape[1]
    state = bc_ref.shape[1] // 2

    @pl.when(pl.program_id(0) == 0)
    def _():
        load_mixer(me_ref, parts, far_kv, far_bc, held, sem)

    h = h_ref[...]
    rank = dot_nt(h, shrink_ref[...]).astype(BF)
    rank_ref[...] = rank

    def part(at, width):
        cols = slice(at, at + width)
        return dot(h, held[:, cols]) + dot(rank, expand_ref[:, cols])

    for at in range(0, inner, 256):
        zx_ref[:, at : at + 256] = part(at, 256).astype(BF)
    qk = part(inner, 2 * HD)
    cos, sin = cos_ref[...], sin_ref[...]
    for k in range(2):
        head = qk[:, k * HD : (k + 1) * HD]
        turned = head * cos + pltpu.roll(head, HD // 2, 1) * sin
        qkv_ref[:, k * HD : (k + 1) * HD] = turned.astype(BF)
    qkv_ref[:, 2 * HD :] = part(inner + 2 * HD, HD).astype(BF)
    for k in range(2):
        bc_ref[:, k * state : (k + 1) * state] = part(inner + 3 * HD + k * state, state).astype(BF)
    step_ref[...] = dot_nt(h, stepw_ref[...]) + dot(rank, expand_ref[:, held.shape[1] :])


def in_back_kernel(
    me_ref, dzx_ref, dbc_ref, dqkv_ref, dstep_ref, h_ref, rank_ref, shrink_ref, expand_ref, stepw_ref, far_kv, far_bc, *rest
):
    parts, rest = (rest[0:2], rest[2:4], rest[4:6]), rest[6:]
    keep_ref, send_ref, gexpand_ref, gshrink_ref, held, du, sem = rest
    inner = dzx_ref.shape[1]

    @pl.when(pl.program_id(0) == 0)
    def _():
        load_mixer(me_ref, parts, far_kv, far_bc, held, sem)
        gexpand_ref[...] = jnp.zeros_like(gexpand_ref)
        gshrink_ref[...] = jnp.zeros_like(gshrink_ref)

    most = held.shape[1]
    du[:, :inner] = dzx_ref[...]
    du[:, inner : inner + 3 * HD] = dqkv_ref[...]
    du[:, inner + 3 * HD : most] = dbc_ref[...]
    du[:, most:] = dstep_ref[...]
    rank = rank_ref[...]
    drank = dot_nt(du[...], expand_ref[...]).astype(BF)
    for at in range(0, du.shape[1], 256):
        cols = slice(at, at + 256)
        gexpand_ref[:, cols] += dot_tn(rank, du[:, cols])
    for at in range(0, h_ref.shape[1], 256):
        cols = slice(at, at + 256)
        value = dot_nt(du[:, :most], held[cols, :]) + dot(du[:, most:], stepw_ref[:, cols]) + dot(drank, shrink_ref[:, cols])
        emit(me_ref, keep_ref, send_ref, cols, value)
        gshrink_ref[:, cols] += dot_tn(drank, h_ref[:, cols])


def out_kernel(me_ref, g_ref, o_ref, shrink_ref, expand_ref, *rest):
    pieces, rest = rest[:2], rest[2:]
    keep_ref, send_ref, rank_ref, held, go, sem = rest

    @pl.when(pl.program_id(0) == 0)
    def _():
        load_weight(me_ref, pieces, held, sem)

    inner = g_ref.shape[1]
    go[:, :inner] = g_ref[...]
    go[:, inner:] = o_ref[...]
    rank = dot_nt(go[...], shrink_ref[...]).astype(BF)
    rank_ref[...] = rank
    for at in range(0, expand_ref.shape[1], 256):
        cols = slice(at, at + 256)
        emit(me_ref, keep_ref, send_ref, cols, dot_nt(go[...], held[cols, :]) + dot(rank, expand_ref[:, cols]))


def out_back_kernel(me_ref, ml_ref, g_ref, o_ref, rank_ref, shrink_ref, expand_ref, *rest):
    pieces, rest = rest[:2], rest[2:]
    dg_ref, do_ref, gexpand_ref, gshrink_ref, held, sem = rest

    @pl.when(pl.program_id(0) == 0)
    def _():
        load_weight(me_ref, pieces, held, sem)
        gexpand_ref[...] = jnp.zeros_like(gexpand_ref)
        gshrink_ref[...] = jnp.zeros_like(gshrink_ref)

    inner = g_ref.shape[1]
    ml = ml_ref[...]
    drank = dot_nt(ml, expand_ref[...]).astype(BF)
    for at in range(0, held.shape[1], 128):
        cols = slice(at, at + 128)
        got = (dot(ml, held[:, cols]) + dot(drank, shrink_ref[:, cols])).astype(BF)
        if at < inner:
            dg_ref[:, cols] = got
            gshrink_ref[:, cols] += dot_tn(drank, g_ref[:, cols])
        else:
            do_ref[:, at - inner : at - inner + 128] = got
            gshrink_ref[:, cols] += dot_tn(drank, o_ref[:, at - inner : at - inner + 128])
    rank = rank_ref[...]
    for at in range(0, ml.shape[1], 256):
        cols = slice(at, at + 256)
        gexpand_ref[:, cols] += dot_tn(rank, ml_ref[:, cols])


def ffn_kernel( me_ref, h_ref, shrink_ref, expand_ref, dshrink_ref, dexpand_ref, *rest):
    (gates, ups, downs), rest = (rest[0:2], rest[2:4], rest[4:6]), rest[6:]
    keep_ref, send_ref, gu_ref, q_ref, rank_ref, drank_ref, held, dheld, sem = rest

    @pl.when(pl.program_id(0) == 0)
    def _():
        load_ffn(me_ref, gates, ups, downs, held, dheld, sem)

    h = h_ref[...]
    half = q_ref.shape[1]
    rank = dot_nt(h, shrink_ref[...]).astype(BF)
    rank_ref[...] = rank
    for start in range(0, half, 256):
        one = slice(start, start + 256)
        two = slice(half + start, half + start + 256)
        gate = dot(h, held[:, one]) + dot(rank, expand_ref[:, one])
        up = dot(h, held[:, two]) + dot(rank, expand_ref[:, two])
        gu_ref[:, one] = gate.astype(BF)
        gu_ref[:, two] = up.astype(BF)
        q_ref[:, one] = (gate * sigmoid(gate) * up).astype(BF)
    q = q_ref[...]
    drank = dot_nt(q, dshrink_ref[...]).astype(BF)
    drank_ref[...] = drank
    for start in range(0, dexpand_ref.shape[1], 256):
        cols = slice(start, start + 256)
        emit(me_ref, keep_ref, send_ref, cols, dot_nt(q, dheld[cols, :]) + dot(drank, dexpand_ref[:, cols]))


def ffn_back_kernel(
    me_ref, dl_ref, h_ref, gu_ref, q_ref, rank_ref, drank_ref, shrink_ref, expand_ref, dshrink_ref, dexpand_ref, *rest
):
    (gates, ups, downs), rest = (rest[0:2], rest[2:4], rest[4:6]), rest[6:]
    keep_ref, send_ref, gshrink_ref, gexpand_ref, gdshrink_ref, gdexpand_ref, held, dheld, dgu, sem = rest

    @pl.when(pl.program_id(0) == 0)
    def _():
        load_ffn(me_ref, gates, ups, downs, held, dheld, sem)
        for ref in (gshrink_ref, gexpand_ref, gdshrink_ref, gdexpand_ref):
            ref[...] = jnp.zeros_like(ref)

    dl = dl_ref[...]
    half = q_ref.shape[1]
    ddrank = dot_nt(dl, dexpand_ref[...]).astype(BF)
    down_rank = drank_ref[...]
    for start in range(0, dl.shape[1], 256):
        cols = slice(start, start + 256)
        gdexpand_ref[:, cols] += dot_tn(down_rank, dl_ref[:, cols])
    rank = rank_ref[...]
    for start in range(0, half, 256):
        one = slice(start, start + 256)
        two = slice(half + start, half + start + 256)
        dq = dot(dl, dheld[:, one]) + dot(ddrank, dshrink_ref[:, one])
        gate = gu_ref[:, one].astype(F32)
        up = gu_ref[:, two].astype(F32)
        sig = sigmoid(gate)
        dgu[:, one] = (dq * up * sig * (1.0 + gate * (1.0 - sig))).astype(BF)
        dgu[:, two] = (dq * gate * sig).astype(BF)
        gdshrink_ref[:, one] += dot_tn(ddrank, q_ref[:, one])
        gexpand_ref[:, one] += dot_tn(rank, dgu[:, one])
        gexpand_ref[:, two] += dot_tn(rank, dgu[:, two])
    drank = dot_nt(dgu[...], expand_ref[...]).astype(BF)
    for start in range(0, h_ref.shape[1], 256):
        cols = slice(start, start + 256)
        emit(me_ref, keep_ref, send_ref, cols, dot_nt(dgu[...], held[cols, :]) + dot(drank, shrink_ref[:, cols]))
        gshrink_ref[:, cols] += dot_tn(drank, h_ref[:, cols])


def attend(q, k, v, place_q, seg_q, place_k, seg_k):
    scores = dot_nt(q, k) * HD ** (-0.5)
    seen = (place_q >= place_k) & (seg_q == seg_k)
    masked = jnp.where(seen, scores, -1e30)
    top = jnp.max(masked, axis=-1, keepdims=True)
    raised = jnp.exp(masked - top)
    probs = raised * (1.0 / jnp.sum(raised, axis=-1, keepdims=True))
    low = probs.astype(BF)
    return probs, low, dot(low, v)


def attn_kernel(q_ref, k_ref, v_ref, col_ref, row_ref, o_ref):
    _, _, out = attend(
        q_ref[...], k_ref[...], v_ref[...], col_ref[:, 6:7], col_ref[:, 5:6], row_ref[1:2, :], row_ref[0:1, :]
    )
    o_ref[...] = out.astype(BF)


def attn_back_kernel(
    q_ref, k_ref, v_ref, col_ref, row_ref, do_ref, cos_ref, sin_ref, cosk_ref, sink_ref, dq_ref, dk_ref, dv_ref, dk_sum, dv_sum
):
    step = pl.program_id(0)

    @pl.when(step == 0)
    def _():
        dk_sum[...] = jnp.zeros_like(dk_sum)
        dv_sum[...] = jnp.zeros_like(dv_sum)

    q, k, v, do = q_ref[...], k_ref[...], v_ref[...], do_ref[...]
    probs, low, out = attend(q, k, v, col_ref[:, 6:7], col_ref[:, 5:6], row_ref[1:2, :], row_ref[0:1, :])
    delta = jnp.sum(do.astype(F32) * out, axis=-1, keepdims=True)
    ds = (probs * (dot_nt(do, v) - delta)).astype(BF)

    def back(turned, cos, sin):
        return (turned * cos - pltpu.roll(turned, HD // 2, 1) * sin) * HD ** (-0.5)

    dq_ref[...] = back(dot(ds, k), cos_ref[...], sin_ref[...]).astype(BF)
    dk_sum[...] += dot_tn(ds, q)
    dv_sum[...] += dot_tn(low, do)

    @pl.when(step == pl.num_programs(0) - 1)
    def _():
        dk_ref[...] = back(dk_sum[...], cosk_ref[...], sink_ref[...]).astype(BF)
        dv_ref[...] = dv_sum[...].astype(BF)


def spread(cols, first, pairs):
    rows = cols.shape[0]
    low = lax.broadcasted_iota(jnp.int32, (rows, 128), 1) < 64
    return jnp.concatenate(
        [
            jnp.where(low, cols[:, first + 2 * p : first + 2 * p + 1], cols[:, first + 2 * p + 1 : first + 2 * p + 2])
            for p in range(pairs)
        ],
        axis=1,
    )


def span(zx_ref, zxp_ref, bc_ref, bcp_ref, step_ref, col_ref, row_ref, taps_ref, heads_ref, ext):
    count, inner2 = zx_ref.shape
    inner = inner2 // 2
    states = bc_ref.shape[1]
    pairs = inner // 128
    ext[0:8, :inner] = zxp_ref[8:16, inner:].astype(F32)
    ext[0:8, inner:] = bcp_ref[8:16, :].astype(F32)
    ext[8:, :inner] = zx_ref[:, inner:].astype(F32)
    ext[8:, inner:] = bc_ref[...].astype(F32)
    pre = taps_ref[0:1, :] * ext[8:, :]
    for k in range(1, CONV):
        pre = pre + taps_ref[k : k + 1, :] * (ext[8 - k : 8 - k + count, :] * col_ref[:, k : k + 1])
    sig = sigmoid(pre)
    conv = pre * sig
    x = conv[:, :inner]
    b = conv[:, inner : inner + states // 2].astype(BF)
    c = conv[:, inner + states // 2 :].astype(BF)
    raw = step_ref[...] + heads_ref[0:1, :]
    dt = jnp.maximum(raw, 0.0) + jnp.log1p(jnp.exp(-jnp.abs(raw)))
    rows = lax.broadcasted_iota(jnp.int32, (count, count), 0)
    lanes = lax.broadcasted_iota(jnp.int32, (count, count), 1)
    cum = dot((rows >= lanes).astype(F32), -heads_ref[1:2, :] * dt, precision=HIGHEST)
    keep = (col_ref[:, 5:6] == row_ref[...]) & (rows >= lanes)
    carry, tail = col_ref[:, 4:5], col_ref[:, 0:1]
    ecum = jnp.exp(cum) * carry
    weight = jnp.exp(cum[count - 1 :, :] - cum) * tail
    turned = jnp.transpose(cum)
    decays = [
        jnp.where(keep, jnp.exp(cum[:, h : h + 1] - turned[h : h + 1, :]), 0.0) for h in range(2 * pairs)
    ]
    scores = dot_nt(c, b)
    mixing = [(scores * decay).astype(BF) for decay in decays]
    xdt = x * spread(dt, 0, pairs)
    return pre, sig, x, b, c, raw, dt, ecum, weight, decays, mixing, xdt, pairs


def halves(value):
    low = lax.broadcasted_iota(jnp.int32, value.shape, 1) < 64
    zero = jnp.zeros_like(value)
    return jnp.concatenate([jnp.where(low, value, zero), jnp.where(low, zero, value)], axis=0)


def mamba_kernel(
    me_ref, zx_ref, zxp_ref, bc_ref, bcp_ref, step_ref, col_ref, row_ref, taps_ref, heads_ref, skip_ref,
    g_ref, hs_ref, state, ext,
):
    @pl.when(pl.program_id(0) == 0)
    def _():
        state[...] = jnp.zeros_like(state)

    _, _, x, b, c, _, _, ecum, weight, _, mixing, xdt, pairs = span(
        zx_ref, zxp_ref, bc_ref, bcp_ref, step_ref, col_ref, row_ref.at[0], taps_ref, heads_ref, ext
    )
    count, inner = x.shape
    held = state[...].astype(BF)
    hs_ref[0] = held
    low = xdt.astype(BF)
    direct = jnp.concatenate(
        [
            dot(jnp.concatenate(mixing[2 * p : 2 * p + 2], axis=1), halves(low[:, 128 * p : 128 * p + 128]))
            for p in range(pairs)
        ],
        axis=1,
    )
    wide = spread(ecum, 0, pairs)
    y = direct + dot(c, held) * wide + skip_ref[...] * x
    z = zx_ref[:, :inner].astype(F32)
    g_ref[...] = (y * z * sigmoid(z)).astype(BF)
    state[...] = state[...] * wide[count - 1 :, :] + dot_tn(b, (xdt * spread(weight, 0, pairs)).astype(BF))


def mamba_back_kernel(
    me_ref, zx_ref, zxp_ref, bc_ref, bcp_ref, step_ref, col_ref, row_ref, taps_ref, heads_ref, skip_ref, hs_ref, dg_ref,
    dzx_ref, dbc_ref, dstep_ref, dstate, ext, later, cross,
):
    @pl.when(pl.program_id(0) == 0)
    def _():
        dstate[...] = jnp.zeros_like(dstate)
        later[...] = jnp.zeros_like(later)
        cross[...] = jnp.zeros_like(cross)

    pre, sig, x, b, c, raw, dt, ecum, weight, decays, mixing, xdt, pairs = span(
        zx_ref, zxp_ref, bc_ref, bcp_ref, step_ref, col_ref, row_ref.at[0], taps_ref, heads_ref, ext
    )
    count, inner = x.shape
    state = hs_ref[0]
    z = zx_ref[:, :inner].astype(F32)
    dg = dg_ref[...].astype(F32)
    sig_z = sigmoid(z)
    dy = dg * z * sig_z
    dyl = dy.astype(BF)
    low = xdt.astype(BF)
    dst = dstate[...]
    dsl = dst.astype(BF)
    directs, dxdts = [], []
    dscores = jnp.zeros((count, count), F32)
    for p in range(pairs):
        lanes = slice(128 * p, 128 * p + 128)
        dy_two = halves(dyl[:, lanes])
        x_two = halves(low[:, lanes])
        directs.append(dot(jnp.concatenate(mixing[2 * p : 2 * p + 2], axis=1), x_two))
        dxdts.append(dot_tn(jnp.concatenate(mixing[2 * p : 2 * p + 2], axis=0), dy_two))
        dmix = dot_nt(dy_two, low[:, lanes])
        dscores = dscores + decays[2 * p] * dmix[:count] + decays[2 * p + 1] * dmix[count:]
    wide = spread(ecum, 0, pairs)
    tails = spread(weight, 0, pairs)
    core = jnp.concatenate(directs, axis=1) + dot(c, state) * wide
    dxdt = jnp.concatenate(dxdts, axis=1) + dot(b, dsl) * tails
    y = core + skip_ref[...] * x
    dz = dg * y * (sig_z * (1.0 + z * (1.0 - sig_z)))
    dsc = dscores.astype(BF)
    into = (dy * wide).astype(BF)
    dc = dot(dsc, b) + dot_nt(into, state)
    db = dot_tn(dsc, c) + dot_nt((xdt * tails).astype(BF), dsl)
    wide_dt = spread(dt, 0, pairs)
    dx = dxdt * wide_dt + skip_ref[...] * dy
    head_rows = lax.broadcasted_iota(jnp.int32, (inner, 128), 0) // 64
    head_lanes = lax.broadcasted_iota(jnp.int32, (inner, 128), 1)
    collect = (head_rows == head_lanes).astype(F32)
    flow = dyl.astype(F32) * core - low.astype(F32) * dxdt
    dcum = dot(flow, collect, precision=HIGHEST)
    rows = lax.broadcasted_iota(jnp.int32, (count, count), 0)
    lanes = lax.broadcasted_iota(jnp.int32, (count, count), 1)
    dcum = dcum + jnp.where(rows == count - 1, cross[0:1, :], 0.0)
    da = dot((lanes >= rows).astype(F32), dcum, precision=HIGHEST)
    ddt = dot(x * dxdt, collect, precision=HIGHEST) - heads_ref[1:2, :] * da
    dstep_ref[...] = jnp.where(lanes < 2 * pairs, ddt * sigmoid(raw), 0.0).astype(BF)
    dnew = dst * wide[count - 1 :, :] + dot_tn(c, into)
    dstate[...] = dnew
    held = jnp.sum(dnew * state.astype(F32), axis=0, keepdims=True)
    cross[...] = dot(jnp.broadcast_to(held, (8, inner)), collect, precision=HIGHEST)
    dzx_ref[:, :inner] = dz.astype(BF)
    dpre = jnp.concatenate([dx, db, dc], axis=1) * (sig * (1.0 + pre * (1.0 - sig)))
    total = taps_ref[0:1, :] * dpre
    for k in range(1, CONV):
        masked = dpre * col_ref[:, k : k + 1]
        ext[0:count, :] = masked
        ext[count:, :] = later[k - 1]
        total = total + taps_ref[k : k + 1, :] * ext[k : k + count, :]
        later[k - 1] = masked[0:8, :]
    dzx_ref[:, inner:] = total[:, :inner].astype(BF)
    dbc_ref[...] = total[:, inner:].astype(BF)


def whole(shape):
    return pl.BlockSpec(shape, lambda i, me: (0,) * len(shape))


def rows_of(width, rows=ROWS):
    return pl.BlockSpec((rows, width), lambda i, me: (i, 0))


ANY = pl.BlockSpec(memory_space=pl.ANY)


def params():
    return pltpu.CompilerParams(vmem_limit_bytes=VMEM)


def sds(shape, dtype):
    return jax.ShapeDtypeStruct(shape, dtype)


def half_rows(width):
    return pl.BlockSpec((ROWS // 2, width), lambda i, me: (i ^ me[1], 0))


def sems(count):
    return pltpu.SemaphoreType.DMA((count,))


def cost(macs, size):
    return pl.CostEstimate(flops=2 * macs // COST, bytes_accessed=size // COST, transcendentals=0)


def call_in(me, h, shrink, expand, cos, sin, stepw, far_kv, far_bc, parts, blocks, inner, states):
    n, d = h.shape
    r = shrink.shape[0]
    width = expand.shape[1]
    return pl.pallas_call(
        in_kernel,
        grid_spec=pltpu.PrefetchScalarGridSpec(
            num_scalar_prefetch=1,
            grid=(n // ROWS,),
            in_specs=[rows_of(d), whole((r, d)), whole((r, width)), rows_of(HD), rows_of(HD), whole((128, d))]
            + [ANY] * (2 + len(parts)),
            out_specs=[rows_of(2 * inner), rows_of(states), rows_of(3 * HD), rows_of(128), rows_of(r)],
            scratch_shapes=[pltpu.VMEM((d, width - 128), BF), pltpu.SemaphoreType.DMA((7, blocks))],
        ),
        out_shape=[sds((n, 2 * inner), BF), sds((n, states), BF), sds((n, 3 * HD), BF), sds((n, 128), F32), sds((n, r), BF)],
        compiler_params=params(),
        cost_estimate=cost(n * d * width, 2 * (n * d + d * width + n * width)),
        name="mixer_in",
    )(me, h, shrink, expand, cos, sin, stepw, far_kv, far_bc, *parts)


def call_in_back(me, dzx, dbc, dqkv, dstep, h, rank, shrink, expand, stepw, far_kv, far_bc, parts, blocks):
    n, d = h.shape
    r, width = expand.shape
    return pl.pallas_call(
        in_back_kernel,
        grid_spec=pltpu.PrefetchScalarGridSpec(
            num_scalar_prefetch=1,
            grid=(n // ROWS,),
            in_specs=[
                rows_of(dzx.shape[1]), rows_of(dbc.shape[1]), rows_of(3 * HD), rows_of(128), rows_of(d), rows_of(r),
                whole((r, d)), whole((r, width)), whole((128, d)),
            ]
            + [ANY] * (2 + len(parts)),
            out_specs=[half_rows(d), half_rows(d), whole((r, width)), whole((r, d))],
            scratch_shapes=[
                pltpu.VMEM((d, width - 128), BF), pltpu.VMEM((ROWS, width), BF), pltpu.SemaphoreType.DMA((7, blocks))
            ],
        ),
        out_shape=[sds((n // 2, d), BF)] * 2 + [sds((r, width), F32), sds((r, d), F32)],
        compiler_params=params(),
        cost_estimate=cost(n * d * width, 2 * (2 * n * d + d * width + n * width)),
        name="mixer_in_back",
    )(me, dzx, dbc, dqkv, dstep, h, rank, shrink, expand, stepw, far_kv, far_bc, *parts)


def call_out(me, g, o, shrink, expand, pieces, blocks):
    n, inner = g.shape
    r, d = expand.shape
    width = shrink.shape[1]
    return pl.pallas_call(
        out_kernel,
        grid_spec=pltpu.PrefetchScalarGridSpec(
            num_scalar_prefetch=1,
            grid=(n // ROWS,),
            in_specs=[rows_of(inner), rows_of(HD), whole((r, width)), whole((r, d))] + [ANY] * len(pieces),
            out_specs=[half_rows(d), half_rows(d), rows_of(r)],
            scratch_shapes=[pltpu.VMEM((d, width), BF), pltpu.VMEM((ROWS, width), BF), sems(blocks)],
        ),
        out_shape=[sds((n // 2, d), BF)] * 2 + [sds((n, r), BF)],
        compiler_params=params(),
        cost_estimate=cost(n * d * width, 2 * (n * d + d * width + n * width)),
        name="mixer_out",
    )(me, g, o, shrink, expand, *pieces)


def call_out_back(me, ml, g, o, rank, shrink, expand, pieces, blocks):
    n, inner = g.shape
    r, d = expand.shape
    width = shrink.shape[1]
    return pl.pallas_call(
        out_back_kernel,
        grid_spec=pltpu.PrefetchScalarGridSpec(
            num_scalar_prefetch=1,
            grid=(n // ROWS,),
            in_specs=[rows_of(d), rows_of(inner), rows_of(HD), rows_of(r), whole((r, width)), whole((r, d))] + [ANY] * len(pieces),
            out_specs=[rows_of(inner), rows_of(HD), whole((r, d)), whole((r, width))],
            scratch_shapes=[pltpu.VMEM((d, width), BF), sems(blocks)],
        ),
        out_shape=[sds((n, inner), BF), sds((n, HD), BF), sds((r, d), F32), sds((r, width), F32)],
        compiler_params=params(),
        cost_estimate=cost(n * d * width, 2 * (n * d + d * width + n * width)),
        name="mixer_out_back",
    )(me, ml, g, o, rank, shrink, expand, *pieces)


def call_ffn(me, h, shrink, expand, dshrink, dexpand, parts, blocks):
    n, d = h.shape
    r, both = expand.shape
    half = both // 2
    return pl.pallas_call(
        ffn_kernel,
        grid_spec=pltpu.PrefetchScalarGridSpec(
            num_scalar_prefetch=1,
            grid=(n // ROWS,),
            in_specs=[rows_of(d), whole((r, d)), whole((r, both)), whole((r, half)), whole((r, d))] + [ANY] * len(parts),
            out_specs=[half_rows(d), half_rows(d), rows_of(both), rows_of(half), rows_of(r), rows_of(r)],
            scratch_shapes=[pltpu.VMEM((d, both), BF), pltpu.VMEM((d, half), BF), pltpu.SemaphoreType.DMA((3, blocks))],
        ),
        out_shape=[sds((n // 2, d), BF)] * 2 + [sds((n, both), BF), sds((n, half), BF), sds((n, r), BF), sds((n, r), BF)],
        compiler_params=params(),
        cost_estimate=cost(3 * n * d * half, 2 * (2 * n * d + 3 * d * half + 3 * n * half)),
        name="ffn",
    )(me, h, shrink, expand, dshrink, dexpand, *parts)


def call_ffn_back(me, dl, h, gu, q, rank, drank, shrink, expand, dshrink, dexpand, parts, blocks):
    n, d = h.shape
    r, both = expand.shape
    half = both // 2
    return pl.pallas_call(
        ffn_back_kernel,
        grid_spec=pltpu.PrefetchScalarGridSpec(
            num_scalar_prefetch=1,
            grid=(n // ROWS,),
            in_specs=[
                rows_of(d), rows_of(d), rows_of(both), rows_of(half), rows_of(r), rows_of(r),
                whole((r, d)), whole((r, both)), whole((r, half)), whole((r, d)),
            ]
            + [ANY] * len(parts),
            out_specs=[half_rows(d), half_rows(d), whole((r, d)), whole((r, both)), whole((r, half)), whole((r, d))],
            scratch_shapes=[
                pltpu.VMEM((d, both), BF), pltpu.VMEM((d, half), BF), pltpu.VMEM((ROWS, both), BF), pltpu.SemaphoreType.DMA((3, blocks))
            ],
        ),
        out_shape=[sds((n // 2, d), BF)] * 2 + [sds((r, d), F32), sds((r, both), F32), sds((r, half), F32), sds((r, d), F32)],
        compiler_params=params(),
        cost_estimate=cost(3 * n * d * half, 2 * (3 * n * d + 3 * d * half + 3 * n * half)),
        name="ffn_back",
    )(me, dl, h, gu, q, rank, drank, shrink, expand, dshrink, dexpand, *parts)


def call_attn(qkv, cols, places):
    n = qkv.shape[0]
    return pl.pallas_call(
        attn_kernel,
        grid=(n // ROWS,),
        in_specs=[
            pl.BlockSpec((ROWS, HD), lambda i: (i, 0)),
            pl.BlockSpec((n, HD), lambda i: (0, 1)),
            pl.BlockSpec((n, HD), lambda i: (0, 2)),
            pl.BlockSpec((ROWS, 128), lambda i: (i, 0)),
            pl.BlockSpec((8, n), lambda i: (0, 0)),
        ],
        out_specs=pl.BlockSpec((ROWS, HD), lambda i: (i, 0)),
        out_shape=sds((n, HD), BF),
        compiler_params=params(),
        cost_estimate=cost(2 * n * n * HD, 8 * n * HD),
        name="attend",
    )(qkv, qkv, qkv, cols, places)


def call_attn_back(qkv, cols, places, do, cos, sin):
    n = qkv.shape[0]
    block = pl.BlockSpec((ROWS, HD), lambda i: (i, 0))
    full = pl.BlockSpec((n, HD), lambda i: (0, 0))
    return pl.pallas_call(
        attn_back_kernel,
        grid=(n // ROWS,),
        in_specs=[
            block,
            pl.BlockSpec((n, HD), lambda i: (0, 1)),
            pl.BlockSpec((n, HD), lambda i: (0, 2)),
            pl.BlockSpec((ROWS, 128), lambda i: (i, 0)),
            pl.BlockSpec((8, n), lambda i: (0, 0)),
            block, block, block, full, full,
        ],
        out_specs=[block, full, full],
        out_shape=[sds((n, HD), BF)] * 3,
        scratch_shapes=[pltpu.VMEM((n, HD), F32)] * 2,
        compiler_params=params(),
        cost_estimate=cost(7 * n * n * HD, 16 * n * HD),
        name="attend_back",
    )(qkv, qkv, qkv, cols, places, do, cos, sin, cos, sin)


def chunk_specs(order, zx, bc, chunk):
    tail = chunk // 16

    def here(i, me):
        return (order(i), 0)

    def before(i, me):
        return (jnp.maximum(order(i) - 1, 0) * tail + tail - 1, 0)

    inner2, states = zx.shape[1], bc.shape[1]
    width = inner2 // 2 + states
    specs = [
        pl.BlockSpec((chunk, inner2), here),
        pl.BlockSpec((16, inner2), before),
        pl.BlockSpec((chunk, states), here),
        pl.BlockSpec((16, states), before),
        pl.BlockSpec((chunk, 128), here),
        pl.BlockSpec((chunk, 128), here),
        pl.BlockSpec((1, 1, chunk), lambda i, me: (order(i), 0, 0)),
        whole((8, width)),
        whole((8, 128)),
        whole((1, inner2 // 2)),
    ]
    return specs, here, width


def call_mamba(me, zx, bc, step, cols, rows, taps, heads, skip, chunk):
    n = zx.shape[0]
    inner, states = zx.shape[1] // 2, bc.shape[1] // 2
    specs, here, width = chunk_specs(lambda i: i, zx, bc, chunk)
    return pl.pallas_call(
        mamba_kernel,
        grid_spec=pltpu.PrefetchScalarGridSpec(
            num_scalar_prefetch=1,
            grid=(n // chunk,),
            in_specs=specs,
            out_specs=[pl.BlockSpec((chunk, inner), here), pl.BlockSpec((1, states, inner), lambda i, me: (i, 0, 0))],
            scratch_shapes=[pltpu.VMEM((states, inner), F32), pltpu.VMEM((chunk + 8, width), F32)],
        ),
        out_shape=[sds((n, inner), BF), sds((n // chunk, states, inner), BF)],
        compiler_params=params(),
        cost_estimate=cost(3 * n * inner * states, 4 * n * width),
        name="mamba",
    )(me, zx, zx, bc, bc, step, cols, rows, taps, heads, skip)


def call_mamba_back(me, zx, bc, step, cols, rows, taps, heads, skip, hs, dg, chunk):
    n = zx.shape[0]
    inner, states = zx.shape[1] // 2, bc.shape[1] // 2
    count = n // chunk

    def order(i):
        return count - 1 - i

    specs, here, width = chunk_specs(order, zx, bc, chunk)
    return pl.pallas_call(
        mamba_back_kernel,
        grid_spec=pltpu.PrefetchScalarGridSpec(
            num_scalar_prefetch=1,
            grid=(count,),
            in_specs=specs
            + [pl.BlockSpec((1, states, inner), lambda i, me: (order(i), 0, 0)), pl.BlockSpec((chunk, inner), here)],
            out_specs=[
                pl.BlockSpec((chunk, 2 * inner), here),
                pl.BlockSpec((chunk, 2 * states), here),
                pl.BlockSpec((chunk, 128), here),
            ],
            scratch_shapes=[
                pltpu.VMEM((states, inner), F32),
                pltpu.VMEM((chunk + 8, width), F32),
                pltpu.VMEM((CONV - 1, 8, width), F32),
                pltpu.VMEM((8, 128), F32),
            ],
        ),
        out_shape=[sds((n, 2 * inner), BF), sds((n, 2 * states), BF), sds((n, 128), BF)],
        compiler_params=params(),
        cost_estimate=cost(10 * n * inner * states, 8 * n * width),
        name="mamba_back",
    )(me, zx, zx, bc, bc, step, cols, rows, taps, heads, skip, hs, dg)


def place_kernel(layers, pieces, *refs):
    ins, outs = refs[: 3 * layers], refs[3 * layers :]
    adapter = pl.program_id(1)
    for l in range(layers):

        @pl.when(pl.program_id(0) == l)
        def _():
            parts = ins[3 * l : 3 * l + 3]
            low = parts[1]
            seqs, _, width = low.shape
            lane = lax.broadcasted_iota(jnp.int32, (1, 128), 1)
            hot = [
                jnp.sum(jnp.where(lane == adapter, low[s, 0:1, width - 128 :].astype(F32), 0.0), axis=1, keepdims=True)
                for s in range(seqs)
            ]
            for out, sources in zip(outs, pieces):
                to = 0
                for which, start, size in sources:
                    value = hot[0] * parts[which][0, :, start : start + size].astype(F32)
                    for s in range(1, seqs):
                        value = value + hot[s] * parts[which][s, :, start : start + size].astype(F32)
                    out[0, 0, :, to : to + size] = value
                    to += size


def call_place(sums, adapters, rank, width, inner, ff, states, kv_width):
    layers = len(sums)
    zx = inner + HD
    gate = zx + 2 * inner + HD + 128

    def both(start, size):
        return ((1, start, size), (2, start, size))

    pieces = (
        ((0, width, width),),
        both(zx + 2 * inner, HD),
        ((0, 2 * width, states),),
        ((0, 2 * width + states, kv_width),),
        both(0, inner),
        both(inner, HD),
        ((0, 0, width),),
        ((0, 2 * width + states + kv_width, width),),
        both(gate + 2 * ff, ff),
        ((0, 3 * width + states + kv_width, width),),
        both(zx, inner),
        both(zx + inner, inner),
        both(gate, ff),
        both(gate + ff, ff),
        ((1, zx + 2 * inner + HD, 128),),
        ((2, zx + 2 * inner + HD, 128),),
    )
    sizes = [sum(size for _, _, size in sources) for sources in pieces]
    arrays = [array for group in sums for array in group]
    return pl.pallas_call(
        functools.partial(place_kernel, layers, pieces),
        grid=(layers, adapters),
        in_specs=[pl.BlockSpec(array.shape, lambda l, a: (0, 0, 0)) for array in arrays],
        out_specs=[pl.BlockSpec((1, 1, rank, size), lambda l, a: (l, a, 0, 0)) for size in sizes],
        out_shape=[sds((layers, adapters, rank, size), F32) for size in sizes],
        compiler_params=params(),
        name="place",
    )(*arrays)


def half_of(array, which, axis):
    size = array.shape[axis] // 2
    return lax.dynamic_slice_in_dim(array, which * size, size, axis)


def on_device(
    dp_axes,
    tokens,
    out_grad,
    doc_lengths,
    adapter_ids,
    mixer_gain,
    ffn_gain,
    ssm_in,
    step_proj,
    query_proj,
    state_proj,
    keyval_proj,
    conv_inner,
    conv_state,
    decay_log,
    step_bias,
    skip_gain,
    ssm_out,
    attn_out,
    gate_up,
    down_proj,
    mixer_shrink,
    inner_expand,
    step_expand,
    query_expand,
    state_expand,
    keyval_expand,
    ssmout_shrink,
    attnout_shrink,
    mixer_expand,
    ffn_shrink,
    gateup_expand,
    down_shrink,
    down_expand,
):
    layers = ssm_in.shape[0]
    zh, zl, ta, tb = (lax.axis_index(a) for a in ("zh", "zl", "ta", "tb"))
    me_w = zh * 2 + zl
    for k, axis in enumerate(dp_axes):
        me_w = me_w + lax.axis_index(axis) * (4 << k)
    me = jnp.stack([me_w, ta, zl, tb]).astype(jnp.int32)
    block, width = tokens.shape[1:]
    n = block * 4
    share = n // 8
    chunk = share
    heads = step_proj.shape[2] // 2
    inner = ssm_in.shape[3] // 2
    states = 2 * state_proj.shape[3]
    rank = mixer_shrink.shape[3]
    local = ssm_in.shape[1]
    ff = gate_up.shape[3] // 2

    def to_own(array):
        mine = half_of(array, tb, 1)
        keep = lax.dynamic_index_in_dim(mine, zh, 0, False)
        away = lax.dynamic_index_in_dim(mine, 1 - zh, 0, False)
        got = lax.ppermute(away, ("zh", "ta"), [(0, 2), (3, 1)])
        return jnp.where(zh == ta, keep, got)

    def all_stages(own, dtype, *tokens):
        own = later(own, *tokens)
        got = lax.ppermute(own, ("zh", "ta"), [(2, 0), (1, 3)])
        near = swap(own, "ta")
        tokens = yield [got, near]
        same = jnp.where(zh == ta, own, near)
        got = later(got, *tokens)
        across = swap(got, "ta")
        tokens = yield [across]
        other = jnp.where(zh == ta, got, across)
        pair = later(jnp.where(zh == 0, jnp.stack([same, other]), jnp.stack([other, same])), *tokens)
        far = swap(pair, "tb")
        yield [far]
        full = jnp.where(tb == 0, jnp.concatenate([pair, far], axis=1), jnp.concatenate([far, pair], axis=1))
        return full.astype(dtype)

    def ordered(axis, own, got, along):
        here = lax.axis_index(axis) == 0
        return jnp.where(here, jnp.concatenate([own, got], axis=along), jnp.concatenate([got, own], axis=along))


    def takes(name, l, tie):
        def cut(array, starts, sizes):
            return lax.dynamic_slice(array, (l,) + starts, (1,) + sizes).reshape(tuple(k for k in sizes if k > 1))

        def pick(which):
            if name in ("a", "b"):
                k = 0 if name == "a" else 1
                left = cut(arrays[0], (0, k, which * inner), (local, 1, inner))
                if name == "a":
                    return [left, cut(arrays[1], (0, which * HD), (local, HD))]
                return [left, cut(arrays[1], (0, tb, ta * HD), (local, 1, HD))]
            if name == "c":
                return [cut(arrays[0], (0, tb, 0), (local, 1, states // 2))]
            if name == "out":
                return [cut(arrays[0], (which * inner, 0), (inner, local)).T, cut(arrays[1], (which * HD, 0), (HD, local)).T]
            if name == "down":
                return [cut(arrays[0], (which * ff, 0), (ff, local)).T]
            return [cut(arrays[0], (0, 0 if name == "gate" else 1, which * ff), (local, 1, ff))]

        sources = {
            "a": (ssm_in, query_proj), "b": (ssm_in, keyval_proj), "c": (state_proj,), "out": (ssm_out, attn_out),
            "gate": (gate_up,), "up": (gate_up,), "down": (down_proj,),
        }
        arrays = tie(*sources[name])
        return pick

    own, sent, near, pair, far_z, got = ({} for _ in range(6))
    last = {}

    def prepare(key, *tokens):
        def tie(*values):
            return tied(*values, *tokens)[: len(values)] if tokens else values

        pick = takes(*key, tie)
        own[key], sent[key] = (jnp.concatenate(pick(which), axis=1) for which in (zl, 1 - zl))

    def order(way):
        return (last[way],) if way in last else ()

    def send_zl(key, *tokens):
        near[key] = last["zl"] = swap(later(sent[key], *order("zl"), *tokens), "zl")

    def send_zh(key, *tokens):
        pair[key] = later(jnp.concatenate([own[key], near[key]], axis=0), *order("zh"), *tokens)
        far_z[key] = last["zh"] = swap(pair[key], "zh")

    def send_dp(key, *tokens):
        held, moved = pair[key], far_z[key]
        for axis in dp_axes:
            held = later(jnp.concatenate([held, moved], axis=0), *order("dp"), *tokens)
            moved = last["dp"] = swap(held, axis)
        got[key] = (held, moved)

    blocks = 4 << len(dp_axes)
    chain = [(name, l) for l in range(layers) for name in ("a", "b", "c", "out", "gate", "up", "down")]
    early = 4
    for key in chain[:3]:
        prepare(key)
        near[key] = swap(sent[key], "zl")
    for key in chain[:3]:
        send_zh(key)
    for key in chain[:3]:
        send_dp(key)
    for k, key in enumerate(chain[3:]):
        prepare(key, far_z[chain[0]] if k < 2 else far_z[chain[1]])
    send_zl(chain[3])
    send_zh(chain[3])
    send_zl(chain[4])
    moved = [5]
    arrived = [near[chain[4]], far_z[chain[3]]]

    def window(value, *tokens):
        out = later(value, *arrived, *tokens)
        arrived.clear()
        k = moved[0]
        moved[0] += 1
        if k < len(chain):
            send_zl(chain[k], *tokens)
            arrived.append(near[chain[k]])
        if k - 1 < len(chain):
            send_zh(chain[k - 1], *tokens)
            arrived.append(far_z[chain[k - 1]])
        if k - 2 < len(chain):
            send_dp(chain[k - 2], *tokens)
            arrived.append(got[chain[k - 2]][1])
        return out

    def step_window(value, tokens, *stages):
        out = later(value, *arrived, *tokens)
        arrived.clear()
        for stage in stages:
            arrived.extend(stage.start(*tokens) or ())
        return out

    step_rows = jnp.pad(jnp.swapaxes(tied(step_proj, far_z["a", 0])[0].reshape(layers, -1, 2, heads), 1, 3), ((0, 0), (0, 8 - heads), (0, 0), (0, 0)))
    stepw = lax.dynamic_index_in_dim(step_rows, zl, 2, False)
    stepw = ordered("zl", stepw, swap(lax.dynamic_index_in_dim(step_rows, 1 - zl, 2, False), "zl"), 2)
    for axis in ("zh",) + dp_axes:
        stepw = ordered(axis, stepw, swap(stepw, axis), 2)
    stepw = jnp.pad(stepw, ((0, 0), (0, 120), (0, 0)))

    def mixer_weights(l):
        def both(key, start):
            return swap(jnp.concatenate([part[:, start:] for part in got[key]], axis=0), "tb")

        parts = got["a", l] + got["b", l] + got["c", l]
        return stepw[l], both(("b", l), inner), both(("c", l), 0), parts, blocks

    lengths = lax.dynamic_index_in_dim(doc_lengths, zh, 0, False)
    aid = lax.dynamic_index_in_dim(adapter_ids, zh, 0, False)
    lengths, positions = tied(lengths, jnp.arange(n, dtype=jnp.int32), far_z["a", 0])[:2]
    seg = segment_of(positions, lengths)
    seg_back = [segment_of(positions - k, lengths) for k in range(1, CONV)]
    starts = (positions // chunk) * chunk
    seg_start = segment_of(starts - 1, lengths)
    seg_end = segment_of(starts + chunk - 1, lengths)
    cols = jnp.stack(
        [(seg == seg_end).astype(F32)]
        + [(seg == s).astype(F32) for s in seg_back]
        + [(seg == seg_start).astype(F32), seg.astype(F32), positions.astype(F32)],
        axis=1,
    )
    cols = jnp.pad(cols, ((0, 0), (0, 128 - cols.shape[1])))
    rows = seg.astype(F32).reshape(n // chunk, 1, chunk)
    places = jnp.pad(jnp.stack([seg.astype(F32), positions.astype(F32)]), ((0, 6), (0, 0)))
    freqs = ROPE_BASE ** (-jnp.arange(HD // 2, dtype=F32) / (HD // 2))
    angles = positions.astype(F32)[:, None] * freqs[None, :]
    cos = jnp.tile(jnp.cos(angles), (1, 2))
    sin = jnp.sin(angles)
    sin = jnp.concatenate([-sin, sin], axis=1)

    def small_of(l, token):
        aid_now = tied(aid, token)[0]

        def pick(table):
            zeros = (0,) * (table.ndim - 2)
            return lax.dynamic_slice(table, (l, aid_now) + zeros, (1, 1) + table.shape[2:]).reshape(table.shape[2:])

        def flat(table):
            return pick(table).T

        inner_e, keyval_e = pick(inner_expand), pick(keyval_expand)
        expand_in = jnp.concatenate(
            [
                half_of(inner_e[:, 0], zl, 1),
                half_of(inner_e[:, 1], zl, 1),
                half_of(pick(query_expand), zl, 1),
                lax.dynamic_slice_in_dim(keyval_e[:, 0], ta * HD, HD, 1),
                lax.dynamic_slice_in_dim(keyval_e[:, 1], ta * HD, HD, 1),
                pick(state_expand).reshape(rank, -1),
                jnp.pad(half_of(pick(step_expand), zl, 1), ((0, 0), (0, 128 - heads))),
            ],
            axis=1,
        )
        shrink_out = jnp.concatenate([half_of(flat(ssmout_shrink), zl, 1), half_of(flat(attnout_shrink), zl, 1)], axis=1)
        gate_e = pick(gateup_expand)
        expand_gu = jnp.concatenate([half_of(gate_e[:, 0], zl, 1), half_of(gate_e[:, 1], zl, 1)], axis=1)
        shrink_down = half_of(flat(down_shrink), zl, 1)
        taps = jnp.pad(
            jnp.concatenate([half_of(conv_inner[l], zl, 1), conv_state[l].reshape(CONV, -1)], axis=1), ((0, 8 - CONV), (0, 0))
        )
        head_rows = jnp.pad(
            jnp.stack([half_of(step_bias[l], zl, 0), jnp.exp(half_of(decay_log[l], zl, 0))]), ((0, 6), (0, 128 - heads))
        )
        skip = jnp.repeat(half_of(skip_gain[l], zl, 0), inner // heads)[None, :]
        return (
            flat(mixer_shrink), expand_in, shrink_out, pick(mixer_expand), flat(ffn_shrink), expand_gu, shrink_down,
            pick(down_expand), taps, head_rows, skip,
        )

    weights, small, saved = [], [], []
    resid = to_own(tied(tokens, near["c", 0])[0]).astype(F32)
    grad_own = to_own(tied(out_grad, far_z["out", 0])[0])
    token = far_z["a", 0]
    for l in range(layers):
        small.append(small_of(l, token))
        shrink_in, expand_in, shrink_out, expand_out, shrink_gu, expand_gu, shrink_down, expand_down, taps, head_rows, skip = small[l]
        gain = mixer_gain[l] if l == 0 else window(mixer_gain[l], resid)
        h = gather_tokens(rms_norm(resid, gain).astype(BF))
        w_in = mixer_weights(l)
        zx, bc, qkv, step, rank_in = call_in(window(me, h), h, shrink_in, expand_in, cos, sin, *w_in, inner, states)
        g, hs = call_mamba(window(me, rank_in), zx, bc, step, cols, rows, taps, head_rows, skip, chunk)
        o = call_attn(qkv, cols, places)
        w_out = (got["out", l], blocks)
        keep, send, rank_out = call_out(me, g, o, shrink_out, expand_out, *w_out)
        mid = resid + scatter_tokens(keep, window(send, rank_out))
        token = mid
        h2 = gather_tokens(rms_norm(mid, window(ffn_gain[l], mid)).astype(BF))
        w_ffn = (got["gate", l] + got["up", l] + got["down", l], blocks)
        keep, send, gu, q, rank_gu, rank_down = call_ffn(window(me, h2), h2, shrink_gu, expand_gu, shrink_down, expand_down, *w_ffn)
        if l + 1 < layers:
            resid_next = mid + scatter_tokens(keep, window(send, rank_down))
        else:
            final = Stages(scatter_stages(keep, send))
        weights.append((w_in, w_out, w_ffn))
        saved.append((resid, mid, h, zx, bc, qkv, step, rank_in, g, hs, o, rank_out, h2, gu, q, rank_gu, rank_down))
        resid = resid_next

    seq_axes = tuple(reversed(dp_axes)) + ("zh",)
    adapters = mixer_shrink.shape[1]
    hot = jnp.pad((aid == jnp.arange(adapters, dtype=jnp.int32)).astype(BF), (0, 128 - adapters))
    hot = jnp.broadcast_to(hot[None], (rank, 128))

    def sum_stages(partial, owned, *tokens):
        mine = jnp.concatenate(partial, axis=1).astype(BF)
        for axis in ("tb", "ta", "zl"):
            bit = lax.axis_index(axis)
            moved = swap(later(half_of(mine, 1 - bit, 1), *tokens), axis)
            tokens = yield [moved]
            mine = (half_of(mine, bit, 1).astype(F32) + moved.astype(F32)).astype(BF)
        size = mine.shape[1]
        held = jnp.concatenate([mine] + [value.astype(BF) for value in owned] + [hot], axis=1)[None]
        for axis in ("zh",) + dp_axes:
            held = later(held, *tokens)
            moved = swap(held, axis)
            tokens = yield [moved]
            held = jnp.concatenate([held, moved], axis=0)
        held = later(held, *tokens)
        moved = swap(held, "zl")
        tokens = yield [moved]
        total = ordered("zl", held[..., :size], moved[..., :size], 2)
        low = zl == 0
        parts = jnp.where(low, held[..., size:], moved[..., size:]), jnp.where(low, moved[..., size:], held[..., size:])
        for axis in ("ta", "tb"):
            total = later(total, *tokens)
            moved = swap(total, axis)
            tokens = yield [moved]
            total = ordered(axis, total, moved, 2)
        return (total,) + parts

    grad = grad_own.astype(F32)
    sums = [None] * layers
    at = 2 * inner
    out_stages, older = None, None
    for l in reversed(range(layers)):
        shrink_in, expand_in, shrink_out, expand_out, shrink_gu, expand_gu, shrink_down, expand_down, taps, head_rows, skip = small[l]
        w_in, w_out, w_ffn = weights[l]
        resid, mid, h, zx, bc, qkv, step, rank_in, g, hs, o, rank_out, h2, gu, q, rank_gu, rank_down = saved[l]
        top = l == layers - 1
        dl = gather_tokens(grad.astype(BF))
        if top:
            now = step_window(me, (dl, rank_down), final)
        else:
            now = step_window(me, (dl,), out_stages, older)
        keep, send, g_shrink_gu, g_expand_gu, g_shrink_down, g_expand_down = call_ffn_back(
            now, dl, h2, gu, q, rank_gu, rank_down, shrink_gu, expand_gu, shrink_down, expand_down, *w_ffn
        )
        send = step_window(send, (g_expand_gu,), *(() if top else (older,)))
        d_mid = scatter_tokens(keep, send)
        grad = grad + norm_back(mid, step_window(ffn_gain[l], (d_mid,)), d_mid)
        ml = gather_tokens(grad.astype(BF))
        now = step_window(me, (ml,), *((final,) if top else (out_stages, older)))
        dg, do, g_expand_out, g_shrink_out = call_out_back(now, ml, g, o, rank_out, shrink_out, expand_out, *w_out)
        dq, dk, dv = call_attn_back(qkv, cols, places, do, cos, sin)
        now = step_window(me, (dq,), *((final,) if top else (older,)))
        dzx, dbc, dstep = call_mamba_back(now, zx, bc, step, cols, rows, taps, head_rows, skip, hs, dg, chunk)
        dqkv = jnp.concatenate([dq, dk, dv], axis=1)
        if top:
            output = mid + final.finish()
            out_stages = Stages(all_stages(output.astype(BF), BF, dstep))
            now = step_window(me, (dstep,), out_stages)
        else:
            now = step_window(me, (dstep,), older)
        keep, send, g_expand_in, g_shrink_in = call_in_back(
            now, dzx, dbc, dqkv, dstep, h, rank_in, shrink_in, expand_in, *w_in
        )
        send = step_window(send, (g_expand_in,))
        kv = jnp.zeros((rank, 2, keyval_proj.shape[3]), F32)
        own_kv = jnp.stack([g_expand_in[:, at + HD : at + 2 * HD], g_expand_in[:, at + 2 * HD : at + 3 * HD]], axis=1)
        kv = lax.dynamic_update_slice_in_dim(kv, own_kv, ta * HD, 2).reshape(rank, -1)
        groups = (
            [g_expand_out, g_shrink_in, g_expand_in[:, at + 3 * HD : at + 3 * HD + states], kv, g_shrink_gu, g_expand_down],
            [
                g_shrink_out, g_expand_in[:, : at + HD], g_expand_in[:, at + 3 * HD + states :],
                g_expand_gu, g_shrink_down,
            ],
        )
        last_sum = Stages(scatter_stages(keep, send))
        first = last_sum.start()
        if not l:
            sums[l] = Stages(sum_stages(*groups, *first))
            sums[l].start()
        d_resid = last_sum.finish()
        grad = grad + norm_back(resid, mixer_gain[l], d_resid)
        if l:
            older = sums[l] = Stages(sum_stages(*groups, d_resid))
            for _ in range(3):
                arrived[:] = older.start()
    output = out_stages.finish()
    input_grad = Stages(all_stages(grad.astype(BF), F32)).finish()
    sums = [stages.finish() for stages in sums]

    kv_width = 2 * keyval_proj.shape[3]
    lead = (layers, adapters, rank)
    (
        mixshrink, queryexpand, stateexpand, keyvalexpand, ssmshrink, attnshrink, mixexpand, ffnshrink, downshrink, downexpand,
        zexpand, xexpand, gateexpand, upexpand, step_low, step_high,
    ) = call_place(sums, adapters, rank, width, inner, ff, states, kv_width)

    def turned(value):
        return jnp.swapaxes(value, 2, 3)

    return (
        output,
        input_grad,
        turned(mixshrink),
        jnp.stack([zexpand, xexpand], axis=3),
        jnp.concatenate([step_low[..., :heads], step_high[..., :heads]], axis=-1),
        queryexpand,
        stateexpand.reshape(lead + (2, -1)),
        keyvalexpand.reshape(lead + (2, -1)),
        turned(ssmshrink),
        turned(attnshrink),
        mixexpand,
        turned(ffnshrink),
        jnp.stack([gateexpand, upexpand], axis=3),
        turned(downshrink),
        downexpand,
    )


def solution(mesh):
    dp, ctx, tensor = (mesh.shape[a] for a in ("dp", "ctx", "tensor"))
    bits = dp.bit_length() - 1
    dp_names = tuple("d%d" % k for k in reversed(range(bits)))
    inside = Mesh(
        mesh.devices.reshape((2,) * bits + (2, ctx // 2, 2, tensor // 2)), dp_names + ("zh", "zl", "ta", "tb")
    )
    dp_axes = tuple(reversed(dp_names))
    d, c, t = dp_names, ("zh", "zl"), ("ta", "tb")
    dc = dp_names + c
    return jax.shard_map(
        functools.partial(on_device, dp_axes),
        mesh=inside,
        in_specs=(
            P(d, c, None),
            P(d, c, None),
            P(d, None),
            P(d),
            P(),
            P(),
            P(None, dc, None, t),
            P(None, dc, t),
            P(None, dc, t),
            P(None, dc, None, None),
            P(None, dc, None, None),
            P(None, None, t),
            P(),
            P(None, t),
            P(None, t),
            P(None, t),
            P(None, t, dc),
            P(None, t, dc),
            P(None, dc, None, t),
            P(None, t, dc),
            P(),
            P(None, None, None, None, t),
            P(None, None, None, t),
            P(None, None, None, t),
            P(),
            P(),
            P(None, None, t, None),
            P(None, None, t, None),
            P(),
            P(),
            P(None, None, None, None, t),
            P(None, None, t, None),
            P(),
        ),
        out_specs=(
            P(d, c, None),
            P(d, c, None),
            P(),
            P(None, None, None, None, t),
            P(None, None, None, t),
            P(None, None, None, t),
            P(),
            P(),
            P(None, None, t, None),
            P(None, None, t, None),
            P(),
            P(),
            P(None, None, None, None, t),
            P(None, None, t, None),
            P(),
        ),
        check_vma=False,
    )
```

```python
import functools

import jax
import jax.numpy as jnp
from jax import lax
from jax.experimental import pallas as pl
from jax.experimental.pallas import tpu as pltpu
from jax.sharding import Mesh
from jax.sharding import PartitionSpec as P

HD = 128
CONV = 4
EPS = 1e-05
ROPE_BASE = 10000.0
HIGHEST = lax.Precision.HIGHEST
BF = jnp.bfloat16
F32 = jnp.float32
TOK = ("ta", "zl", "tb")
ROWS = 512
TILE = 256
AHEAD = 4
BACK = 2
COST = 1000
VMEM = 56 * 1024 * 1024


def dot(a, b, **kw):
    return jnp.dot(a, b, preferred_element_type=F32, **kw)


def dot_nt(a, b):
    return lax.dot_general(a, b, (((1,), (1,)), ((), ())), preferred_element_type=F32)


def dot_tn(a, b):
    return lax.dot_general(a, b, (((0,), (0,)), ((), ())), preferred_element_type=F32)


def sigmoid(v):
    return 0.5 * jnp.tanh(0.5 * v) + 0.5


def swap(value, axis):
    return lax.ppermute(value, axis, [(0, 1), (1, 0)])


def rms_norm(stream, gain):
    return stream * lax.rsqrt(jnp.mean(stream * stream, axis=-1, keepdims=True) + EPS) * gain


def norm_back(stream, gain, upstream):
    scale = lax.rsqrt(jnp.mean(stream * stream, axis=-1, keepdims=True) + EPS)
    weighted = upstream * gain
    inner = jnp.mean(stream * weighted, axis=-1, keepdims=True)
    return scale * weighted - stream * (scale * scale * scale * inner)


def segment_of(positions, lengths):
    ends = jnp.cumsum(lengths)
    inside = jnp.sum((positions[:, None] >= ends[None, :]).astype(jnp.int32), axis=1)
    return jnp.where(positions < 0, -1, inside)


def gather_tokens(own):
    return lax.all_gather(own, TOK, axis=0, tiled=True)


def scatter_stages(keep, send, *tokens):
    b, half = keep.shape[0] // 4, keep.shape[1] // 2
    recv = swap(later(send, *tokens), "tb")
    tokens = yield [recv]

    def pair(rows, cols):
        return keep[rows, cols].astype(F32) + recv[rows, cols].astype(F32)

    first, second = slice(0, half), slice(half, 2 * half)

    def odd(cols, k):
        return jnp.concatenate([pair(slice(k * b, k * b + b), cols), pair(slice((k + 2) * b, (k + 3) * b), cols)], axis=0)

    got_a = swap(later(pair(slice(2 * b, 4 * b), first).astype(BF), *tokens), "ta")
    got_b = swap(later(odd(second, 1).astype(BF), *tokens), "zl")
    tokens = yield [got_a, got_b]
    sum_a = pair(slice(0, 2 * b), first) + got_a.astype(F32)
    sum_b = odd(second, 0) + got_b.astype(F32)
    last_a = swap(later(sum_a[b:].astype(BF), *tokens), "zl")
    last_b = swap(later(sum_b[b:].astype(BF), *tokens), "ta")
    yield [last_a, last_b]
    return jnp.concatenate([sum_a[:b] + last_a.astype(F32), sum_b[:b] + last_b.astype(F32)], axis=1)


def scatter_tokens(keep, send):
    return Stages(scatter_stages(keep, send)).finish()


class Stages:
    def __init__(self, chain):
        self.chain, self.begun, self.result = chain, False, None

    def start(self, *tokens):
        try:
            if self.begun:
                return self.chain.send(tokens)
            self.begun = True
            return next(self.chain)
        except StopIteration as end:
            self.result = end.value
            return None

    def finish(self):
        while self.start() is not None:
            pass
        return self.result


def later(value, *tokens):
    return tied(value, *tokens)[0] if tokens else value


def tied(*values):
    return lax.optimization_barrier(values)


def blocks_of(me_ref, parts, rows):
    out, j = [], 0
    for part in parts:
        for k in range(part.shape[0] // rows):
            at = pl.multiple_of((j ^ me_ref[0]) * rows, rows)
            out.append((part.at[pl.ds(k * rows, rows), :], pl.ds(at, rows)))
            j += 1
    return out


def weight_copies(me_ref, parts, held, sem):
    rows = held.shape[0] // sem.shape[0]
    return [
        pltpu.make_async_copy(block, held.at[at, :], sem.at[j]) for j, (block, at) in enumerate(blocks_of(me_ref, parts, rows))
    ]


def at_first(do, copies):
    @pl.when(pl.program_id(0) == 0)
    def _():
        for copy in copies():
            getattr(copy, do)()


def mixer_copies(me_ref, parts, far_kv, far_bc, held, sem):
    rows = held.shape[0] // sem.shape[1]
    states = far_bc.shape[1]
    inner = (held.shape[1] - 3 * HD - 2 * states - 128) // 2
    core = me_ref[3]

    def key(which):
        return pl.ds(pl.multiple_of(2 * inner + HD + which * HD, HD), HD)

    def state(which):
        return pl.ds(pl.multiple_of(2 * inner + 3 * HD + 128 + which * states, HD), states)

    first, second, third = (blocks_of(me_ref, part, rows) for part in parts)
    copies = []
    for j, ((one, at), (two, _), (three, _)) in enumerate(zip(first, second, third)):
        here = pl.ds(j * rows, rows)
        for k, (source, cols) in enumerate(
            (
                (one.at[:, pl.ds(0, inner)], pl.ds(0, inner)),
                (one.at[:, pl.ds(inner, HD)], pl.ds(2 * inner, HD)),
                (two.at[:, pl.ds(0, inner)], pl.ds(inner, inner)),
                (two.at[:, pl.ds(inner, HD)], key(core)),
                (three.at[:, pl.ds(0, states)], state(core)),
                (three.at[:, pl.ds(states, 128)], pl.ds(2 * inner + 3 * HD, 128)),
                (far_kv.at[here, :], key(1 - core)),
                (far_bc.at[here, :], state(1 - core)),
            )
        ):
            copies.append(pltpu.make_async_copy(source, held.at[at, cols], sem.at[k, j]))
    return copies


def turned_rows(me_ref, size):
    b = size // 4
    out = []
    for core in (me_ref[3], 1 - me_ref[3]):
        for z in range(2):
            out.append(pl.ds(pl.multiple_of(((z ^ me_ref[2]) * 2 + core) * b, b), b))
    return out


def emit(keep_ref, send_ref, cols, value):
    half = value.shape[0] // 2
    low = value.astype(BF)
    keep_ref[:, cols] = low[:half]
    send_ref[:, cols] = low[half:]


def in_kernel(me_ref, h_ref, shrink_ref, expand_ref, cos_ref, sin_ref, far_kv, far_bc, *rest):
    parts, rest = (rest[0:2], rest[2:4], rest[4:6]), rest[6:]
    zx_ref, bc_ref, qkv_ref, step_ref, rank_ref, held, sem = rest
    inner = zx_ref.shape[1]
    states = bc_ref.shape[1]

    def copies():
        return mixer_copies(me_ref, parts, far_kv, far_bc, held, sem)

    at_first("start", copies)
    h = h_ref[...]
    rank = dot_nt(h, shrink_ref[...]).astype(BF)
    rank_ref[...] = rank
    at_first("wait", copies)

    def part(at, width):
        cols = slice(at, at + width)
        return dot(h, held[:, cols]) + dot(rank, expand_ref[:, cols])

    for at in range(0, inner, 256):
        zx_ref[:, at : at + 256] = part(at, 256).astype(BF)
    qk = part(inner, 2 * HD)
    cos, sin = cos_ref[...], sin_ref[...]
    for k in range(2):
        head = qk[:, k * HD : (k + 1) * HD]
        turned = head * cos + pltpu.roll(head, HD // 2, 1) * sin
        qkv_ref[:, k * HD : (k + 1) * HD] = turned.astype(BF)
    last = part(inner + 2 * HD, HD + 128)
    qkv_ref[:, 2 * HD :] = last[:, :HD].astype(BF)
    step_ref[...] = last[:, HD:]
    for at in range(0, states, 256):
        bc_ref[:, at : at + 256] = part(inner + 3 * HD + 128 + at, 256).astype(BF)


def in_back_kernel(
    me_ref, dzx_ref, dbc_ref, dqkv_ref, dstep_ref, h_ref, rank_ref, shrink_ref, expand_ref, far_kv, far_bc, *rest
):
    parts, rest = (rest[0:2], rest[2:4], rest[4:6]), rest[6:]
    keep_ref, send_ref, gexpand_ref, gshrink_ref, held, du, low, sem = rest
    inner = dzx_ref.shape[1]

    def copies():
        return mixer_copies(me_ref, parts, far_kv, far_bc, held, sem)

    at_first("start", copies)

    @pl.when(pl.program_id(0) == 0)
    def _():
        gexpand_ref[...] = jnp.zeros_like(gexpand_ref)
        gshrink_ref[...] = jnp.zeros_like(gshrink_ref)

    size = du.shape[0]
    b = size // 4
    rank = rank_ref[...]
    where = turned_rows(me_ref, size)
    at = 0
    for source in (dzx_ref, dqkv_ref, dstep_ref, dbc_ref):
        wide = source.shape[1]
        gexpand_ref[:, at : at + wide] += dot_tn(rank, source[...])
        for k in range(4):
            du[k * b : (k + 1) * b, at : at + wide] = source[where[k], :]
        at += wide
    drank = dot_nt(du[...], expand_ref[...]).astype(BF)
    for k in range(4):
        low[where[k], :] = drank[k * b : (k + 1) * b]
    natural = low[...]
    for at in range(0, h_ref.shape[1], 256):
        cols = slice(at, at + 256)
        gshrink_ref[:, cols] += dot_tn(natural, h_ref[:, cols])
    at_first("wait", copies)
    for at in range(0, h_ref.shape[1], 256):
        cols = slice(at, at + 256)
        emit(keep_ref, send_ref, cols, dot_nt(du[...], held[cols, :]) + dot(drank, shrink_ref[:, cols]))


def out_kernel(me_ref, g_ref, o_ref, shrink_ref, expand_ref, *rest):
    pieces, rest = rest[:2], rest[2:]
    keep_ref, send_ref, rank_ref, held, go, sem = rest

    def copies():
        return weight_copies(me_ref, pieces, held, sem)

    at_first("start", copies)
    inner = g_ref.shape[1]
    size = go.shape[0]
    b = size // 4
    where = turned_rows(me_ref, size)
    for k in range(4):
        go[k * b : (k + 1) * b, :inner] = g_ref[where[k], :]
        go[k * b : (k + 1) * b, inner:] = o_ref[where[k], :]
    rank = dot_nt(go[...], shrink_ref[...]).astype(BF)
    for k in range(4):
        rank_ref[where[k], :] = rank[k * b : (k + 1) * b]
    at_first("wait", copies)
    for at in range(0, expand_ref.shape[1], 256):
        cols = slice(at, at + 256)
        emit(keep_ref, send_ref, cols, dot_nt(go[...], held[cols, :]) + dot(rank, expand_ref[:, cols]))


def out_back_kernel(me_ref, ml_ref, g_ref, o_ref, rank_ref, shrink_ref, expand_ref, *rest):
    pieces, rest = rest[:2], rest[2:]
    dg_ref, do_ref, gexpand_ref, gshrink_ref, held, sem = rest

    def copies():
        return weight_copies(me_ref, pieces, held, sem)

    at_first("start", copies)

    @pl.when(pl.program_id(0) == 0)
    def _():
        gexpand_ref[...] = jnp.zeros_like(gexpand_ref)
        gshrink_ref[...] = jnp.zeros_like(gshrink_ref)

    inner = g_ref.shape[1]
    ml = ml_ref[...]
    drank = dot_nt(ml, expand_ref[...]).astype(BF)
    rank = rank_ref[...]
    for at in range(0, ml.shape[1], 256):
        cols = slice(at, at + 256)
        gexpand_ref[:, cols] += dot_tn(rank, ml_ref[:, cols])
    gshrink_ref[:, :inner] += dot_tn(drank, g_ref[...])
    gshrink_ref[:, inner:] += dot_tn(drank, o_ref[...])
    at_first("wait", copies)
    for at in range(0, held.shape[1], 256):
        cols = slice(at, at + 256)
        got = (dot(ml, held[:, cols]) + dot(drank, shrink_ref[:, cols])).astype(BF)
        for to in (at, at + 128):
            if to < inner:
                dg_ref[:, to : to + 128] = got[:, to - at : to - at + 128]
            else:
                do_ref[:, to - inner : to - inner + 128] = got[:, to - at : to - at + 128]


def ffn_kernel(me_ref, h_ref, shrink_ref, expand_ref, dshrink_ref, dexpand_ref, *rest):
    (gates, ups, downs), rest = (rest[0:2], rest[2:4], rest[4:6]), rest[6:]
    keep_ref, send_ref, gu_ref, q_ref, rank_ref, drank_ref, held, dheld, qt, sem = rest
    half = dheld.shape[1]

    def both():
        return weight_copies(me_ref, gates, held.at[:, pl.ds(0, half)], sem.at[0]) + weight_copies(
            me_ref, ups, held.at[:, pl.ds(half, half)], sem.at[1]
        )

    def down():
        return weight_copies(me_ref, downs, dheld, sem.at[2])

    at_first("start", lambda: both() + down())
    h = h_ref[...]
    rank = dot_nt(h, shrink_ref[...]).astype(BF)
    rank_ref[...] = rank
    at_first("wait", both)
    for at in range(0, half, 256):
        one = slice(at, at + 256)
        two = slice(half + at, half + at + 256)
        gate = dot(h, held[:, one]) + dot(rank, expand_ref[:, one])
        up = dot(h, held[:, two]) + dot(rank, expand_ref[:, two])
        gu_ref[:, one] = gate.astype(BF)
        gu_ref[:, two] = up.astype(BF)
        q_ref[:, one] = (gate * sigmoid(gate) * up).astype(BF)
    size = qt.shape[0]
    b = size // 4
    where = turned_rows(me_ref, size)
    for k in range(4):
        qt[k * b : (k + 1) * b, :] = q_ref[where[k], :]
    drank = dot_nt(qt[...], dshrink_ref[...]).astype(BF)
    for k in range(4):
        drank_ref[where[k], :] = drank[k * b : (k + 1) * b]
    at_first("wait", down)
    for at in range(0, dexpand_ref.shape[1], 256):
        cols = slice(at, at + 256)
        emit(keep_ref, send_ref, cols, dot_nt(qt[...], dheld[cols, :]) + dot(drank, dexpand_ref[:, cols]))


def ffn_back_kernel(
    me_ref, dl_ref, h_ref, gu_ref, q_ref, rank_ref, drank_ref, shrink_ref, expand_ref, dshrink_ref, dexpand_ref, *rest
):
    (gates, ups, downs), rest = (rest[0:2], rest[2:4], rest[4:6]), rest[6:]
    keep_ref, send_ref, gshrink_ref, gexpand_ref, gdshrink_ref, gdexpand_ref, held, dheld, dgu, turned, low, sem = rest
    half = dheld.shape[1]

    def both():
        return weight_copies(me_ref, gates, held.at[:, pl.ds(0, half)], sem.at[0]) + weight_copies(
            me_ref, ups, held.at[:, pl.ds(half, half)], sem.at[1]
        )

    def down():
        return weight_copies(me_ref, downs, dheld, sem.at[2])

    at_first("start", lambda: down() + both())

    @pl.when(pl.program_id(0) == 0)
    def _():
        for ref in (gshrink_ref, gexpand_ref, gdshrink_ref, gdexpand_ref):
            ref[...] = jnp.zeros_like(ref)

    dl = dl_ref[...]
    ddrank = dot_nt(dl, dexpand_ref[...]).astype(BF)
    down_rank = drank_ref[...]
    for at in range(0, dl.shape[1], 256):
        cols = slice(at, at + 256)
        gdexpand_ref[:, cols] += dot_tn(down_rank, dl_ref[:, cols])
    gdshrink_ref[...] += dot_tn(ddrank, q_ref[...])
    rank = rank_ref[...]
    at_first("wait", down)
    for at in range(0, half, 256):
        one = slice(at, at + 256)
        two = slice(half + at, half + at + 256)
        dq = dot(dl, dheld[:, one]) + dot(ddrank, dshrink_ref[:, one])
        gate = gu_ref[:, one].astype(F32)
        up = gu_ref[:, two].astype(F32)
        sig = sigmoid(gate)
        dgu[:, one] = (dq * up * sig * (1.0 + gate * (1.0 - sig))).astype(BF)
        dgu[:, two] = (dq * gate * sig).astype(BF)
    gexpand_ref[...] += dot_tn(rank, dgu[...])
    size = dgu.shape[0]
    b = size // 4
    where = turned_rows(me_ref, size)
    for k in range(4):
        turned[k * b : (k + 1) * b, :] = dgu[where[k], :]
    drank = dot_nt(turned[...], expand_ref[...]).astype(BF)
    for k in range(4):
        low[where[k], :] = drank[k * b : (k + 1) * b]
    natural = low[...]
    for at in range(0, h_ref.shape[1], 256):
        cols = slice(at, at + 256)
        gshrink_ref[:, cols] += dot_tn(natural, h_ref[:, cols])
    at_first("wait", both)
    for at in range(0, h_ref.shape[1], 256):
        cols = slice(at, at + 256)
        emit(keep_ref, send_ref, cols, dot_nt(turned[...], held[cols, :]) + dot(drank, shrink_ref[:, cols]))


def attend(q, k, v, place_q, seg_q, place_k, seg_k):
    scores = dot_nt(q, k) * HD ** (-0.5)
    seen = (place_q >= place_k) & (seg_q == seg_k)
    masked = jnp.where(seen, scores, -1e30)
    top = jnp.max(masked, axis=-1, keepdims=True)
    raised = jnp.exp(masked - top)
    probs = raised * (1.0 / jnp.sum(raised, axis=-1, keepdims=True))
    low = probs.astype(BF)
    return probs, low, dot(low, v)


def attn_kernel(qkv_ref, col_ref, row_ref, o_ref):
    for start in range(0, o_ref.shape[0], TILE):
        at, seen = slice(start, start + TILE), slice(0, start + TILE)
        _, _, out = attend(
            qkv_ref[at, :HD], qkv_ref[seen, HD : 2 * HD], qkv_ref[seen, 2 * HD :],
            col_ref[at, 6:7], col_ref[at, 5:6], row_ref[1:2, seen], row_ref[0:1, seen],
        )
        o_ref[at, :] = out.astype(BF)


def attn_back_kernel(qkv_ref, col_ref, row_ref, do_ref, cos_ref, sin_ref, dqkv_ref, dk_sum, dv_sum):
    def back(turned, cos, sin):
        return ((turned * cos - pltpu.roll(turned, HD // 2, 1) * sin) * HD ** (-0.5)).astype(BF)

    dk_sum[...] = jnp.zeros_like(dk_sum)
    dv_sum[...] = jnp.zeros_like(dv_sum)
    for start in range(0, do_ref.shape[0], TILE):
        at, seen = slice(start, start + TILE), slice(0, start + TILE)
        q, k, v, do = qkv_ref[at, :HD], qkv_ref[seen, HD : 2 * HD], qkv_ref[seen, 2 * HD :], do_ref[at, :]
        probs, low, out = attend(
            q, k, v, col_ref[at, 6:7], col_ref[at, 5:6], row_ref[1:2, seen], row_ref[0:1, seen]
        )
        delta = jnp.sum(do.astype(F32) * out, axis=-1, keepdims=True)
        ds = (probs * (dot_nt(do, v) - delta)).astype(BF)
        dqkv_ref[at, :HD] = back(dot(ds, k), cos_ref[at, :], sin_ref[at, :])
        dk_sum[seen, :] += dot_tn(ds, q)
        dv_sum[seen, :] += dot_tn(low, do)
    dqkv_ref[:, HD : 2 * HD] = back(dk_sum[...], cos_ref[...], sin_ref[...])
    dqkv_ref[:, 2 * HD :] = dv_sum[...].astype(BF)


def spread(cols, first, pairs):
    rows = cols.shape[0]
    low = lax.broadcasted_iota(jnp.int32, (rows, 128), 1) < 64
    return jnp.concatenate(
        [
            jnp.where(low, cols[:, first + 2 * p : first + 2 * p + 1], cols[:, first + 2 * p + 1 : first + 2 * p + 2])
            for p in range(pairs)
        ],
        axis=1,
    )


def exact(ones, value):
    high = value.astype(BF)
    return dot(ones, high) + dot(ones, (value - high.astype(F32)).astype(BF))


def collected(value, ones):
    high = value.astype(BF)
    return dot(high, ones) + dot((value - high.astype(F32)).astype(BF), ones)


def span(pre, step, col_ref, row_ref, tri_ref, heads_ref, inner):
    count = pre.shape[0]
    states = pre.shape[1] - inner
    pairs = inner // 128
    sig = sigmoid(pre)
    conv = pre * sig
    x = conv[:, :inner]
    b = conv[:, inner : inner + states // 2].astype(BF)
    c = conv[:, inner + states // 2 :].astype(BF)
    raw = step + heads_ref[0:1, :]
    dt = jnp.maximum(raw, 0.0) + jnp.log1p(jnp.exp(-jnp.abs(raw)))
    tri = tri_ref[0]
    cum = exact(tri, -heads_ref[1:2, :] * dt)
    keep = (col_ref[:, 5:6] == row_ref[...]) & (tri > 0)
    carry, tail = col_ref[:, 4:5], col_ref[:, 0:1]
    ecum = jnp.exp(cum) * carry
    weight = jnp.exp(cum[count - 1 :, :] - cum) * tail
    turned = jnp.transpose(cum)
    decays = [
        jnp.where(keep, jnp.exp(cum[:, h : h + 1] - turned[h : h + 1, :]), 0.0) for h in range(2 * pairs)
    ]
    scores = dot_nt(c, b)
    mixing = [(scores * decay).astype(BF) for decay in decays]
    xdt = x * spread(dt, 0, pairs)
    return sig, x, b, c, raw, dt, ecum, weight, decays, mixing, xdt, pairs


def halves(value):
    low = lax.broadcasted_iota(jnp.int32, value.shape, 1) < 64
    zero = jnp.zeros_like(value)
    return jnp.concatenate([jnp.where(low, value, zero), jnp.where(low, zero, value)], axis=0)


def mamba_kernel(
    me_ref, zx_ref, zxp_ref, bc_ref, bcp_ref, step_ref, col_ref, row_ref, taps_ref, heads_ref, skip_ref, tri_ref,
    g_ref, hs_ref, pre_ref, state, ext,
):
    @pl.when(pl.program_id(0) == 0)
    def _():
        state[...] = jnp.zeros_like(state)

    count, inner = zx_ref.shape[0], zx_ref.shape[1] // 2
    ext[0:8, :inner] = zxp_ref[8:16, inner:].astype(F32)
    ext[0:8, inner:] = bcp_ref[8:16, :].astype(F32)
    ext[8:, :inner] = zx_ref[:, inner:].astype(F32)
    ext[8:, inner:] = bc_ref[...].astype(F32)
    chunk = tri_ref.shape[1]
    for k in range(count // chunk):
        at = slice(k * chunk, (k + 1) * chunk)
        pre = taps_ref[0:1, :] * ext[8 + k * chunk : 8 + (k + 1) * chunk, :]
        for tap in range(1, CONV):
            first = 8 - tap + k * chunk
            pre = pre + taps_ref[tap : tap + 1, :] * (ext[first : first + chunk, :] * col_ref[at, tap : tap + 1])
        pre_ref[at, :] = pre.astype(BF)
        _, x, b, c, _, _, ecum, weight, _, mixing, xdt, pairs = span(
            pre, step_ref[at, :], col_ref.at[at, :], row_ref.at[k], tri_ref, heads_ref, inner
        )
        old = state[...]
        held = old.astype(BF)
        hs_ref[k] = held
        low = xdt.astype(BF)
        direct = jnp.concatenate(
            [
                dot(jnp.concatenate(mixing[2 * p : 2 * p + 2], axis=1), halves(low[:, 128 * p : 128 * p + 128]))
                for p in range(pairs)
            ],
            axis=1,
        )
        wide = spread(ecum, 0, pairs)
        y = direct + dot(c, held) * wide + skip_ref[...] * x
        z = zx_ref[at, :inner].astype(F32)
        g_ref[at, :] = (y * z * sigmoid(z)).astype(BF)
        state[...] = old * wide[chunk - 1 :, :] + dot_tn(b, (xdt * spread(weight, 0, pairs)).astype(BF))


def mamba_back_kernel(
    me_ref, z_ref, pre_ref, step_ref, col_ref, row_ref, taps_ref, heads_ref, skip_ref, tri_ref, collect_ref, hs_ref, dg_ref,
    dzx_ref, dbc_ref, dstep_ref, dstate, ext, later_rows, cross,
):
    @pl.when(pl.program_id(0) == 0)
    def _():
        dstate[...] = jnp.zeros_like(dstate)
        later_rows[...] = jnp.zeros_like(later_rows)
        cross[...] = jnp.zeros_like(cross)

    chunk = tri_ref.shape[1]
    for k in reversed(range(z_ref.shape[0] // chunk)):
        at = pl.ds(k * chunk, chunk)
        mamba_back_chunk(
            z_ref.at[at, :], pre_ref.at[at, :], step_ref.at[at, :], col_ref.at[at, :], row_ref.at[k], taps_ref, heads_ref, skip_ref,
            tri_ref, collect_ref, hs_ref.at[k], dg_ref.at[at, :], dzx_ref.at[at, :], dbc_ref.at[at, :], dstep_ref.at[at, :],
            dstate, ext, later_rows, cross,
        )


def mamba_back_chunk(
    z_ref, pre_ref, step_ref, col_ref, row_ref, taps_ref, heads_ref, skip_ref, tri_ref, collect_ref, hs_ref, dg_ref,
    dzx_ref, dbc_ref, dstep_ref, dstate, ext, later_rows, cross,
):
    pre = pre_ref[...].astype(F32)
    sig, x, b, c, raw, dt, ecum, weight, decays, mixing, xdt, pairs = span(
        pre, step_ref[...], col_ref, row_ref, tri_ref, heads_ref, z_ref.shape[1]
    )
    count, inner = x.shape
    state = hs_ref[...]
    z = z_ref[...].astype(F32)
    dg = dg_ref[...].astype(F32)
    sig_z = sigmoid(z)
    dy = dg * z * sig_z
    dyl = dy.astype(BF)
    low = xdt.astype(BF)
    dst = dstate[...]
    dsl = dst.astype(BF)
    directs, dxdts = [], []
    dscores = jnp.zeros((count, count), F32)
    for p in range(pairs):
        lanes = slice(128 * p, 128 * p + 128)
        dy_two = halves(dyl[:, lanes])
        x_two = halves(low[:, lanes])
        directs.append(dot(jnp.concatenate(mixing[2 * p : 2 * p + 2], axis=1), x_two))
        dxdts.append(dot_tn(jnp.concatenate(mixing[2 * p : 2 * p + 2], axis=0), dy_two))
        dmix = dot_nt(dy_two, low[:, lanes])
        dscores = dscores + decays[2 * p] * dmix[:count] + decays[2 * p + 1] * dmix[count:]
    wide = spread(ecum, 0, pairs)
    tails = spread(weight, 0, pairs)
    core = jnp.concatenate(directs, axis=1) + dot(c, state) * wide
    dxdt = jnp.concatenate(dxdts, axis=1) + dot(b, dsl) * tails
    y = core + skip_ref[...] * x
    dz = dg * y * (sig_z * (1.0 + z * (1.0 - sig_z)))
    dsc = dscores.astype(BF)
    into = (dy * wide).astype(BF)
    dc = dot(dsc, b) + dot_nt(into, state)
    db = dot_tn(dsc, c) + dot_nt((xdt * tails).astype(BF), dsl)
    wide_dt = spread(dt, 0, pairs)
    dx = dxdt * wide_dt + skip_ref[...] * dy
    collect = collect_ref[...]
    flow = dyl.astype(F32) * core - low.astype(F32) * dxdt
    dcum = collected(flow, collect)
    rows = lax.broadcasted_iota(jnp.int32, (count, 128), 0)
    dcum = dcum + jnp.where(rows == count - 1, cross[0:1, :], 0.0)
    da = exact(tri_ref[1], dcum)
    ddt = collected(x * dxdt, collect) - heads_ref[1:2, :] * da
    lanes = lax.broadcasted_iota(jnp.int32, (count, 128), 1)
    dstep_ref[...] = jnp.where(lanes < 2 * pairs, ddt * sigmoid(raw), 0.0).astype(BF)
    dnew = dst * wide[count - 1 :, :] + dot_tn(c, into)
    dstate[...] = dnew
    held = jnp.sum(dnew * state.astype(F32), axis=0, keepdims=True)
    cross[...] = collected(jnp.broadcast_to(held, (8, inner)), collect)
    dzx_ref[:, :inner] = dz.astype(BF)
    dpre = jnp.concatenate([dx, db, dc], axis=1) * (sig * (1.0 + pre * (1.0 - sig)))
    total = taps_ref[0:1, :] * dpre
    for k in range(1, CONV):
        masked = dpre * col_ref[:, k : k + 1]
        ext[0:count, :] = masked
        ext[count:, :] = later_rows[k - 1]
        total = total + taps_ref[k : k + 1, :] * ext[k : k + count, :]
        later_rows[k - 1] = masked[0:8, :]
    dzx_ref[:, inner:] = total[:, :inner].astype(BF)
    dbc_ref[...] = total[:, inner:].astype(BF)


def whole(shape):
    return pl.BlockSpec(shape, lambda i, me: (0,) * len(shape))


def rows_of(width, rows=ROWS):
    return pl.BlockSpec((rows, width), lambda i, me: (i, 0))


ANY = pl.BlockSpec(memory_space=pl.ANY)


def params():
    return pltpu.CompilerParams(vmem_limit_bytes=VMEM)


def sds(shape, dtype):
    return jax.ShapeDtypeStruct(shape, dtype)


def half_rows(width):
    return pl.BlockSpec((ROWS // 2, width), lambda i, me: (i ^ me[1], 0))


def sems(count):
    return pltpu.SemaphoreType.DMA((count,))


def cost(macs, size):
    return pl.CostEstimate(flops=2 * macs // COST, bytes_accessed=size // COST, transcendentals=0)


def call_in(me, h, shrink, expand, cos, sin, far_kv, far_bc, parts, blocks, inner, states):
    n, d = h.shape
    r = shrink.shape[0]
    width = expand.shape[1]
    return pl.pallas_call(
        in_kernel,
        grid_spec=pltpu.PrefetchScalarGridSpec(
            num_scalar_prefetch=1,
            grid=(n // ROWS,),
            in_specs=[rows_of(d), whole((r, d)), whole((r, width)), rows_of(HD), rows_of(HD)]
            + [ANY] * (2 + len(parts)),
            out_specs=[rows_of(2 * inner), rows_of(states), rows_of(3 * HD), rows_of(128), rows_of(r)],
            scratch_shapes=[pltpu.VMEM((d, width), BF), pltpu.SemaphoreType.DMA((8, blocks))],
        ),
        out_shape=[sds((n, 2 * inner), BF), sds((n, states), BF), sds((n, 3 * HD), BF), sds((n, 128), F32), sds((n, r), BF)],
        compiler_params=params(),
        cost_estimate=cost(n * d * width, 2 * (n * d + d * width + n * width)),
        name="mixer_in",
    )(me, h, shrink, expand, cos, sin, far_kv, far_bc, *parts)


def call_in_back(me, dzx, dbc, dqkv, dstep, h, rank, shrink, expand, far_kv, far_bc, parts, blocks):
    n, d = h.shape
    r, width = expand.shape
    return pl.pallas_call(
        in_back_kernel,
        grid_spec=pltpu.PrefetchScalarGridSpec(
            num_scalar_prefetch=1,
            grid=(n // ROWS,),
            in_specs=[
                rows_of(dzx.shape[1]), rows_of(dbc.shape[1]), rows_of(3 * HD), rows_of(128), rows_of(d), rows_of(r),
                whole((r, d)), whole((r, width)),
            ]
            + [ANY] * (2 + len(parts)),
            out_specs=[half_rows(d), half_rows(d), whole((r, width)), whole((r, d))],
            scratch_shapes=[
                pltpu.VMEM((d, width), BF), pltpu.VMEM((ROWS, width), BF), pltpu.VMEM((ROWS, r), BF),
                pltpu.SemaphoreType.DMA((8, blocks)),
            ],
        ),
        out_shape=[sds((n // 2, d), BF)] * 2 + [sds((r, width), F32), sds((r, d), F32)],
        compiler_params=params(),
        cost_estimate=cost(n * d * width, 2 * (2 * n * d + d * width + n * width)),
        name="mixer_in_back",
    )(me, dzx, dbc, dqkv, dstep, h, rank, shrink, expand, far_kv, far_bc, *parts)


def call_out(me, g, o, shrink, expand, pieces, blocks):
    n, inner = g.shape
    r, d = expand.shape
    width = shrink.shape[1]
    return pl.pallas_call(
        out_kernel,
        grid_spec=pltpu.PrefetchScalarGridSpec(
            num_scalar_prefetch=1,
            grid=(n // ROWS,),
            in_specs=[rows_of(inner), rows_of(HD), whole((r, width)), whole((r, d))] + [ANY] * len(pieces),
            out_specs=[half_rows(d), half_rows(d), rows_of(r)],
            scratch_shapes=[pltpu.VMEM((d, width), BF), pltpu.VMEM((ROWS, width), BF), sems(blocks)],
        ),
        out_shape=[sds((n // 2, d), BF)] * 2 + [sds((n, r), BF)],
        compiler_params=params(),
        cost_estimate=cost(n * d * width, 2 * (n * d + d * width + n * width)),
        name="mixer_out",
    )(me, g, o, shrink, expand, *pieces)


def call_out_back(me, ml, g, o, rank, shrink, expand, pieces, blocks):
    n, inner = g.shape
    r, d = expand.shape
    width = shrink.shape[1]
    return pl.pallas_call(
        out_back_kernel,
        grid_spec=pltpu.PrefetchScalarGridSpec(
            num_scalar_prefetch=1,
            grid=(n // ROWS,),
            in_specs=[rows_of(d), rows_of(inner), rows_of(HD), rows_of(r), whole((r, width)), whole((r, d))] + [ANY] * len(pieces),
            out_specs=[rows_of(inner), rows_of(HD), whole((r, d)), whole((r, width))],
            scratch_shapes=[pltpu.VMEM((d, width), BF), sems(blocks)],
        ),
        out_shape=[sds((n, inner), BF), sds((n, HD), BF), sds((r, d), F32), sds((r, width), F32)],
        compiler_params=params(),
        cost_estimate=cost(n * d * width, 2 * (n * d + d * width + n * width)),
        name="mixer_out_back",
    )(me, ml, g, o, rank, shrink, expand, *pieces)


def call_ffn(me, h, shrink, expand, dshrink, dexpand, parts, blocks):
    n, d = h.shape
    r, both = expand.shape
    half = both // 2
    return pl.pallas_call(
        ffn_kernel,
        grid_spec=pltpu.PrefetchScalarGridSpec(
            num_scalar_prefetch=1,
            grid=(n // ROWS,),
            in_specs=[rows_of(d), whole((r, d)), whole((r, both)), whole((r, half)), whole((r, d))] + [ANY] * len(parts),
            out_specs=[half_rows(d), half_rows(d), rows_of(both), rows_of(half), rows_of(r), rows_of(r)],
            scratch_shapes=[
                pltpu.VMEM((d, both), BF), pltpu.VMEM((d, half), BF), pltpu.VMEM((ROWS, half), BF), pltpu.SemaphoreType.DMA((3, blocks))
            ],
        ),
        out_shape=[sds((n // 2, d), BF)] * 2 + [sds((n, both), BF), sds((n, half), BF), sds((n, r), BF), sds((n, r), BF)],
        compiler_params=params(),
        cost_estimate=cost(3 * n * d * half, 2 * (2 * n * d + 3 * d * half + 3 * n * half)),
        name="ffn",
    )(me, h, shrink, expand, dshrink, dexpand, *parts)


def call_ffn_back(me, dl, h, gu, q, rank, drank, shrink, expand, dshrink, dexpand, parts, blocks):
    n, d = h.shape
    r, both = expand.shape
    half = both // 2
    return pl.pallas_call(
        ffn_back_kernel,
        grid_spec=pltpu.PrefetchScalarGridSpec(
            num_scalar_prefetch=1,
            grid=(n // ROWS,),
            in_specs=[
                rows_of(d), rows_of(d), rows_of(both), rows_of(half), rows_of(r), rows_of(r),
                whole((r, d)), whole((r, both)), whole((r, half)), whole((r, d)),
            ]
            + [ANY] * len(parts),
            out_specs=[half_rows(d), half_rows(d), whole((r, d)), whole((r, both)), whole((r, half)), whole((r, d))],
            scratch_shapes=[
                pltpu.VMEM((d, both), BF), pltpu.VMEM((d, half), BF), pltpu.VMEM((ROWS, both), BF), pltpu.VMEM((ROWS, both), BF),
                pltpu.VMEM((ROWS, r), BF), pltpu.SemaphoreType.DMA((3, blocks)),
            ],
        ),
        out_shape=[sds((n // 2, d), BF)] * 2 + [sds((r, d), F32), sds((r, both), F32), sds((r, half), F32), sds((r, d), F32)],
        compiler_params=params(),
        cost_estimate=cost(3 * n * d * half, 2 * (3 * n * d + 3 * d * half + 3 * n * half)),
        name="ffn_back",
    )(me, dl, h, gu, q, rank, drank, shrink, expand, dshrink, dexpand, *parts)


def call_attn(qkv, cols, places):
    n = qkv.shape[0]
    return pl.pallas_call(
        attn_kernel,
        in_specs=[pl.BlockSpec(memory_space=pltpu.VMEM)] * 3,
        out_specs=pl.BlockSpec(memory_space=pltpu.VMEM),
        out_shape=sds((n, HD), BF),
        compiler_params=params(),
        cost_estimate=cost(2 * n * n * HD, 8 * n * HD),
        name="attend",
    )(qkv, cols, places)


def call_attn_back(qkv, cols, places, do, cos, sin):
    n = qkv.shape[0]
    return pl.pallas_call(
        attn_back_kernel,
        in_specs=[pl.BlockSpec(memory_space=pltpu.VMEM)] * 6,
        out_specs=pl.BlockSpec(memory_space=pltpu.VMEM),
        out_shape=sds((n, 3 * HD), BF),
        scratch_shapes=[pltpu.VMEM((n, HD), F32)] * 2,
        compiler_params=params(),
        cost_estimate=cost(7 * n * n * HD, 16 * n * HD),
        name="attend_back",
    )(qkv, cols, places, do, cos, sin)


def triangles(chunk):
    rows = jnp.arange(chunk, dtype=jnp.int32)
    lower = rows[:, None] >= rows[None, :]
    return jnp.stack([lower, lower.T]).astype(BF)


def call_mamba(me, zx, bc, step, cols, rows, taps, heads, skip, chunk):
    n = zx.shape[0]
    inner, states = zx.shape[1] // 2, bc.shape[1] // 2
    width = inner + 2 * states
    wide = AHEAD * chunk
    tail = wide // 16

    def here(i, me):
        return (i, 0)

    def before(i, me):
        return (jnp.maximum(i - 1, 0) * tail + tail - 1, 0)

    return pl.pallas_call(
        mamba_kernel,
        grid_spec=pltpu.PrefetchScalarGridSpec(
            num_scalar_prefetch=1,
            grid=(n // wide,),
            in_specs=[
                pl.BlockSpec((wide, 2 * inner), here),
                pl.BlockSpec((16, 2 * inner), before),
                pl.BlockSpec((wide, 2 * states), here),
                pl.BlockSpec((16, 2 * states), before),
                pl.BlockSpec((wide, 128), here),
                pl.BlockSpec((wide, 128), here),
                pl.BlockSpec((AHEAD, 1, chunk), lambda i, me: (i, 0, 0)),
                whole((8, width)),
                whole((8, 128)),
                whole((1, inner)),
                whole((2, chunk, chunk)),
            ],
            out_specs=[
                pl.BlockSpec((wide, inner), here),
                pl.BlockSpec((AHEAD, states, inner), lambda i, me: (i, 0, 0)),
                pl.BlockSpec((wide, width), here),
            ],
            scratch_shapes=[pltpu.VMEM((states, inner), F32), pltpu.VMEM((wide + 8, width), F32)],
        ),
        out_shape=[sds((n, inner), BF), sds((n // chunk, states, inner), BF), sds((n, width), BF)],
        compiler_params=params(),
        cost_estimate=cost(3 * n * inner * states, 4 * n * width),
        name="mamba",
    )(me, zx, zx, bc, bc, step, cols, rows, taps, heads, skip, triangles(chunk))


def call_mamba_back(me, zx, pre, step, cols, rows, taps, heads, skip, hs, dg, chunk):
    n = zx.shape[0]
    inner = zx.shape[1] // 2
    width = pre.shape[1]
    states = (width - inner) // 2
    wide = BACK * chunk
    count = n // wide
    collect = (jnp.arange(inner, dtype=jnp.int32)[:, None] // 64 == jnp.arange(128, dtype=jnp.int32)[None, :]).astype(BF)

    def here(i, me):
        return (count - 1 - i, 0)

    def deep(i, me):
        return (count - 1 - i, 0, 0)

    return pl.pallas_call(
        mamba_back_kernel,
        grid_spec=pltpu.PrefetchScalarGridSpec(
            num_scalar_prefetch=1,
            grid=(count,),
            in_specs=[
                pl.BlockSpec((wide, inner), here),
                pl.BlockSpec((wide, width), here),
                pl.BlockSpec((wide, 128), here),
                pl.BlockSpec((wide, 128), here),
                pl.BlockSpec((BACK, 1, chunk), deep),
                whole((8, width)),
                whole((8, 128)),
                whole((1, inner)),
                whole((2, chunk, chunk)),
                whole((inner, 128)),
                pl.BlockSpec((BACK, states, inner), deep),
                pl.BlockSpec((wide, inner), here),
            ],
            out_specs=[
                pl.BlockSpec((wide, 2 * inner), here),
                pl.BlockSpec((wide, 2 * states), here),
                pl.BlockSpec((wide, 128), here),
            ],
            scratch_shapes=[
                pltpu.VMEM((states, inner), F32),
                pltpu.VMEM((chunk + 8, width), F32),
                pltpu.VMEM((CONV - 1, 8, width), F32),
                pltpu.VMEM((8, 128), F32),
            ],
        ),
        out_shape=[sds((n, 2 * inner), BF), sds((n, 2 * states), BF), sds((n, 128), BF)],
        compiler_params=params(),
        cost_estimate=cost(10 * n * inner * states, 8 * n * width),
        name="mamba_back",
    )(me, zx, pre, step, cols, rows, taps, heads, skip, triangles(chunk), collect, hs, dg)


def place_kernel(pieces, parts, *outs):
    adapter = pl.program_id(0)
    seqs, _, width = parts[0].shape
    lane = lax.broadcasted_iota(jnp.int32, (1, 128), 1)
    hot = [
        jnp.sum(jnp.where(lane == adapter, parts[0][s, 0:1, width - 128 :].astype(F32), 0.0), axis=1, keepdims=True)
        for s in range(seqs)
    ]
    for out, rows in zip(outs, pieces):
        for k, sources in enumerate(rows):
            to = 0
            for which, start, size in sources:
                value = hot[0] * parts[which][0, :, start : start + size].astype(F32)
                for s in range(1, seqs):
                    value = value + hot[s] * parts[which][s, :, start : start + size].astype(F32)
                if len(rows) > 1:
                    out[0, 0, :, k, to : to + size] = value
                else:
                    out[0, 0, :, to : to + size] = value
                to += size


def call_place(l, layers, group, before, adapters, rank, width, inner, ff, states, kv_width):
    kv = 2 * width + states
    of = len(group) - 1
    first, second = inner + HD + 2 * inner + HD + 128, 3 * ff
    sums = kv + kv_width + (0 if of else 2 * width)
    owned = first + (0 if of else second)
    ffn = 0 if of else kv + kv_width

    def both(at, size):
        return ((0, sums + at, size), (0, sums + owned + at, size))

    def ffn_both(at, size):
        if of:
            return ((1, 2 * width + at, size), (1, 2 * width + second + at, size))
        return both(first + at, size)

    zx = inner + HD
    pieces = (
        (((0, width, width),),),
        (both(zx, inner), both(zx + inner, inner)),
        (both(zx + 2 * inner, HD),),
        (((0, 2 * width, states // 2),), ((0, 2 * width + states // 2, states // 2),)),
        (((0, kv, kv_width // 2),), ((0, kv + kv_width // 2, kv_width // 2),)),
        (both(0, inner),),
        (both(inner, HD),),
        (((0, 0, width),),),
        (((of, ffn, width),),),
        (ffn_both(0, ff), ffn_both(ff, ff)),
        (ffn_both(2 * ff, ff),),
        (((of, ffn + width, width),),),
        (((0, sums + zx + 2 * inner + HD, 128),),),
        (((0, sums + owned + zx + 2 * inner + HD, 128),),),
    )
    shapes = []
    for rows in pieces:
        size = sum(size for _, _, size in rows[0])
        shapes.append((rank, len(rows), size) if len(rows) > 1 else (rank, size))

    def block(shape):
        zeros = (0,) * len(shape)
        return pl.BlockSpec((1, 1) + shape, lambda a: (l, a) + zeros)

    def body(*refs):
        place_kernel(pieces, refs[: len(group)], *refs[len(group) + len(before) :])

    return pl.pallas_call(
        body,
        grid=(adapters,),
        in_specs=[pl.BlockSpec(array.shape, lambda a: (0, 0, 0)) for array in group] + [ANY] * len(before),
        out_specs=[block(shape) for shape in shapes],
        out_shape=[sds((layers, adapters) + shape, F32) for shape in shapes],
        input_output_aliases={len(group) + k: k for k in range(len(before))},
        compiler_params=params(),
        name="place",
    )(*group, *before)


def half_of(array, which, axis):
    size = array.shape[axis] // 2
    return lax.dynamic_slice_in_dim(array, which * size, size, axis)


def on_device(
    dp_axes,
    tokens,
    out_grad,
    doc_lengths,
    adapter_ids,
    mixer_gain,
    ffn_gain,
    ssm_in,
    step_proj,
    query_proj,
    state_proj,
    keyval_proj,
    conv_inner,
    conv_state,
    decay_log,
    step_bias,
    skip_gain,
    ssm_out,
    attn_out,
    gate_up,
    down_proj,
    mixer_shrink,
    inner_expand,
    step_expand,
    query_expand,
    state_expand,
    keyval_expand,
    ssmout_shrink,
    attnout_shrink,
    mixer_expand,
    ffn_shrink,
    gateup_expand,
    down_shrink,
    down_expand,
):
    layers = ssm_in.shape[0]
    zh, zl, ta, tb = (lax.axis_index(a) for a in ("zh", "zl", "ta", "tb"))
    me_w = zh * 2 + zl
    for k, axis in enumerate(dp_axes):
        me_w = me_w + lax.axis_index(axis) * (4 << k)
    me = jnp.stack([me_w, ta, zl, tb]).astype(jnp.int32)
    block, width = tokens.shape[1:]
    n = block * 4
    share = n // 8
    chunk = share
    heads = step_proj.shape[2] // 2
    inner = ssm_in.shape[3] // 2
    states = 2 * state_proj.shape[3]
    rank = mixer_shrink.shape[3]
    local = ssm_in.shape[1]
    ff = gate_up.shape[3] // 2

    def own_stages(array, *tokens):
        mine = half_of(array, tb, 1)
        keep = lax.dynamic_index_in_dim(mine, zh, 0, False)
        away = lax.dynamic_index_in_dim(mine, 1 - zh, 0, False)
        rows = away.shape[0] // 2
        got = swap(later(jnp.where(zh == ta, away[:rows], away[rows:]), *tokens), "zh")
        tokens = yield [got]
        beside = swap(later(got, *tokens), "ta")
        yield [beside]
        return jnp.where(zh == ta, keep, jnp.concatenate([got, beside], axis=0))

    def all_stages(own, dtype, *tokens):
        own = later(own, *tokens)
        got = lax.ppermute(own, ("zh", "ta"), [(2, 0), (1, 3)])
        near = swap(own, "ta")
        tokens = yield [got, near]
        same = jnp.where(zh == ta, own, near)
        got = later(got, *tokens)
        across = swap(got, "ta")
        tokens = yield [across]
        other = jnp.where(zh == ta, got, across)
        pair = later(jnp.where(zh == 0, jnp.stack([same, other]), jnp.stack([other, same])), *tokens)
        far = swap(pair, "tb")
        yield [far]
        full = jnp.where(tb == 0, jnp.concatenate([pair, far], axis=1), jnp.concatenate([far, pair], axis=1))
        return full.astype(dtype)

    def ordered(axis, own, got, along):
        here = lax.axis_index(axis) == 0
        return jnp.where(here, jnp.concatenate([own, got], axis=along), jnp.concatenate([got, own], axis=along))


    def takes(name, l, tie):
        def cut(array, starts, sizes):
            return lax.dynamic_slice(array, (l,) + starts, (1,) + sizes).reshape(tuple(k for k in sizes if k > 1))

        def pick(which):
            if name in ("a", "b"):
                k = 0 if name == "a" else 1
                left = cut(arrays[0], (0, k, which * inner), (local, 1, inner))
                if name == "a":
                    return [left, cut(arrays[1], (0, which * HD), (local, HD))]
                return [left, cut(arrays[1], (0, tb, ta * HD), (local, 1, HD))]
            if name == "c":
                step = cut(arrays[1], (0, which * heads), (local, heads))
                return [cut(arrays[0], (0, tb, 0), (local, 1, states // 2)), jnp.pad(step, ((0, 0), (0, 128 - heads)))]
            if name == "out":
                return [cut(arrays[0], (which * inner, 0), (inner, local)).T, cut(arrays[1], (which * HD, 0), (HD, local)).T]
            if name == "down":
                return [cut(arrays[0], (which * ff, 0), (ff, local)).T]
            return [cut(arrays[0], (0, 0 if name == "gate" else 1, which * ff), (local, 1, ff))]

        sources = {
            "a": (ssm_in, query_proj), "b": (ssm_in, keyval_proj), "c": (state_proj, step_proj), "out": (ssm_out, attn_out),
            "gate": (gate_up,), "up": (gate_up,), "down": (down_proj,),
        }
        arrays = tie(*sources[name])
        return pick

    own, sent, near, pair, far_z, got = ({} for _ in range(6))
    last = {}

    def gathered(keys, *tokens):
        def tie(*values):
            return tied(*values, *tokens)[: len(values)] if tokens else values

        picks = [takes(*key, tie) for key in keys]
        mine, away = (jnp.concatenate([c for pick in picks for c in pick(which)], axis=1) for which in (zl, 1 - zl))
        return keys, mine, away

    def exchange(group, *tokens):
        keys, mine, away = group
        moved = swap(later(away, *tokens), "zl")
        at = 0
        for key in keys:
            size = widths[key[0]]
            own[key], near[key] = mine[:, at : at + size], moved[:, at : at + size]
            at += size
        return moved

    def prepare(keys, *tokens):
        return exchange(gathered(keys, *tokens))

    def order(way):
        return (last[way],) if way in last else ()

    def send_zh(key, *tokens, parts=1):
        pair[key] = later(jnp.concatenate([own[key], near[key]], axis=0), *order("zh"), *tokens)
        if parts == 1:
            far_z[key] = last["zh"] = swap(pair[key], "zh")
            return
        moved = []
        for part in jnp.split(pair[key], parts, axis=0):
            moved.append(swap(later(part, *moved[-1:]), "zh"))
        far_z[key] = jnp.concatenate(moved, axis=0)
        last["zh"] = moved[-1]

    def send_dp(key, *tokens):
        held, moved = pair[key], far_z[key]
        for axis in dp_axes:
            held = later(jnp.concatenate([held, moved], axis=0), *order("dp"), *tokens)
            moved = last["dp"] = swap(held, axis)
        got[key] = (held, moved)

    blocks = 4 << len(dp_axes)
    chain = [(name, 0) for name in ("a", "b", "c", "out", "gate", "up", "down")]
    for l in range(1, layers):
        chain += [(name, l) for name in ("a", "c", "b", "out", "gate", "up", "down")]
    widths = {
        "a": inner + HD, "b": inner + HD, "c": states // 2 + 128, "out": inner + HD, "gate": ff, "up": ff, "down": ff
    }
    first = prepare(chain[:1])
    second = prepare(chain[1:3], first)
    for key in chain[:3]:
        send_zh(key)
    for key in chain[:3]:
        send_dp(key)
    third = prepare(chain[3:5], far_z[chain[0]])
    send_zh(chain[3])
    near_first = prepare(chain[5:7], far_z[chain[1]], third)
    moved = [5]
    arrived = [far_z[chain[3]], near_first]
    ahead = {1: (0, 3), 4: (3, 5), 7: (5, 7)}
    groups = {}

    def ready_for(l, w, *tokens):
        if l + 1 < layers:
            start, end = ahead[w]
            groups[l, w] = gathered(chain[7 * l + 7 + start : 7 * l + 7 + end], *tokens)
            arrived.extend(groups[l, w][1:])

    def window(value, *tokens, parts=1):
        out = later(value, *arrived, *tokens)
        arrived.clear()
        k = moved[0]
        moved[0] += 1
        if k - 1 < len(chain):
            send_zh(chain[k - 1], *tokens, parts=parts)
            arrived.append(last["zh"])
        if k - 2 < len(chain):
            send_dp(chain[k - 2], *tokens)
            arrived.append(got[chain[k - 2]][1])
        for w in ahead:
            l, rest = divmod(k - 5 - w, 7)
            if not rest and (l, w) in groups:
                arrived.append(exchange(groups[l, w], *tokens))
        return out

    def step_window(value, tokens, *stages):
        out = later(value, *arrived, *tokens)
        arrived.clear()
        for stage in stages:
            arrived.extend(stage.start(*tokens) or ())
        return out


    def mixer_weights(l):
        def both(key, start, size):
            return swap(jnp.concatenate([part[:, start : start + size] for part in got[key]], axis=0), "tb")

        parts = got["a", l] + got["b", l] + got["c", l]
        return both(("b", l), inner, HD), both(("c", l), 0, states // 2), parts, blocks

    lengths = lax.dynamic_index_in_dim(doc_lengths, zh, 0, False)
    aid = lax.dynamic_index_in_dim(adapter_ids, zh, 0, False)
    lengths, positions = tied(lengths, jnp.arange(n, dtype=jnp.int32), far_z["a", 0])[:2]
    seg = segment_of(positions, lengths)
    seg_back = [segment_of(positions - k, lengths) for k in range(1, CONV)]
    starts = (positions // chunk) * chunk
    seg_start = segment_of(starts - 1, lengths)
    seg_end = segment_of(starts + chunk - 1, lengths)
    cols = jnp.stack(
        [(seg == seg_end).astype(F32)]
        + [(seg == s).astype(F32) for s in seg_back]
        + [(seg == seg_start).astype(F32), seg.astype(F32), positions.astype(F32)],
        axis=1,
    )
    cols = jnp.pad(cols, ((0, 0), (0, 128 - cols.shape[1])))
    rows = seg.astype(F32).reshape(n // chunk, 1, chunk)
    places = jnp.pad(jnp.stack([seg.astype(F32), positions.astype(F32)]), ((0, 6), (0, 0)))
    freqs = ROPE_BASE ** (-jnp.arange(HD // 2, dtype=F32) / (HD // 2))
    angles = positions.astype(F32)[:, None] * freqs[None, :]
    cos = jnp.tile(jnp.cos(angles), (1, 2))
    sin = jnp.sin(angles)
    sin = jnp.concatenate([-sin, sin], axis=1)

    def small_of(l, token):
        aid_now = tied(aid, token)[0]

        def pick(table):
            zeros = (0,) * (table.ndim - 2)
            return lax.dynamic_slice(table, (l, aid_now) + zeros, (1, 1) + table.shape[2:]).reshape(table.shape[2:])

        def flat(table):
            return pick(table).T

        inner_e, keyval_e = pick(inner_expand), pick(keyval_expand)
        expand_in = jnp.concatenate(
            [
                half_of(inner_e[:, 0], zl, 1),
                half_of(inner_e[:, 1], zl, 1),
                half_of(pick(query_expand), zl, 1),
                lax.dynamic_slice_in_dim(keyval_e[:, 0], ta * HD, HD, 1),
                lax.dynamic_slice_in_dim(keyval_e[:, 1], ta * HD, HD, 1),
                jnp.pad(half_of(pick(step_expand), zl, 1), ((0, 0), (0, 128 - heads))),
                pick(state_expand).reshape(rank, -1),
            ],
            axis=1,
        )
        shrink_out = jnp.concatenate([half_of(flat(ssmout_shrink), zl, 1), half_of(flat(attnout_shrink), zl, 1)], axis=1)
        gate_e = pick(gateup_expand)
        expand_gu = jnp.concatenate([half_of(gate_e[:, 0], zl, 1), half_of(gate_e[:, 1], zl, 1)], axis=1)
        shrink_down = half_of(flat(down_shrink), zl, 1)
        taps = jnp.pad(
            jnp.concatenate([half_of(conv_inner[l], zl, 1), conv_state[l].reshape(CONV, -1)], axis=1), ((0, 8 - CONV), (0, 0))
        )
        head_rows = jnp.pad(
            jnp.stack([half_of(step_bias[l], zl, 0), jnp.exp(half_of(decay_log[l], zl, 0))]), ((0, 6), (0, 128 - heads))
        )
        skip = jnp.repeat(half_of(skip_gain[l], zl, 0), inner // heads)[None, :]
        return (
            flat(mixer_shrink), expand_in, shrink_out, pick(mixer_expand), flat(ffn_shrink), expand_gu, shrink_down,
            pick(down_expand), taps, head_rows, skip,
        )

    weights, small, saved = [], [], []
    resid = Stages(own_stages(tied(tokens, near["a", 0])[0])).finish().astype(F32)
    grad_stages = None
    token = far_z["a", 0]
    for l in range(layers):
        small.append(small_of(l, token))
        shrink_in, expand_in, shrink_out, expand_out, shrink_gu, expand_gu, shrink_down, expand_down, taps, head_rows, skip = small[l]
        if l:
            gain = window(mixer_gain[l], resid)
            if grad_stages is not None and l + 1 == layers:
                arrived.extend(grad_stages.start(resid))
            ready_for(l - 1, 7, resid)
        else:
            gain = later(mixer_gain[l], far_z["c", l], got["b", l][1], third, cols, cos, sin, places, rows, *small[l])
        h = gather_tokens(rms_norm(resid, gain).astype(BF))
        w_in = mixer_weights(l)
        if not l:
            ready_for(l, 1, far_z["c", l])
        zx, bc, qkv, step, rank_in = call_in(window(me, h), h, shrink_in, expand_in, cos, sin, *w_in, inner, states)
        if l + 1 == layers:
            grad = (grad_stages or Stages(own_stages(out_grad))).finish().astype(F32)
            top_grad = gather_tokens(grad.astype(BF))
        g, hs, pre = call_mamba(window(me, rank_in), zx, bc, step, cols, rows, taps, head_rows, skip, chunk)
        o = call_attn(qkv, cols, places)
        w_out = (got["out", l], blocks)
        keep, send, rank_out = call_out(me, g, o, shrink_out, expand_out, *w_out)
        if l + 1 == layers:
            arrived.append(top_grad)
        mid = resid + scatter_tokens(keep, window(send, rank_out, parts=2))
        token = mid
        h2 = gather_tokens(rms_norm(mid, window(ffn_gain[l], mid)).astype(BF))
        ready_for(l, 4, mid)
        w_ffn = (got["gate", l] + got["up", l] + got["down", l], blocks)
        keep, send, gu, q, rank_gu, rank_down = call_ffn(window(me, h2), h2, shrink_gu, expand_gu, shrink_down, expand_down, *w_ffn)
        if l + 1 < layers:
            send = window(send, rank_down, parts=2)
            if l + 2 == layers:
                grad_stages = Stages(own_stages(out_grad, last["zh"]))
                arrived.extend(grad_stages.start())
            resid_next = mid + scatter_tokens(keep, send)
        else:
            final = Stages(scatter_stages(keep, send))
        weights.append((w_in, w_out, w_ffn))
        saved.append((resid, mid, h, zx, pre, qkv, step, rank_in, g, hs, o, rank_out, h2, gu, q, rank_gu, rank_down))
        resid = resid_next

    seq_axes = tuple(reversed(dp_axes)) + ("zh",)
    adapters = mixer_shrink.shape[1]
    hot = jnp.pad((aid == jnp.arange(adapters, dtype=jnp.int32)).astype(BF), (0, 128 - adapters))
    hot = jnp.broadcast_to(hot[None], (rank, 128))

    def sum_stages(partial, owned, *tokens):
        mine = jnp.concatenate(partial, axis=1).astype(BF)
        size = mine.shape[1]
        for axis in ("tb", "ta"):
            mine = later(mine, *tokens)
            moved = swap(mine, axis)
            tokens = yield [moved]
            mine = (mine.astype(F32) + moved.astype(F32)).astype(BF)
        mine = later(jnp.concatenate([mine] + [value.astype(BF) for value in owned], axis=1), *tokens)
        moved = swap(mine, "zl")
        tokens = yield [moved]
        total = (mine[:, :size].astype(F32) + moved[:, :size].astype(F32)).astype(BF)
        held = jnp.concatenate([total, ordered("zl", mine[:, size:], moved[:, size:], 1), hot], axis=1)[None]
        for axis in ("zh",) + dp_axes:
            held = later(held, *tokens)
            moved = swap(held, axis)
            tokens = yield [moved]
            held = jnp.concatenate([held, moved], axis=0)
        return (held,)

    def place(l, group, tables):
        return call_place(l, layers, group, tables, adapters, rank, width, inner, ff, states, 2 * keyval_proj.shape[3])

    sums = [None] * layers
    at = 2 * inner
    out_stages, older = None, None
    for l in reversed(range(layers)):
        shrink_in, expand_in, shrink_out, expand_out, shrink_gu, expand_gu, shrink_down, expand_down, taps, head_rows, skip = small[l]
        w_in, w_out, w_ffn = weights[l]
        resid, mid, h, zx, pre, qkv, step, rank_in, g, hs, o, rank_out, h2, gu, q, rank_gu, rank_down = saved[l]
        top = l == layers - 1
        dl = top_grad if top else gather_tokens(grad.astype(BF))
        if top:
            now = step_window(me, (dl, rank_down), final)
        else:
            now = step_window(me, (dl,), out_stages, older)
        keep, send, g_shrink_gu, g_expand_gu, g_shrink_down, g_expand_down = call_ffn_back(
            now, dl, h2, gu, q, rank_gu, rank_down, shrink_gu, expand_gu, shrink_down, expand_down, *w_ffn
        )
        of_ffn = [g_shrink_gu, g_expand_down], [g_expand_gu, g_shrink_down]
        if not l:
            rest = Stages(sum_stages(*of_ffn))
        send = step_window(send, (g_expand_gu,), *(() if top else (older,)), *(() if l else (rest,)))
        d_mid = scatter_tokens(keep, send)
        grad = grad + norm_back(mid, step_window(ffn_gain[l], (d_mid,), *(() if l else (rest, rest))), d_mid)
        ml = gather_tokens(grad.astype(BF))
        now = step_window(me, (ml,), *((final,) if top else (out_stages,)), *(() if l else (rest,)))
        dg, do, g_expand_out, g_shrink_out = call_out_back(now, ml, g, o, rank_out, shrink_out, expand_out, *w_out)
        dqkv = call_attn_back(qkv, cols, places, do, cos, sin)
        now = step_window(me, (dqkv,), *((final,) if top else ()), *(() if l else (rest,)))
        dzx, dbc, dstep = call_mamba_back(now, zx, pre, step, cols, rows, taps, head_rows, skip, hs, dg, chunk)
        if top:
            output = mid + final.finish()
            out_stages = Stages(all_stages(output.astype(BF), BF, dstep))
            now = step_window(me, (dstep,), out_stages)
        else:
            now = step_window(me, (dstep,))
        keep, send, g_expand_in, g_shrink_in = call_in_back(
            now, dzx, dbc, dqkv, dstep, h, rank_in, shrink_in, expand_in, *w_in
        )
        send = step_window(send, (g_expand_in,))
        kv = jnp.zeros((rank, 2, keyval_proj.shape[3]), F32)
        own_kv = jnp.stack([g_expand_in[:, at + HD : at + 2 * HD], g_expand_in[:, at + 2 * HD : at + 3 * HD]], axis=1)
        kv = lax.dynamic_update_slice_in_dim(kv, own_kv, ta * HD, 2).reshape(rank, -1)
        partial = [g_expand_out, g_shrink_in, g_expand_in[:, at + 3 * HD + 128 :], kv]
        owned = [g_shrink_out, g_expand_in[:, : at + HD], g_expand_in[:, at + 3 * HD : at + 3 * HD + 128]]
        last_sum = Stages(scatter_stages(keep, send))
        if not l:
            tables = ()
            for k in reversed(range(1, layers)):
                tables = place(k, sums[k].finish(), tables)
            last_sum.start()
            last_sum.start()
            last_sum.start(*tables[-1:])
        d_resid = last_sum.finish()
        grad = grad + norm_back(resid, mixer_gain[l], d_resid)
        if l:
            older = sums[l] = Stages(sum_stages(partial + of_ffn[0], owned + of_ffn[1], d_resid))
            for _ in range(3):
                arrived[:] = older.start()
        else:
            sums[l] = Stages(sum_stages(partial, owned))
            for _ in range(4):
                moving = sums[l].start()
    output = out_stages.finish()
    input_grad = Stages(all_stages(grad.astype(BF), F32, *moving)).finish()

    tables = place(0, sums[0].finish() + rest.finish(), tables)

    def turned(value):
        return jnp.swapaxes(value, 2, 3)

    (
        mixshrink, innerexpand, queryexpand, stateexpand, keyvalexpand, ssmshrink, attnshrink, mixexpand, ffnshrink, gateexpand,
        downshrink, downexpand, step_low, step_high,
    ) = tables
    return (
        output,
        input_grad,
        turned(mixshrink),
        innerexpand,
        jnp.concatenate([step_low[..., :heads], step_high[..., :heads]], axis=-1),
        queryexpand,
        stateexpand,
        keyvalexpand,
        turned(ssmshrink),
        turned(attnshrink),
        mixexpand,
        turned(ffnshrink),
        gateexpand,
        turned(downshrink),
        downexpand,
    )


def solution(mesh):
    dp, ctx, tensor = (mesh.shape[a] for a in ("dp", "ctx", "tensor"))
    bits = dp.bit_length() - 1
    dp_names = tuple("d%d" % k for k in reversed(range(bits)))
    inside = Mesh(
        mesh.devices.reshape((2,) * bits + (2, ctx // 2, 2, tensor // 2)), dp_names + ("zh", "zl", "ta", "tb")
    )
    dp_axes = tuple(reversed(dp_names))
    d, c, t = dp_names, ("zh", "zl"), ("ta", "tb")
    dc = dp_names + c
    return jax.shard_map(
        functools.partial(on_device, dp_axes),
        mesh=inside,
        in_specs=(
            P(d, c, None),
            P(d, c, None),
            P(d, None),
            P(d),
            P(),
            P(),
            P(None, dc, None, t),
            P(None, dc, t),
            P(None, dc, t),
            P(None, dc, None, None),
            P(None, dc, None, None),
            P(None, None, t),
            P(),
            P(None, t),
            P(None, t),
            P(None, t),
            P(None, t, dc),
            P(None, t, dc),
            P(None, dc, None, t),
            P(None, t, dc),
            P(),
            P(None, None, None, None, t),
            P(None, None, None, t),
            P(None, None, None, t),
            P(),
            P(),
            P(None, None, t, None),
            P(None, None, t, None),
            P(),
            P(),
            P(None, None, None, None, t),
            P(None, None, t, None),
            P(),
        ),
        out_specs=(
            P(d, c, None),
            P(d, c, None),
            P(),
            P(None, None, None, None, t),
            P(None, None, None, t),
            P(None, None, None, t),
            P(),
            P(),
            P(None, None, t, None),
            P(None, None, t, None),
            P(),
            P(),
            P(None, None, None, None, t),
            P(None, None, t, None),
            P(),
        ),
        check_vma=False,
    )
```

```python
import functools

import jax
import jax.numpy as jnp
from jax import lax
from jax.experimental import pallas as pl
from jax.experimental.pallas import tpu as pltpu
from jax.sharding import Mesh
from jax.sharding import PartitionSpec as P

HD = 128
CONV = 4
EPS = 1e-05
ROPE_BASE = 10000.0
HIGHEST = lax.Precision.HIGHEST
BF = jnp.bfloat16
F32 = jnp.float32
TOK = ("ta", "zl", "tb")
ROWS = 512
TILE = 256
AHEAD = 4
BACK = 2
COST = 1000
VMEM = 56 * 1024 * 1024


def dot(a, b, **kw):
    return jnp.dot(a, b, preferred_element_type=F32, **kw)


def dot_nt(a, b):
    return lax.dot_general(a, b, (((1,), (1,)), ((), ())), preferred_element_type=F32)


def dot_tn(a, b):
    return lax.dot_general(a, b, (((0,), (0,)), ((), ())), preferred_element_type=F32)


def sigmoid(v):
    return 0.5 * jnp.tanh(0.5 * v) + 0.5


def swap(value, axis):
    return lax.ppermute(value, axis, [(0, 1), (1, 0)])


def rms_norm(stream, gain):
    return stream * lax.rsqrt(jnp.mean(stream * stream, axis=-1, keepdims=True) + EPS) * gain


def norm_back(stream, gain, upstream):
    scale = lax.rsqrt(jnp.mean(stream * stream, axis=-1, keepdims=True) + EPS)
    weighted = upstream * gain
    inner = jnp.mean(stream * weighted, axis=-1, keepdims=True)
    return scale * weighted - stream * (scale * scale * scale * inner)


def segment_of(positions, lengths):
    ends = jnp.cumsum(lengths)
    inside = jnp.sum((positions[:, None] >= ends[None, :]).astype(jnp.int32), axis=1)
    return jnp.where(positions < 0, -1, inside)


def gather_tokens(own):
    return lax.all_gather(own, TOK, axis=0, tiled=True)


def scatter_stages(keep, send, *tokens):
    b, half = keep.shape[0] // 4, keep.shape[1] // 2
    recv = swap(later(send, *tokens), "tb")
    tokens = yield [recv]

    def pair(rows, cols):
        return keep[rows, cols].astype(F32) + recv[rows, cols].astype(F32)

    first, second = slice(0, half), slice(half, 2 * half)

    def odd(cols, k):
        return jnp.concatenate([pair(slice(k * b, k * b + b), cols), pair(slice((k + 2) * b, (k + 3) * b), cols)], axis=0)

    got_a = swap(later(pair(slice(2 * b, 4 * b), first).astype(BF), *tokens), "ta")
    got_b = swap(later(odd(second, 1).astype(BF), *tokens), "zl")
    tokens = yield [got_a, got_b]
    sum_a = pair(slice(0, 2 * b), first) + got_a.astype(F32)
    sum_b = odd(second, 0) + got_b.astype(F32)
    last_a = swap(later(sum_a[b:].astype(BF), *tokens), "zl")
    last_b = swap(later(sum_b[b:].astype(BF), *tokens), "ta")
    yield [last_a, last_b]
    return jnp.concatenate([sum_a[:b] + last_a.astype(F32), sum_b[:b] + last_b.astype(F32)], axis=1)


def scatter_tokens(keep, send):
    return Stages(scatter_stages(keep, send)).finish()


class Stages:
    def __init__(self, chain):
        self.chain, self.begun, self.result = chain, False, None

    def start(self, *tokens):
        try:
            if self.begun:
                return self.chain.send(tokens)
            self.begun = True
            return next(self.chain)
        except StopIteration as end:
            self.result = end.value
            return None

    def finish(self):
        while self.start() is not None:
            pass
        return self.result


def later(value, *tokens):
    return tied(value, *tokens)[0] if tokens else value


def tied(*values):
    return lax.optimization_barrier(values)


def blocks_of(me_ref, parts, rows):
    out, j = [], 0
    for part in parts:
        for k in range(part.shape[0] // rows):
            at = pl.multiple_of((j ^ me_ref[0]) * rows, rows)
            out.append((part.at[pl.ds(k * rows, rows), :], pl.ds(at, rows)))
            j += 1
    return out


def weight_copies(me_ref, parts, held, sem):
    rows = held.shape[0] // sem.shape[0]
    return [
        pltpu.make_async_copy(block, held.at[at, :], sem.at[j]) for j, (block, at) in enumerate(blocks_of(me_ref, parts, rows))
    ]


def at_first(do, copies):
    @pl.when(pl.program_id(0) == 0)
    def _():
        for copy in copies():
            getattr(copy, do)()


def mixer_copies(me_ref, parts, far_kv, far_bc, held, sem):
    rows = held.shape[0] // sem.shape[1]
    states = far_bc.shape[1]
    inner = (held.shape[1] - 3 * HD - 2 * states - 128) // 2
    core = me_ref[3]

    def key(which):
        return pl.ds(pl.multiple_of(2 * inner + HD + which * HD, HD), HD)

    def state(which):
        return pl.ds(pl.multiple_of(2 * inner + 3 * HD + 128 + which * states, HD), states)

    first, second, third = (blocks_of(me_ref, part, rows) for part in parts)
    copies = []
    for j, ((one, at), (two, _), (three, _)) in enumerate(zip(first, second, third)):
        here = pl.ds(j * rows, rows)
        for k, (source, cols) in enumerate(
            (
                (one.at[:, pl.ds(0, inner)], pl.ds(0, inner)),
                (one.at[:, pl.ds(inner, HD)], pl.ds(2 * inner, HD)),
                (two.at[:, pl.ds(0, inner)], pl.ds(inner, inner)),
                (two.at[:, pl.ds(inner, HD)], key(core)),
                (three.at[:, pl.ds(0, states)], state(core)),
                (three.at[:, pl.ds(states, 128)], pl.ds(2 * inner + 3 * HD, 128)),
                (far_kv.at[here, :], key(1 - core)),
                (far_bc.at[here, :], state(1 - core)),
            )
        ):
            copies.append(pltpu.make_async_copy(source, held.at[at, cols], sem.at[k, j]))
    return copies


def turned_rows(me_ref, size):
    b = size // 4
    out = []
    for core in (me_ref[3], 1 - me_ref[3]):
        for z in range(2):
            out.append(pl.ds(pl.multiple_of(((z ^ me_ref[2]) * 2 + core) * b, b), b))
    return out


def emit(keep_ref, send_ref, cols, value):
    half = value.shape[0] // 2
    low = value.astype(BF)
    keep_ref[:, cols] = low[:half]
    send_ref[:, cols] = low[half:]


def in_kernel(me_ref, h_ref, shrink_ref, expand_ref, cos_ref, sin_ref, far_kv, far_bc, *rest):
    parts, rest = (rest[0:2], rest[2:4], rest[4:6]), rest[6:]
    zx_ref, bc_ref, qkv_ref, step_ref, rank_ref, held, sem = rest
    inner = zx_ref.shape[1]
    states = bc_ref.shape[1]

    def copies(wide):
        return lambda: [
            copy
            for k, copy in enumerate(mixer_copies(me_ref, parts, far_kv, far_bc, held, sem))
            if (k % sem.shape[0] in (0, 2)) == wide
        ]

    at_first("start", copies(True))
    h = h_ref[...]
    rank = dot_nt(h, shrink_ref[...]).astype(BF)
    rank_ref[...] = rank
    at_first("wait", copies(True))
    at_first("start", copies(False))

    def part(at, width):
        cols = slice(at, at + width)
        return dot(h, held[:, cols]) + dot(rank, expand_ref[:, cols])

    for at in range(0, inner, 256):
        zx_ref[:, at : at + 256] = part(at, 256).astype(BF)
    at_first("wait", copies(False))
    qk = part(inner, 2 * HD)
    cos, sin = cos_ref[...], sin_ref[...]
    for k in range(2):
        head = qk[:, k * HD : (k + 1) * HD]
        turned = head * cos + pltpu.roll(head, HD // 2, 1) * sin
        qkv_ref[:, k * HD : (k + 1) * HD] = turned.astype(BF)
    last = part(inner + 2 * HD, HD + 128)
    qkv_ref[:, 2 * HD :] = last[:, :HD].astype(BF)
    step_ref[...] = last[:, HD:]
    for at in range(0, states, 256):
        bc_ref[:, at : at + 256] = part(inner + 3 * HD + 128 + at, 256).astype(BF)


def in_back_kernel(
    me_ref, dzx_ref, dbc_ref, dqkv_ref, dstep_ref, h_ref, rank_ref, shrink_ref, expand_ref, far_kv, far_bc, *rest
):
    parts, rest = (rest[0:2], rest[2:4], rest[4:6]), rest[6:]
    keep_ref, send_ref, gexpand_ref, gshrink_ref, held, du, low, sem = rest
    inner = dzx_ref.shape[1]

    def copies():
        return mixer_copies(me_ref, parts, far_kv, far_bc, held, sem)

    at_first("start", copies)

    @pl.when(pl.program_id(0) == 0)
    def _():
        gexpand_ref[...] = jnp.zeros_like(gexpand_ref)
        gshrink_ref[...] = jnp.zeros_like(gshrink_ref)

    size = du.shape[0]
    b = size // 4
    rank = rank_ref[...]
    where = turned_rows(me_ref, size)
    at = 0
    for source in (dzx_ref, dqkv_ref, dstep_ref, dbc_ref):
        wide = source.shape[1]
        gexpand_ref[:, at : at + wide] += dot_tn(rank, source[...])
        for k in range(4):
            du[k * b : (k + 1) * b, at : at + wide] = source[where[k], :]
        at += wide
    drank = dot_nt(du[...], expand_ref[...]).astype(BF)
    for k in range(4):
        low[where[k], :] = drank[k * b : (k + 1) * b]
    natural = low[...]
    for at in range(0, h_ref.shape[1], 256):
        cols = slice(at, at + 256)
        gshrink_ref[:, cols] += dot_tn(natural, h_ref[:, cols])
    at_first("wait", copies)
    for at in range(0, h_ref.shape[1], 256):
        cols = slice(at, at + 256)
        emit(keep_ref, send_ref, cols, dot_nt(du[...], held[cols, :]) + dot(drank, shrink_ref[:, cols]))


def out_kernel(me_ref, g_ref, o_ref, shrink_ref, expand_ref, *rest):
    pieces, rest = rest[:2], rest[2:]
    keep_ref, send_ref, rank_ref, held, go, sem = rest

    def copies():
        return weight_copies(me_ref, pieces, held, sem)

    at_first("start", copies)
    inner = g_ref.shape[1]
    size = go.shape[0]
    b = size // 4
    where = turned_rows(me_ref, size)
    for k in range(4):
        go[k * b : (k + 1) * b, :inner] = g_ref[where[k], :]
        go[k * b : (k + 1) * b, inner:] = o_ref[where[k], :]
    rank = dot_nt(go[...], shrink_ref[...]).astype(BF)
    for k in range(4):
        rank_ref[where[k], :] = rank[k * b : (k + 1) * b]
    at_first("wait", copies)
    for at in range(0, expand_ref.shape[1], 256):
        cols = slice(at, at + 256)
        emit(keep_ref, send_ref, cols, dot_nt(go[...], held[cols, :]) + dot(rank, expand_ref[:, cols]))


def out_back_kernel(me_ref, ml_ref, g_ref, o_ref, rank_ref, shrink_ref, expand_ref, *rest):
    pieces, rest = rest[:2], rest[2:]
    dg_ref, do_ref, gexpand_ref, gshrink_ref, held, sem = rest

    def copies():
        return weight_copies(me_ref, pieces, held, sem)

    at_first("start", copies)

    @pl.when(pl.program_id(0) == 0)
    def _():
        gexpand_ref[...] = jnp.zeros_like(gexpand_ref)
        gshrink_ref[...] = jnp.zeros_like(gshrink_ref)

    inner = g_ref.shape[1]
    ml = ml_ref[...]
    drank = dot_nt(ml, expand_ref[...]).astype(BF)
    rank = rank_ref[...]
    for at in range(0, ml.shape[1], 256):
        cols = slice(at, at + 256)
        gexpand_ref[:, cols] += dot_tn(rank, ml_ref[:, cols])
    gshrink_ref[:, :inner] += dot_tn(drank, g_ref[...])
    gshrink_ref[:, inner:] += dot_tn(drank, o_ref[...])
    at_first("wait", copies)
    for at in range(0, held.shape[1], 256):
        cols = slice(at, at + 256)
        got = (dot(ml, held[:, cols]) + dot(drank, shrink_ref[:, cols])).astype(BF)
        for to in (at, at + 128):
            if to < inner:
                dg_ref[:, to : to + 128] = got[:, to - at : to - at + 128]
            else:
                do_ref[:, to - inner : to - inner + 128] = got[:, to - at : to - at + 128]


def ffn_kernel(me_ref, h_ref, shrink_ref, expand_ref, dshrink_ref, dexpand_ref, *rest):
    (gates, ups, downs), rest = (rest[0:2], rest[2:4], rest[4:6]), rest[6:]
    keep_ref, send_ref, gu_ref, q_ref, rank_ref, drank_ref, held, dheld, qt, sem = rest
    half = dheld.shape[1]

    def both():
        return weight_copies(me_ref, gates, held.at[:, pl.ds(0, half)], sem.at[0]) + weight_copies(
            me_ref, ups, held.at[:, pl.ds(half, half)], sem.at[1]
        )

    def down():
        return weight_copies(me_ref, downs, dheld, sem.at[2])

    at_first("start", lambda: both() + down())
    h = h_ref[...]
    rank = dot_nt(h, shrink_ref[...]).astype(BF)
    rank_ref[...] = rank
    at_first("wait", both)
    for at in range(0, half, 256):
        one = slice(at, at + 256)
        two = slice(half + at, half + at + 256)
        gate = dot(h, held[:, one]) + dot(rank, expand_ref[:, one])
        up = dot(h, held[:, two]) + dot(rank, expand_ref[:, two])
        gu_ref[:, one] = gate.astype(BF)
        gu_ref[:, two] = up.astype(BF)
        q_ref[:, one] = (gate * sigmoid(gate) * up).astype(BF)
    size = qt.shape[0]
    b = size // 4
    where = turned_rows(me_ref, size)
    for k in range(4):
        qt[k * b : (k + 1) * b, :] = q_ref[where[k], :]
    drank = dot_nt(qt[...], dshrink_ref[...]).astype(BF)
    for k in range(4):
        drank_ref[where[k], :] = drank[k * b : (k + 1) * b]
    at_first("wait", down)
    for at in range(0, dexpand_ref.shape[1], 256):
        cols = slice(at, at + 256)
        emit(keep_ref, send_ref, cols, dot_nt(qt[...], dheld[cols, :]) + dot(drank, dexpand_ref[:, cols]))


def ffn_back_kernel(
    me_ref, dl_ref, h_ref, gu_ref, q_ref, rank_ref, drank_ref, shrink_ref, expand_ref, dshrink_ref, dexpand_ref, *rest
):
    (gates, ups, downs), rest = (rest[0:2], rest[2:4], rest[4:6]), rest[6:]
    keep_ref, send_ref, gshrink_ref, gexpand_ref, gdshrink_ref, gdexpand_ref, held, dheld, dgu, turned, low, sem = rest
    half = dheld.shape[1]

    def both():
        return weight_copies(me_ref, gates, held.at[:, pl.ds(0, half)], sem.at[0]) + weight_copies(
            me_ref, ups, held.at[:, pl.ds(half, half)], sem.at[1]
        )

    def down():
        return weight_copies(me_ref, downs, dheld, sem.at[2])

    at_first("start", lambda: down() + both())

    @pl.when(pl.program_id(0) == 0)
    def _():
        for ref in (gshrink_ref, gexpand_ref, gdshrink_ref, gdexpand_ref):
            ref[...] = jnp.zeros_like(ref)

    dl = dl_ref[...]
    ddrank = dot_nt(dl, dexpand_ref[...]).astype(BF)
    down_rank = drank_ref[...]
    for at in range(0, dl.shape[1], 256):
        cols = slice(at, at + 256)
        gdexpand_ref[:, cols] += dot_tn(down_rank, dl_ref[:, cols])
    gdshrink_ref[...] += dot_tn(ddrank, q_ref[...])
    rank = rank_ref[...]
    at_first("wait", down)
    for at in range(0, half, 256):
        one = slice(at, at + 256)
        two = slice(half + at, half + at + 256)
        dq = dot(dl, dheld[:, one]) + dot(ddrank, dshrink_ref[:, one])
        gate = gu_ref[:, one].astype(F32)
        up = gu_ref[:, two].astype(F32)
        sig = sigmoid(gate)
        dgu[:, one] = (dq * up * sig * (1.0 + gate * (1.0 - sig))).astype(BF)
        dgu[:, two] = (dq * gate * sig).astype(BF)
    gexpand_ref[...] += dot_tn(rank, dgu[...])
    size = dgu.shape[0]
    b = size // 4
    where = turned_rows(me_ref, size)
    for k in range(4):
        turned[k * b : (k + 1) * b, :] = dgu[where[k], :]
    drank = dot_nt(turned[...], expand_ref[...]).astype(BF)
    for k in range(4):
        low[where[k], :] = drank[k * b : (k + 1) * b]
    natural = low[...]
    for at in range(0, h_ref.shape[1], 256):
        cols = slice(at, at + 256)
        gshrink_ref[:, cols] += dot_tn(natural, h_ref[:, cols])
    at_first("wait", both)
    for at in range(0, h_ref.shape[1], 256):
        cols = slice(at, at + 256)
        emit(keep_ref, send_ref, cols, dot_nt(turned[...], held[cols, :]) + dot(drank, shrink_ref[:, cols]))


def attend(q, k, v, place_q, seg_q, place_k, seg_k):
    scores = dot_nt(q, k) * HD ** (-0.5)
    seen = (place_q >= place_k) & (seg_q == seg_k)
    masked = jnp.where(seen, scores, -1e30)
    top = jnp.max(masked, axis=-1, keepdims=True)
    raised = jnp.exp(masked - top)
    probs = raised * (1.0 / jnp.sum(raised, axis=-1, keepdims=True))
    low = probs.astype(BF)
    return probs, low, dot(low, v)


def attn_kernel(qkv_ref, col_ref, row_ref, o_ref):
    for start in range(0, o_ref.shape[0], TILE):
        at, seen = slice(start, start + TILE), slice(0, start + TILE)
        _, _, out = attend(
            qkv_ref[at, :HD], qkv_ref[seen, HD : 2 * HD], qkv_ref[seen, 2 * HD :],
            col_ref[at, 6:7], col_ref[at, 5:6], row_ref[1:2, seen], row_ref[0:1, seen],
        )
        o_ref[at, :] = out.astype(BF)


def attn_back_kernel(qkv_ref, col_ref, row_ref, do_ref, cos_ref, sin_ref, dqkv_ref, dk_sum, dv_sum):
    def back(turned, cos, sin):
        return ((turned * cos - pltpu.roll(turned, HD // 2, 1) * sin) * HD ** (-0.5)).astype(BF)

    dk_sum[...] = jnp.zeros_like(dk_sum)
    dv_sum[...] = jnp.zeros_like(dv_sum)
    for start in range(0, do_ref.shape[0], TILE):
        at, seen = slice(start, start + TILE), slice(0, start + TILE)
        q, k, v, do = qkv_ref[at, :HD], qkv_ref[seen, HD : 2 * HD], qkv_ref[seen, 2 * HD :], do_ref[at, :]
        probs, low, out = attend(
            q, k, v, col_ref[at, 6:7], col_ref[at, 5:6], row_ref[1:2, seen], row_ref[0:1, seen]
        )
        delta = jnp.sum(do.astype(F32) * out, axis=-1, keepdims=True)
        ds = (probs * (dot_nt(do, v) - delta)).astype(BF)
        dqkv_ref[at, :HD] = back(dot(ds, k), cos_ref[at, :], sin_ref[at, :])
        dk_sum[seen, :] += dot_tn(ds, q)
        dv_sum[seen, :] += dot_tn(low, do)
    dqkv_ref[:, HD : 2 * HD] = back(dk_sum[...], cos_ref[...], sin_ref[...])
    dqkv_ref[:, 2 * HD :] = dv_sum[...].astype(BF)


def spread(cols, first, pairs):
    rows = cols.shape[0]
    low = lax.broadcasted_iota(jnp.int32, (rows, 128), 1) < 64
    return jnp.concatenate(
        [
            jnp.where(low, cols[:, first + 2 * p : first + 2 * p + 1], cols[:, first + 2 * p + 1 : first + 2 * p + 2])
            for p in range(pairs)
        ],
        axis=1,
    )


def exact(ones, value):
    high = value.astype(BF)
    return dot(ones, high) + dot(ones, (value - high.astype(F32)).astype(BF))


def collected(value, ones):
    high = value.astype(BF)
    return dot(high, ones) + dot((value - high.astype(F32)).astype(BF), ones)


def span(pre, step, col_ref, row_ref, tri_ref, heads_ref, inner):
    count = pre.shape[0]
    states = pre.shape[1] - inner
    pairs = inner // 128
    sig = sigmoid(pre)
    conv = pre * sig
    x = conv[:, :inner]
    b = conv[:, inner : inner + states // 2].astype(BF)
    c = conv[:, inner + states // 2 :].astype(BF)
    raw = step + heads_ref[0:1, :]
    dt = jnp.maximum(raw, 0.0) + jnp.log1p(jnp.exp(-jnp.abs(raw)))
    tri = tri_ref[0]
    cum = exact(tri, -heads_ref[1:2, :] * dt)
    keep = (col_ref[:, 5:6] == row_ref[...]) & (tri > 0)
    carry, tail = col_ref[:, 4:5], col_ref[:, 0:1]
    ecum = jnp.exp(cum) * carry
    weight = jnp.exp(cum[count - 1 :, :] - cum) * tail
    turned = jnp.transpose(cum)
    decays = [
        jnp.where(keep, jnp.exp(cum[:, h : h + 1] - turned[h : h + 1, :]), 0.0) for h in range(2 * pairs)
    ]
    scores = dot_nt(c, b)
    mixing = [(scores * decay).astype(BF) for decay in decays]
    xdt = x * spread(dt, 0, pairs)
    return sig, x, b, c, raw, dt, ecum, weight, decays, mixing, xdt, pairs


def halves(value):
    low = lax.broadcasted_iota(jnp.int32, value.shape, 1) < 64
    zero = jnp.zeros_like(value)
    return jnp.concatenate([jnp.where(low, value, zero), jnp.where(low, zero, value)], axis=0)


def mamba_kernel(
    me_ref, zx_ref, zxp_ref, bc_ref, bcp_ref, step_ref, col_ref, row_ref, taps_ref, heads_ref, skip_ref, tri_ref,
    g_ref, hs_ref, pre_ref, state, ext,
):
    @pl.when(pl.program_id(0) == 0)
    def _():
        state[...] = jnp.zeros_like(state)

    count, inner = zx_ref.shape[0], zx_ref.shape[1] // 2
    ext[0:8, :inner] = zxp_ref[8:16, inner:].astype(F32)
    ext[0:8, inner:] = bcp_ref[8:16, :].astype(F32)
    ext[8:, :inner] = zx_ref[:, inner:].astype(F32)
    ext[8:, inner:] = bc_ref[...].astype(F32)
    chunk = tri_ref.shape[1]
    for k in range(count // chunk):
        at = slice(k * chunk, (k + 1) * chunk)
        pre = taps_ref[0:1, :] * ext[8 + k * chunk : 8 + (k + 1) * chunk, :]
        for tap in range(1, CONV):
            first = 8 - tap + k * chunk
            pre = pre + taps_ref[tap : tap + 1, :] * (ext[first : first + chunk, :] * col_ref[at, tap : tap + 1])
        pre_ref[at, :] = pre.astype(BF)
        _, x, b, c, _, _, ecum, weight, _, mixing, xdt, pairs = span(
            pre, step_ref[at, :], col_ref.at[at, :], row_ref.at[k], tri_ref, heads_ref, inner
        )
        old = state[...]
        held = old.astype(BF)
        hs_ref[k] = held
        low = xdt.astype(BF)
        direct = jnp.concatenate(
            [
                dot(jnp.concatenate(mixing[2 * p : 2 * p + 2], axis=1), halves(low[:, 128 * p : 128 * p + 128]))
                for p in range(pairs)
            ],
            axis=1,
        )
        wide = spread(ecum, 0, pairs)
        y = direct + dot(c, held) * wide + skip_ref[...] * x
        z = zx_ref[at, :inner].astype(F32)
        g_ref[at, :] = (y * z * sigmoid(z)).astype(BF)
        state[...] = old * wide[chunk - 1 :, :] + dot_tn(b, (xdt * spread(weight, 0, pairs)).astype(BF))


def mamba_back_kernel(
    me_ref, z_ref, pre_ref, step_ref, col_ref, row_ref, taps_ref, heads_ref, skip_ref, tri_ref, collect_ref, hs_ref, dg_ref,
    dzx_ref, dbc_ref, dstep_ref, dstate, ext, later_rows, cross,
):
    @pl.when(pl.program_id(0) == 0)
    def _():
        dstate[...] = jnp.zeros_like(dstate)
        later_rows[...] = jnp.zeros_like(later_rows)
        cross[...] = jnp.zeros_like(cross)

    chunk = tri_ref.shape[1]
    for k in reversed(range(z_ref.shape[0] // chunk)):
        at = pl.ds(k * chunk, chunk)
        mamba_back_chunk(
            z_ref.at[at, :], pre_ref.at[at, :], step_ref.at[at, :], col_ref.at[at, :], row_ref.at[k], taps_ref, heads_ref, skip_ref,
            tri_ref, collect_ref, hs_ref.at[k], dg_ref.at[at, :], dzx_ref.at[at, :], dbc_ref.at[at, :], dstep_ref.at[at, :],
            dstate, ext, later_rows, cross,
        )


def mamba_back_chunk(
    z_ref, pre_ref, step_ref, col_ref, row_ref, taps_ref, heads_ref, skip_ref, tri_ref, collect_ref, hs_ref, dg_ref,
    dzx_ref, dbc_ref, dstep_ref, dstate, ext, later_rows, cross,
):
    pre = pre_ref[...].astype(F32)
    sig, x, b, c, raw, dt, ecum, weight, decays, mixing, xdt, pairs = span(
        pre, step_ref[...], col_ref, row_ref, tri_ref, heads_ref, z_ref.shape[1]
    )
    count, inner = x.shape
    state = hs_ref[...]
    z = z_ref[...].astype(F32)
    dg = dg_ref[...].astype(F32)
    sig_z = sigmoid(z)
    dy = dg * z * sig_z
    dyl = dy.astype(BF)
    low = xdt.astype(BF)
    dst = dstate[...]
    dsl = dst.astype(BF)
    directs, dxdts = [], []
    dscores = jnp.zeros((count, count), F32)
    for p in range(pairs):
        lanes = slice(128 * p, 128 * p + 128)
        dy_two = halves(dyl[:, lanes])
        x_two = halves(low[:, lanes])
        directs.append(dot(jnp.concatenate(mixing[2 * p : 2 * p + 2], axis=1), x_two))
        dxdts.append(dot_tn(jnp.concatenate(mixing[2 * p : 2 * p + 2], axis=0), dy_two))
        dmix = dot_nt(dy_two, low[:, lanes])
        dscores = dscores + decays[2 * p] * dmix[:count] + decays[2 * p + 1] * dmix[count:]
    wide = spread(ecum, 0, pairs)
    tails = spread(weight, 0, pairs)
    core = jnp.concatenate(directs, axis=1) + dot(c, state) * wide
    dxdt = jnp.concatenate(dxdts, axis=1) + dot(b, dsl) * tails
    y = core + skip_ref[...] * x
    dz = dg * y * (sig_z * (1.0 + z * (1.0 - sig_z)))
    dsc = dscores.astype(BF)
    into = (dy * wide).astype(BF)
    dc = dot(dsc, b) + dot_nt(into, state)
    db = dot_tn(dsc, c) + dot_nt((xdt * tails).astype(BF), dsl)
    wide_dt = spread(dt, 0, pairs)
    dx = dxdt * wide_dt + skip_ref[...] * dy
    collect = collect_ref[...]
    flow = dyl.astype(F32) * core - low.astype(F32) * dxdt
    dcum = collected(flow, collect)
    rows = lax.broadcasted_iota(jnp.int32, (count, 128), 0)
    dcum = dcum + jnp.where(rows == count - 1, cross[0:1, :], 0.0)
    da = exact(tri_ref[1], dcum)
    ddt = collected(x * dxdt, collect) - heads_ref[1:2, :] * da
    lanes = lax.broadcasted_iota(jnp.int32, (count, 128), 1)
    dstep_ref[...] = jnp.where(lanes < 2 * pairs, ddt * sigmoid(raw), 0.0).astype(BF)
    dnew = dst * wide[count - 1 :, :] + dot_tn(c, into)
    dstate[...] = dnew
    held = jnp.sum(dnew * state.astype(F32), axis=0, keepdims=True)
    cross[...] = collected(jnp.broadcast_to(held, (8, inner)), collect)
    dzx_ref[:, :inner] = dz.astype(BF)
    dpre = jnp.concatenate([dx, db, dc], axis=1) * (sig * (1.0 + pre * (1.0 - sig)))
    total = taps_ref[0:1, :] * dpre
    for k in range(1, CONV):
        masked = dpre * col_ref[:, k : k + 1]
        ext[0:count, :] = masked
        ext[count:, :] = later_rows[k - 1]
        total = total + taps_ref[k : k + 1, :] * ext[k : k + count, :]
        later_rows[k - 1] = masked[0:8, :]
    dzx_ref[:, inner:] = total[:, :inner].astype(BF)
    dbc_ref[...] = total[:, inner:].astype(BF)


def whole(shape):
    return pl.BlockSpec(shape, lambda i, me: (0,) * len(shape))


def rows_of(width, rows=ROWS):
    return pl.BlockSpec((rows, width), lambda i, me: (i, 0))


ANY = pl.BlockSpec(memory_space=pl.ANY)


def params():
    return pltpu.CompilerParams(vmem_limit_bytes=VMEM)


def sds(shape, dtype):
    return jax.ShapeDtypeStruct(shape, dtype)


def half_rows(width):
    return pl.BlockSpec((ROWS // 2, width), lambda i, me: (i ^ me[1], 0))


def sems(count):
    return pltpu.SemaphoreType.DMA((count,))


def cost(macs, size):
    return pl.CostEstimate(flops=2 * macs // COST, bytes_accessed=size // COST, transcendentals=0)


def call_in(me, h, shrink, expand, cos, sin, far_kv, far_bc, parts, blocks, inner, states):
    n, d = h.shape
    r = shrink.shape[0]
    width = expand.shape[1]
    return pl.pallas_call(
        in_kernel,
        grid_spec=pltpu.PrefetchScalarGridSpec(
            num_scalar_prefetch=1,
            grid=(n // ROWS,),
            in_specs=[rows_of(d), whole((r, d)), whole((r, width)), rows_of(HD), rows_of(HD)]
            + [ANY] * (2 + len(parts)),
            out_specs=[rows_of(2 * inner), rows_of(states), rows_of(3 * HD), rows_of(128), rows_of(r)],
            scratch_shapes=[pltpu.VMEM((d, width), BF), pltpu.SemaphoreType.DMA((8, blocks))],
        ),
        out_shape=[sds((n, 2 * inner), BF), sds((n, states), BF), sds((n, 3 * HD), BF), sds((n, 128), F32), sds((n, r), BF)],
        compiler_params=params(),
        cost_estimate=cost(n * d * width, 2 * (n * d + d * width + n * width)),
        name="mixer_in",
    )(me, h, shrink, expand, cos, sin, far_kv, far_bc, *parts)


def call_in_back(me, dzx, dbc, dqkv, dstep, h, rank, shrink, expand, far_kv, far_bc, parts, blocks):
    n, d = h.shape
    r, width = expand.shape
    return pl.pallas_call(
        in_back_kernel,
        grid_spec=pltpu.PrefetchScalarGridSpec(
            num_scalar_prefetch=1,
            grid=(n // ROWS,),
            in_specs=[
                rows_of(dzx.shape[1]), rows_of(dbc.shape[1]), rows_of(3 * HD), rows_of(128), rows_of(d), rows_of(r),
                whole((r, d)), whole((r, width)),
            ]
            + [ANY] * (2 + len(parts)),
            out_specs=[half_rows(d), half_rows(d), whole((r, width)), whole((r, d))],
            scratch_shapes=[
                pltpu.VMEM((d, width), BF), pltpu.VMEM((ROWS, width), BF), pltpu.VMEM((ROWS, r), BF),
                pltpu.SemaphoreType.DMA((8, blocks)),
            ],
        ),
        out_shape=[sds((n // 2, d), BF)] * 2 + [sds((r, width), F32), sds((r, d), F32)],
        compiler_params=params(),
        cost_estimate=cost(n * d * width, 2 * (2 * n * d + d * width + n * width)),
        name="mixer_in_back",
    )(me, dzx, dbc, dqkv, dstep, h, rank, shrink, expand, far_kv, far_bc, *parts)


def call_out(me, g, o, shrink, expand, pieces, blocks):
    n, inner = g.shape
    r, d = expand.shape
    width = shrink.shape[1]
    return pl.pallas_call(
        out_kernel,
        grid_spec=pltpu.PrefetchScalarGridSpec(
            num_scalar_prefetch=1,
            grid=(n // ROWS,),
            in_specs=[rows_of(inner), rows_of(HD), whole((r, width)), whole((r, d))] + [ANY] * len(pieces),
            out_specs=[half_rows(d), half_rows(d), rows_of(r)],
            scratch_shapes=[pltpu.VMEM((d, width), BF), pltpu.VMEM((ROWS, width), BF), sems(blocks)],
        ),
        out_shape=[sds((n // 2, d), BF)] * 2 + [sds((n, r), BF)],
        compiler_params=params(),
        cost_estimate=cost(n * d * width, 2 * (n * d + d * width + n * width)),
        name="mixer_out",
    )(me, g, o, shrink, expand, *pieces)


def call_out_back(me, ml, g, o, rank, shrink, expand, pieces, blocks):
    n, inner = g.shape
    r, d = expand.shape
    width = shrink.shape[1]
    return pl.pallas_call(
        out_back_kernel,
        grid_spec=pltpu.PrefetchScalarGridSpec(
            num_scalar_prefetch=1,
            grid=(n // ROWS,),
            in_specs=[rows_of(d), rows_of(inner), rows_of(HD), rows_of(r), whole((r, width)), whole((r, d))] + [ANY] * len(pieces),
            out_specs=[rows_of(inner), rows_of(HD), whole((r, d)), whole((r, width))],
            scratch_shapes=[pltpu.VMEM((d, width), BF), sems(blocks)],
        ),
        out_shape=[sds((n, inner), BF), sds((n, HD), BF), sds((r, d), F32), sds((r, width), F32)],
        compiler_params=params(),
        cost_estimate=cost(n * d * width, 2 * (n * d + d * width + n * width)),
        name="mixer_out_back",
    )(me, ml, g, o, rank, shrink, expand, *pieces)


def call_ffn(me, h, shrink, expand, dshrink, dexpand, parts, blocks):
    n, d = h.shape
    r, both = expand.shape
    half = both // 2
    return pl.pallas_call(
        ffn_kernel,
        grid_spec=pltpu.PrefetchScalarGridSpec(
            num_scalar_prefetch=1,
            grid=(n // ROWS,),
            in_specs=[rows_of(d), whole((r, d)), whole((r, both)), whole((r, half)), whole((r, d))] + [ANY] * len(parts),
            out_specs=[half_rows(d), half_rows(d), rows_of(both), rows_of(half), rows_of(r), rows_of(r)],
            scratch_shapes=[
                pltpu.VMEM((d, both), BF), pltpu.VMEM((d, half), BF), pltpu.VMEM((ROWS, half), BF), pltpu.SemaphoreType.DMA((3, blocks))
            ],
        ),
        out_shape=[sds((n // 2, d), BF)] * 2 + [sds((n, both), BF), sds((n, half), BF), sds((n, r), BF), sds((n, r), BF)],
        compiler_params=params(),
        cost_estimate=cost(3 * n * d * half, 2 * (2 * n * d + 3 * d * half + 3 * n * half)),
        name="ffn",
    )(me, h, shrink, expand, dshrink, dexpand, *parts)


def call_ffn_back(me, dl, h, gu, q, rank, drank, shrink, expand, dshrink, dexpand, parts, blocks):
    n, d = h.shape
    r, both = expand.shape
    half = both // 2
    return pl.pallas_call(
        ffn_back_kernel,
        grid_spec=pltpu.PrefetchScalarGridSpec(
            num_scalar_prefetch=1,
            grid=(n // ROWS,),
            in_specs=[
                rows_of(d), rows_of(d), rows_of(both), rows_of(half), rows_of(r), rows_of(r),
                whole((r, d)), whole((r, both)), whole((r, half)), whole((r, d)),
            ]
            + [ANY] * len(parts),
            out_specs=[half_rows(d), half_rows(d), whole((r, d)), whole((r, both)), whole((r, half)), whole((r, d))],
            scratch_shapes=[
                pltpu.VMEM((d, both), BF), pltpu.VMEM((d, half), BF), pltpu.VMEM((ROWS, both), BF), pltpu.VMEM((ROWS, both), BF),
                pltpu.VMEM((ROWS, r), BF), pltpu.SemaphoreType.DMA((3, blocks)),
            ],
        ),
        out_shape=[sds((n // 2, d), BF)] * 2 + [sds((r, d), F32), sds((r, both), F32), sds((r, half), F32), sds((r, d), F32)],
        compiler_params=params(),
        cost_estimate=cost(3 * n * d * half, 2 * (3 * n * d + 3 * d * half + 3 * n * half)),
        name="ffn_back",
    )(me, dl, h, gu, q, rank, drank, shrink, expand, dshrink, dexpand, *parts)


def call_attn(qkv, cols, places):
    n = qkv.shape[0]
    return pl.pallas_call(
        attn_kernel,
        in_specs=[pl.BlockSpec(memory_space=pltpu.VMEM)] * 3,
        out_specs=pl.BlockSpec(memory_space=pltpu.VMEM),
        out_shape=sds((n, HD), BF),
        compiler_params=params(),
        cost_estimate=cost(2 * n * n * HD, 8 * n * HD),
        name="attend",
    )(qkv, cols, places)


def call_attn_back(qkv, cols, places, do, cos, sin):
    n = qkv.shape[0]
    return pl.pallas_call(
        attn_back_kernel,
        in_specs=[pl.BlockSpec(memory_space=pltpu.VMEM)] * 6,
        out_specs=pl.BlockSpec(memory_space=pltpu.VMEM),
        out_shape=sds((n, 3 * HD), BF),
        scratch_shapes=[pltpu.VMEM((n, HD), F32)] * 2,
        compiler_params=params(),
        cost_estimate=cost(7 * n * n * HD, 16 * n * HD),
        name="attend_back",
    )(qkv, cols, places, do, cos, sin)


def triangles(chunk):
    rows = jnp.arange(chunk, dtype=jnp.int32)
    lower = rows[:, None] >= rows[None, :]
    return jnp.stack([lower, lower.T]).astype(BF)


def call_mamba(me, zx, bc, step, cols, rows, taps, heads, skip, chunk):
    n = zx.shape[0]
    inner, states = zx.shape[1] // 2, bc.shape[1] // 2
    width = inner + 2 * states
    wide = AHEAD * chunk
    tail = wide // 16

    def here(i, me):
        return (i, 0)

    def before(i, me):
        return (jnp.maximum(i - 1, 0) * tail + tail - 1, 0)

    return pl.pallas_call(
        mamba_kernel,
        grid_spec=pltpu.PrefetchScalarGridSpec(
            num_scalar_prefetch=1,
            grid=(n // wide,),
            in_specs=[
                pl.BlockSpec((wide, 2 * inner), here),
                pl.BlockSpec((16, 2 * inner), before),
                pl.BlockSpec((wide, 2 * states), here),
                pl.BlockSpec((16, 2 * states), before),
                pl.BlockSpec((wide, 128), here),
                pl.BlockSpec((wide, 128), here),
                pl.BlockSpec((AHEAD, 1, chunk), lambda i, me: (i, 0, 0)),
                whole((8, width)),
                whole((8, 128)),
                whole((1, inner)),
                whole((2, chunk, chunk)),
            ],
            out_specs=[
                pl.BlockSpec((wide, inner), here),
                pl.BlockSpec((AHEAD, states, inner), lambda i, me: (i, 0, 0)),
                pl.BlockSpec((wide, width), here),
            ],
            scratch_shapes=[pltpu.VMEM((states, inner), F32), pltpu.VMEM((wide + 8, width), F32)],
        ),
        out_shape=[sds((n, inner), BF), sds((n // chunk, states, inner), BF), sds((n, width), BF)],
        compiler_params=params(),
        cost_estimate=cost(3 * n * inner * states, 4 * n * width),
        name="mamba",
    )(me, zx, zx, bc, bc, step, cols, rows, taps, heads, skip, triangles(chunk))


def call_mamba_back(me, zx, pre, step, cols, rows, taps, heads, skip, hs, dg, chunk):
    n = zx.shape[0]
    inner = zx.shape[1] // 2
    width = pre.shape[1]
    states = (width - inner) // 2
    wide = BACK * chunk
    count = n // wide
    collect = (jnp.arange(inner, dtype=jnp.int32)[:, None] // 64 == jnp.arange(128, dtype=jnp.int32)[None, :]).astype(BF)

    def here(i, me):
        return (count - 1 - i, 0)

    def deep(i, me):
        return (count - 1 - i, 0, 0)

    return pl.pallas_call(
        mamba_back_kernel,
        grid_spec=pltpu.PrefetchScalarGridSpec(
            num_scalar_prefetch=1,
            grid=(count,),
            in_specs=[
                pl.BlockSpec((wide, inner), here),
                pl.BlockSpec((wide, width), here),
                pl.BlockSpec((wide, 128), here),
                pl.BlockSpec((wide, 128), here),
                pl.BlockSpec((BACK, 1, chunk), deep),
                whole((8, width)),
                whole((8, 128)),
                whole((1, inner)),
                whole((2, chunk, chunk)),
                whole((inner, 128)),
                pl.BlockSpec((BACK, states, inner), deep),
                pl.BlockSpec((wide, inner), here),
            ],
            out_specs=[
                pl.BlockSpec((wide, 2 * inner), here),
                pl.BlockSpec((wide, 2 * states), here),
                pl.BlockSpec((wide, 128), here),
            ],
            scratch_shapes=[
                pltpu.VMEM((states, inner), F32),
                pltpu.VMEM((chunk + 8, width), F32),
                pltpu.VMEM((CONV - 1, 8, width), F32),
                pltpu.VMEM((8, 128), F32),
            ],
        ),
        out_shape=[sds((n, 2 * inner), BF), sds((n, 2 * states), BF), sds((n, 128), BF)],
        compiler_params=params(),
        cost_estimate=cost(10 * n * inner * states, 8 * n * width),
        name="mamba_back",
    )(me, zx, pre, step, cols, rows, taps, heads, skip, triangles(chunk), collect, hs, dg)


def place_kernel(pieces, parts, *outs):
    adapter = pl.program_id(0)
    seqs, _, width = parts[0].shape
    lane = lax.broadcasted_iota(jnp.int32, (1, 128), 1)
    hot = [
        jnp.sum(jnp.where(lane == adapter, parts[0][s, 0:1, width - 128 :].astype(F32), 0.0), axis=1, keepdims=True)
        for s in range(seqs)
    ]
    for out, rows in zip(outs, pieces):
        for k, sources in enumerate(rows):
            to = 0
            for which, start, size in sources:
                value = hot[0] * parts[which][0, :, start : start + size].astype(F32)
                for s in range(1, seqs):
                    value = value + hot[s] * parts[which][s, :, start : start + size].astype(F32)
                if len(rows) > 1:
                    out[0, 0, :, k, to : to + size] = value
                else:
                    out[0, 0, :, to : to + size] = value
                to += size


def call_place(l, layers, group, before, adapters, rank, width, inner, ff, states, kv_width):
    kv = 2 * width + states
    of = len(group) - 1
    first, second = inner + HD + 2 * inner + HD + 128, 3 * ff
    sums = kv + kv_width + (0 if of else 2 * width)
    owned = first + (0 if of else second)
    ffn = 0 if of else kv + kv_width

    def both(at, size):
        return ((0, sums + at, size), (0, sums + owned + at, size))

    def ffn_both(at, size):
        if of:
            return ((1, 2 * width + at, size), (1, 2 * width + second + at, size))
        return both(first + at, size)

    zx = inner + HD
    pieces = (
        (((0, width, width),),),
        (both(zx, inner), both(zx + inner, inner)),
        (both(zx + 2 * inner, HD),),
        (((0, 2 * width, states // 2),), ((0, 2 * width + states // 2, states // 2),)),
        (((0, kv, kv_width // 2),), ((0, kv + kv_width // 2, kv_width // 2),)),
        (both(0, inner),),
        (both(inner, HD),),
        (((0, 0, width),),),
        (((of, ffn, width),),),
        (ffn_both(0, ff), ffn_both(ff, ff)),
        (ffn_both(2 * ff, ff),),
        (((of, ffn + width, width),),),
        (((0, sums + zx + 2 * inner + HD, 128),),),
        (((0, sums + owned + zx + 2 * inner + HD, 128),),),
    )
    shapes = []
    for rows in pieces:
        size = sum(size for _, _, size in rows[0])
        shapes.append((rank, len(rows), size) if len(rows) > 1 else (rank, size))

    def block(shape):
        zeros = (0,) * len(shape)
        return pl.BlockSpec((1, 1) + shape, lambda a: (l, a) + zeros)

    def body(*refs):
        place_kernel(pieces, refs[: len(group)], *refs[len(group) + len(before) :])

    return pl.pallas_call(
        body,
        grid=(adapters,),
        in_specs=[pl.BlockSpec(array.shape, lambda a: (0, 0, 0)) for array in group] + [ANY] * len(before),
        out_specs=[block(shape) for shape in shapes],
        out_shape=[sds((layers, adapters) + shape, F32) for shape in shapes],
        input_output_aliases={len(group) + k: k for k in range(len(before))},
        compiler_params=params(),
        name="place",
    )(*group, *before)


def half_of(array, which, axis):
    size = array.shape[axis] // 2
    return lax.dynamic_slice_in_dim(array, which * size, size, axis)


def on_device(
    dp_axes,
    tokens,
    out_grad,
    doc_lengths,
    adapter_ids,
    mixer_gain,
    ffn_gain,
    ssm_in,
    step_proj,
    query_proj,
    state_proj,
    keyval_proj,
    conv_inner,
    conv_state,
    decay_log,
    step_bias,
    skip_gain,
    ssm_out,
    attn_out,
    gate_up,
    down_proj,
    mixer_shrink,
    inner_expand,
    step_expand,
    query_expand,
    state_expand,
    keyval_expand,
    ssmout_shrink,
    attnout_shrink,
    mixer_expand,
    ffn_shrink,
    gateup_expand,
    down_shrink,
    down_expand,
):
    layers = ssm_in.shape[0]
    zh, zl, ta, tb = (lax.axis_index(a) for a in ("zh", "zl", "ta", "tb"))
    me_w = zh * 2 + zl
    for k, axis in enumerate(dp_axes):
        me_w = me_w + lax.axis_index(axis) * (4 << k)
    me = jnp.stack([me_w, ta, zl, tb]).astype(jnp.int32)
    block, width = tokens.shape[1:]
    n = block * 4
    share = n // 8
    chunk = share
    heads = step_proj.shape[2] // 2
    inner = ssm_in.shape[3] // 2
    states = 2 * state_proj.shape[3]
    rank = mixer_shrink.shape[3]
    local = ssm_in.shape[1]
    ff = gate_up.shape[3] // 2

    def own_stages(array, *tokens):
        mine = half_of(array, tb, 1)
        keep = lax.dynamic_index_in_dim(mine, zh, 0, False)
        away = lax.dynamic_index_in_dim(mine, 1 - zh, 0, False)
        rows = away.shape[0] // 2
        got = swap(later(jnp.where(zh == ta, away[:rows], away[rows:]), *tokens), "zh")
        tokens = yield [got]
        beside = swap(later(got, *tokens), "ta")
        yield [beside]
        return jnp.where(zh == ta, keep, jnp.concatenate([got, beside], axis=0))

    def all_stages(own, dtype, *tokens):
        own = later(own, *tokens)
        got = lax.ppermute(own, ("zh", "ta"), [(2, 0), (1, 3)])
        near = swap(own, "ta")
        tokens = yield [got, near]
        same = jnp.where(zh == ta, own, near)
        got = later(got, *tokens)
        across = swap(got, "ta")
        tokens = yield [across]
        other = jnp.where(zh == ta, got, across)
        pair = later(jnp.where(zh == 0, jnp.stack([same, other]), jnp.stack([other, same])), *tokens)
        far = swap(pair, "tb")
        yield [far]
        full = jnp.where(tb == 0, jnp.concatenate([pair, far], axis=1), jnp.concatenate([far, pair], axis=1))
        return full.astype(dtype)

    def ordered(axis, own, got, along):
        here = lax.axis_index(axis) == 0
        return jnp.where(here, jnp.concatenate([own, got], axis=along), jnp.concatenate([got, own], axis=along))


    def takes(name, l, tie):
        def cut(array, starts, sizes):
            return lax.dynamic_slice(array, (l,) + starts, (1,) + sizes).reshape(tuple(k for k in sizes if k > 1))

        def pick(which):
            if name in ("a", "b"):
                k = 0 if name == "a" else 1
                left = cut(arrays[0], (0, k, which * inner), (local, 1, inner))
                if name == "a":
                    return [left, cut(arrays[1], (0, which * HD), (local, HD))]
                return [left, cut(arrays[1], (0, tb, ta * HD), (local, 1, HD))]
            if name == "c":
                step = cut(arrays[1], (0, which * heads), (local, heads))
                return [cut(arrays[0], (0, tb, 0), (local, 1, states // 2)), jnp.pad(step, ((0, 0), (0, 128 - heads)))]
            if name == "out":
                return [cut(arrays[0], (which * inner, 0), (inner, local)).T, cut(arrays[1], (which * HD, 0), (HD, local)).T]
            if name == "down":
                return [cut(arrays[0], (which * ff, 0), (ff, local)).T]
            return [cut(arrays[0], (0, 0 if name == "gate" else 1, which * ff), (local, 1, ff))]

        sources = {
            "a": (ssm_in, query_proj), "b": (ssm_in, keyval_proj), "c": (state_proj, step_proj), "out": (ssm_out, attn_out),
            "gate": (gate_up,), "up": (gate_up,), "down": (down_proj,),
        }
        arrays = tie(*sources[name])
        return pick

    own, sent, near, pair, far_z, got = ({} for _ in range(6))
    last = {}

    def gathered(keys, *tokens):
        def tie(*values):
            return tied(*values, *tokens)[: len(values)] if tokens else values

        picks = [takes(*key, tie) for key in keys]
        mine, away = (jnp.concatenate([c for pick in picks for c in pick(which)], axis=1) for which in (zl, 1 - zl))
        return keys, mine, away

    def exchange(group, *tokens):
        keys, mine, away = group
        moved = swap(later(away, *tokens), "zl")
        at = 0
        for key in keys:
            size = widths[key[0]]
            own[key], near[key] = mine[:, at : at + size], moved[:, at : at + size]
            at += size
        return moved

    def prepare(keys, *tokens):
        return exchange(gathered(keys, *tokens))

    def order(way):
        return (last[way],) if way in last else ()

    def send_zh(key, *tokens, parts=1):
        pair[key] = later(jnp.concatenate([own[key], near[key]], axis=0), *order("zh"), *tokens)
        if parts == 1:
            far_z[key] = last["zh"] = swap(pair[key], "zh")
            return
        moved = []
        for part in jnp.split(pair[key], parts, axis=0):
            moved.append(swap(later(part, *moved[-1:]), "zh"))
        far_z[key] = jnp.concatenate(moved, axis=0)
        last["zh"] = moved[-1]

    def send_dp(key, *tokens):
        held, moved = pair[key], far_z[key]
        for axis in dp_axes:
            held = later(jnp.concatenate([held, moved], axis=0), *order("dp"), *tokens)
            moved = last["dp"] = swap(held, axis)
        got[key] = (held, moved)

    blocks = 4 << len(dp_axes)
    chain = [(name, 0) for name in ("a", "b", "c", "out", "gate", "up", "down")]
    for l in range(1, layers):
        chain += [(name, l) for name in ("a", "c", "b", "out", "gate", "up", "down")]
    widths = {
        "a": inner + HD, "b": inner + HD, "c": states // 2 + 128, "out": inner + HD, "gate": ff, "up": ff, "down": ff
    }
    first = prepare(chain[:1])
    second = prepare(chain[1:3], first)
    for key in chain[:3]:
        send_zh(key)
    for key in chain[:3]:
        send_dp(key)
    third = prepare(chain[3:5], far_z[chain[0]])
    send_zh(chain[3])
    near_first = prepare(chain[5:7], far_z[chain[1]], third)
    moved = [5]
    arrived = [far_z[chain[3]], near_first]
    ahead = {1: (0, 3), 4: (3, 7)}
    groups = {}

    def ready_for(l, w, *tokens):
        if l + 1 < layers:
            start, end = ahead[w]
            groups[l, w] = gathered(chain[7 * l + 7 + start : 7 * l + 7 + end], *tokens)
            arrived.extend(groups[l, w][1:])

    def window(value, *tokens, parts=1, early=False):
        out = later(value, *arrived, *tokens)
        before = tuple(a for group in groups.values() for a in group[1:] if any(a is b for b in arrived)) if early else tokens
        arrived.clear()
        k = moved[0]
        moved[0] += 1
        if k - 1 < len(chain):
            send_zh(chain[k - 1], *tokens, parts=parts)
            arrived.append(last["zh"])
        if k - 2 < len(chain):
            send_dp(chain[k - 2], *before)
            arrived.append(got[chain[k - 2]][1])
        for w in ahead:
            l, rest = divmod(k - 5 - w, 7)
            if not rest and (l, w) in groups:
                arrived.append(exchange(groups[l, w], *tokens))
        return out

    def step_window(value, tokens, *stages):
        out = later(value, *arrived, *tokens)
        arrived.clear()
        for stage in stages:
            arrived.extend(stage.start(*tokens) or ())
        return out


    def mixer_weights(l):
        def both(key, start, size):
            return swap(jnp.concatenate([part[:, start : start + size] for part in got[key]], axis=0), "tb")

        parts = got["a", l] + got["b", l] + got["c", l]
        return both(("b", l), inner, HD), both(("c", l), 0, states // 2), parts, blocks

    lengths = lax.dynamic_index_in_dim(doc_lengths, zh, 0, False)
    aid = lax.dynamic_index_in_dim(adapter_ids, zh, 0, False)
    lengths, positions = tied(lengths, jnp.arange(n, dtype=jnp.int32), far_z["a", 0])[:2]
    seg = segment_of(positions, lengths)
    seg_back = [segment_of(positions - k, lengths) for k in range(1, CONV)]
    starts = (positions // chunk) * chunk
    seg_start = segment_of(starts - 1, lengths)
    seg_end = segment_of(starts + chunk - 1, lengths)
    cols = jnp.stack(
        [(seg == seg_end).astype(F32)]
        + [(seg == s).astype(F32) for s in seg_back]
        + [(seg == seg_start).astype(F32), seg.astype(F32), positions.astype(F32)],
        axis=1,
    )
    cols = jnp.pad(cols, ((0, 0), (0, 128 - cols.shape[1])))
    rows = seg.astype(F32).reshape(n // chunk, 1, chunk)
    places = jnp.pad(jnp.stack([seg.astype(F32), positions.astype(F32)]), ((0, 6), (0, 0)))
    freqs = ROPE_BASE ** (-jnp.arange(HD // 2, dtype=F32) / (HD // 2))
    angles = positions.astype(F32)[:, None] * freqs[None, :]
    cos = jnp.tile(jnp.cos(angles), (1, 2))
    sin = jnp.sin(angles)
    sin = jnp.concatenate([-sin, sin], axis=1)

    def small_of(l, token):
        aid_now = tied(aid, token)[0]

        def pick(table):
            zeros = (0,) * (table.ndim - 2)
            return lax.dynamic_slice(table, (l, aid_now) + zeros, (1, 1) + table.shape[2:]).reshape(table.shape[2:])

        def flat(table):
            return pick(table).T

        inner_e, keyval_e = pick(inner_expand), pick(keyval_expand)
        expand_in = jnp.concatenate(
            [
                half_of(inner_e[:, 0], zl, 1),
                half_of(inner_e[:, 1], zl, 1),
                half_of(pick(query_expand), zl, 1),
                lax.dynamic_slice_in_dim(keyval_e[:, 0], ta * HD, HD, 1),
                lax.dynamic_slice_in_dim(keyval_e[:, 1], ta * HD, HD, 1),
                jnp.pad(half_of(pick(step_expand), zl, 1), ((0, 0), (0, 128 - heads))),
                pick(state_expand).reshape(rank, -1),
            ],
            axis=1,
        )
        shrink_out = jnp.concatenate([half_of(flat(ssmout_shrink), zl, 1), half_of(flat(attnout_shrink), zl, 1)], axis=1)
        gate_e = pick(gateup_expand)
        expand_gu = jnp.concatenate([half_of(gate_e[:, 0], zl, 1), half_of(gate_e[:, 1], zl, 1)], axis=1)
        shrink_down = half_of(flat(down_shrink), zl, 1)
        taps = jnp.pad(
            jnp.concatenate([half_of(conv_inner[l], zl, 1), conv_state[l].reshape(CONV, -1)], axis=1), ((0, 8 - CONV), (0, 0))
        )
        head_rows = jnp.pad(
            jnp.stack([half_of(step_bias[l], zl, 0), jnp.exp(half_of(decay_log[l], zl, 0))]), ((0, 6), (0, 128 - heads))
        )
        skip = jnp.repeat(half_of(skip_gain[l], zl, 0), inner // heads)[None, :]
        return (
            flat(mixer_shrink), expand_in, shrink_out, pick(mixer_expand), flat(ffn_shrink), expand_gu, shrink_down,
            pick(down_expand), taps, head_rows, skip,
        )

    weights, small, saved = [], [], []
    resid = Stages(own_stages(tied(tokens, near["a", 0])[0])).finish().astype(F32)
    grad_stages = None
    token = far_z["a", 0]
    for l in range(layers):
        small.append(small_of(l, token))
        shrink_in, expand_in, shrink_out, expand_out, shrink_gu, expand_gu, shrink_down, expand_down, taps, head_rows, skip = small[l]
        if l:
            gain = window(mixer_gain[l], resid)
            if grad_stages is not None and l + 1 == layers:
                arrived.extend(grad_stages.start(resid))
        else:
            gain = later(mixer_gain[l], far_z["c", l], got["b", l][1], third, cols, cos, sin, places, rows, *small[l])
        h = gather_tokens(rms_norm(resid, gain).astype(BF))
        w_in = mixer_weights(l)
        if not l:
            ready_for(l, 1, far_z["c", l])
        zx, bc, qkv, step, rank_in = call_in(window(me, h, early=bool(l)), h, shrink_in, expand_in, cos, sin, *w_in, inner, states)
        if l + 1 == layers:
            grad = (grad_stages or Stages(own_stages(out_grad))).finish().astype(F32)
            top_grad = gather_tokens(grad.astype(BF))
        g, hs, pre = call_mamba(window(me, rank_in), zx, bc, step, cols, rows, taps, head_rows, skip, chunk)
        o = call_attn(qkv, cols, places)
        w_out = (got["out", l], blocks)
        keep, send, rank_out = call_out(me, g, o, shrink_out, expand_out, *w_out)
        mid = resid + scatter_tokens(keep, window(send, rank_out, parts=2))
        if l + 1 == layers:
            arrived.append(top_grad)
        token = mid
        h2 = gather_tokens(rms_norm(mid, window(ffn_gain[l], mid)).astype(BF))
        ready_for(l, 4, mid)
        w_ffn = (got["gate", l] + got["up", l] + got["down", l], blocks)
        keep, send, gu, q, rank_gu, rank_down = call_ffn(window(me, h2, early=True), h2, shrink_gu, expand_gu, shrink_down, expand_down, *w_ffn)
        if l + 1 < layers:
            send = window(send, rank_down, parts=2)
            if l + 2 == layers:
                grad_stages = Stages(own_stages(out_grad, last["zh"]))
                arrived.extend(grad_stages.start())
            resid_next = mid + scatter_tokens(keep, send)
        else:
            final = Stages(scatter_stages(keep, send))
        weights.append((w_in, w_out, w_ffn))
        saved.append((resid, mid, h, zx, pre, qkv, step, rank_in, g, hs, o, rank_out, h2, gu, q, rank_gu, rank_down))
        resid = resid_next

    seq_axes = tuple(reversed(dp_axes)) + ("zh",)
    adapters = mixer_shrink.shape[1]
    hot = jnp.pad((aid == jnp.arange(adapters, dtype=jnp.int32)).astype(BF), (0, 128 - adapters))
    hot = jnp.broadcast_to(hot[None], (rank, 128))

    def sum_stages(partial, owned, *tokens):
        mine = jnp.concatenate(partial, axis=1).astype(BF)
        size = mine.shape[1]
        for axis in ("tb", "ta"):
            mine = later(mine, *tokens)
            moved = swap(mine, axis)
            tokens = yield [moved]
            mine = (mine.astype(F32) + moved.astype(F32)).astype(BF)
        mine = later(jnp.concatenate([mine] + [value.astype(BF) for value in owned], axis=1), *tokens)
        moved = swap(mine, "zl")
        tokens = yield [moved]
        total = (mine[:, :size].astype(F32) + moved[:, :size].astype(F32)).astype(BF)
        held = jnp.concatenate([total, ordered("zl", mine[:, size:], moved[:, size:], 1), hot], axis=1)[None]
        for axis in ("zh",) + dp_axes:
            held = later(held, *tokens)
            moved = swap(held, axis)
            tokens = yield [moved]
            held = jnp.concatenate([held, moved], axis=0)
        return (held,)

    def place(l, group, tables):
        return call_place(l, layers, group, tables, adapters, rank, width, inner, ff, states, 2 * keyval_proj.shape[3])

    sums = [None] * layers
    at = 2 * inner
    out_stages, older = None, None
    for l in reversed(range(layers)):
        shrink_in, expand_in, shrink_out, expand_out, shrink_gu, expand_gu, shrink_down, expand_down, taps, head_rows, skip = small[l]
        w_in, w_out, w_ffn = weights[l]
        resid, mid, h, zx, pre, qkv, step, rank_in, g, hs, o, rank_out, h2, gu, q, rank_gu, rank_down = saved[l]
        top = l == layers - 1
        dl = top_grad if top else gather_tokens(grad.astype(BF))
        if top:
            now = step_window(me, (dl, rank_down), final)
        else:
            now = step_window(me, (dl,), out_stages, older)
        keep, send, g_shrink_gu, g_expand_gu, g_shrink_down, g_expand_down = call_ffn_back(
            now, dl, h2, gu, q, rank_gu, rank_down, shrink_gu, expand_gu, shrink_down, expand_down, *w_ffn
        )
        of_ffn = [g_shrink_gu, g_expand_down], [g_expand_gu, g_shrink_down]
        if not l:
            rest = Stages(sum_stages(*of_ffn))
        send = step_window(send, (g_expand_gu,), *(() if top else (older,)), *(() if l else (rest,)))
        d_mid = scatter_tokens(keep, send)
        grad = grad + norm_back(mid, step_window(ffn_gain[l], (d_mid,), *(() if l else (rest, rest))), d_mid)
        ml = gather_tokens(grad.astype(BF))
        now = step_window(me, (ml,), *((final,) if top else (out_stages,)), *(() if l else (rest,)))
        dg, do, g_expand_out, g_shrink_out = call_out_back(now, ml, g, o, rank_out, shrink_out, expand_out, *w_out)
        dqkv = call_attn_back(qkv, cols, places, do, cos, sin)
        now = step_window(me, (dqkv,), *((final,) if top else ()), *(() if l else (rest,)))
        dzx, dbc, dstep = call_mamba_back(now, zx, pre, step, cols, rows, taps, head_rows, skip, hs, dg, chunk)
        if top:
            output = mid + final.finish()
            out_stages = Stages(all_stages(output.astype(BF), BF, dstep))
            now = step_window(me, (dstep,), out_stages)
        else:
            now = step_window(me, (dstep,))
        keep, send, g_expand_in, g_shrink_in = call_in_back(
            now, dzx, dbc, dqkv, dstep, h, rank_in, shrink_in, expand_in, *w_in
        )
        send = step_window(send, (g_expand_in,))
        kv = jnp.zeros((rank, 2, keyval_proj.shape[3]), F32)
        own_kv = jnp.stack([g_expand_in[:, at + HD : at + 2 * HD], g_expand_in[:, at + 2 * HD : at + 3 * HD]], axis=1)
        kv = lax.dynamic_update_slice_in_dim(kv, own_kv, ta * HD, 2).reshape(rank, -1)
        partial = [g_expand_out, g_shrink_in, g_expand_in[:, at + 3 * HD + 128 :], kv]
        owned = [g_shrink_out, g_expand_in[:, : at + HD], g_expand_in[:, at + 3 * HD : at + 3 * HD + 128]]
        last_sum = Stages(scatter_stages(keep, send))
        for _ in range(3):
            summed = last_sum.start()
        d_resid = last_sum.finish()
        grad = grad + norm_back(resid, mixer_gain[l], d_resid)
        if l:
            older = sums[l] = Stages(sum_stages(partial + of_ffn[0], owned + of_ffn[1], d_resid))
            for _ in range(3):
                arrived[:] = older.start()
        else:
            sums[l] = Stages(sum_stages(partial, owned))
            for _ in range(4):
                moving = sums[l].start()
    output = out_stages.finish()
    last_grad = Stages(all_stages(grad.astype(BF), F32, *moving))
    last_grad.start()
    tables = ()
    for k in reversed(range(1, layers)):
        tables = place(k, tied(*sums[k].finish(), *summed)[:-2], tables)
    last_grad.start(*tables[-1:])

    tables = place(0, sums[0].finish() + rest.finish(), tables)
    last_grad.start(*tables[-1:])
    input_grad = last_grad.finish()

    def turned(value):
        return jnp.swapaxes(value, 2, 3)

    (
        mixshrink, innerexpand, queryexpand, stateexpand, keyvalexpand, ssmshrink, attnshrink, mixexpand, ffnshrink, gateexpand,
        downshrink, downexpand, step_low, step_high,
    ) = tables
    return (
        output,
        input_grad,
        turned(mixshrink),
        innerexpand,
        jnp.concatenate([step_low[..., :heads], step_high[..., :heads]], axis=-1),
        queryexpand,
        stateexpand,
        keyvalexpand,
        turned(ssmshrink),
        turned(attnshrink),
        mixexpand,
        turned(ffnshrink),
        gateexpand,
        turned(downshrink),
        downexpand,
    )


def solution(mesh):
    dp, ctx, tensor = (mesh.shape[a] for a in ("dp", "ctx", "tensor"))
    bits = dp.bit_length() - 1
    dp_names = tuple("d%d" % k for k in reversed(range(bits)))
    inside = Mesh(
        mesh.devices.reshape((2,) * bits + (2, ctx // 2, 2, tensor // 2)), dp_names + ("zh", "zl", "ta", "tb")
    )
    dp_axes = tuple(reversed(dp_names))
    d, c, t = dp_names, ("zh", "zl"), ("ta", "tb")
    dc = dp_names + c
    return jax.shard_map(
        functools.partial(on_device, dp_axes),
        mesh=inside,
        in_specs=(
            P(d, c, None),
            P(d, c, None),
            P(d, None),
            P(d),
            P(),
            P(),
            P(None, dc, None, t),
            P(None, dc, t),
            P(None, dc, t),
            P(None, dc, None, None),
            P(None, dc, None, None),
            P(None, None, t),
            P(),
            P(None, t),
            P(None, t),
            P(None, t),
            P(None, t, dc),
            P(None, t, dc),
            P(None, dc, None, t),
            P(None, t, dc),
            P(),
            P(None, None, None, None, t),
            P(None, None, None, t),
            P(None, None, None, t),
            P(),
            P(),
            P(None, None, t, None),
            P(None, None, t, None),
            P(),
            P(),
            P(None, None, None, None, t),
            P(None, None, t, None),
            P(),
        ),
        out_specs=(
            P(d, c, None),
            P(d, c, None),
            P(),
            P(None, None, None, None, t),
            P(None, None, None, t),
            P(None, None, None, t),
            P(),
            P(),
            P(None, None, t, None),
            P(None, None, t, None),
            P(),
            P(),
            P(None, None, None, None, t),
            P(None, None, t, None),
            P(),
        ),
        check_vma=False,
    )
```

```python
import functools

import jax
import jax.numpy as jnp
from jax import lax
from jax.experimental import pallas as pl
from jax.experimental.pallas import tpu as pltpu
from jax.sharding import Mesh
from jax.sharding import PartitionSpec as P

HD = 128
CONV = 4
EPS = 1e-05
ROPE_BASE = 10000.0
HIGHEST = lax.Precision.HIGHEST
BF = jnp.bfloat16
F32 = jnp.float32
TOK = ("ta", "zl", "tb")
ROWS = 512
TILE = 256
AHEAD = 4
BACK = 2
COST = 1000
VMEM = 56 * 1024 * 1024


def dot(a, b, **kw):
    return jnp.dot(a, b, preferred_element_type=F32, **kw)


def dot_nt(a, b):
    return lax.dot_general(a, b, (((1,), (1,)), ((), ())), preferred_element_type=F32)


def dot_tn(a, b):
    return lax.dot_general(a, b, (((0,), (0,)), ((), ())), preferred_element_type=F32)


def sigmoid(v):
    return 0.5 * jnp.tanh(0.5 * v) + 0.5


def swap(value, axis):
    return lax.ppermute(value, axis, [(0, 1), (1, 0)])


def rms_norm(stream, gain):
    return stream * lax.rsqrt(jnp.mean(stream * stream, axis=-1, keepdims=True) + EPS) * gain


def norm_back(stream, gain, upstream):
    scale = lax.rsqrt(jnp.mean(stream * stream, axis=-1, keepdims=True) + EPS)
    weighted = upstream * gain
    inner = jnp.mean(stream * weighted, axis=-1, keepdims=True)
    return scale * weighted - stream * (scale * scale * scale * inner)


def segment_of(positions, lengths):
    ends = jnp.cumsum(lengths)
    inside = jnp.sum((positions[:, None] >= ends[None, :]).astype(jnp.int32), axis=1)
    return jnp.where(positions < 0, -1, inside)


def gather_tokens(own):
    return lax.all_gather(own, TOK, axis=0, tiled=True)


def scatter_stages(keep, send, *tokens):
    b, half = keep.shape[0] // 4, keep.shape[1] // 2
    recv = swap(later(send, *tokens), "tb")
    tokens = yield [recv]

    def pair(rows, cols):
        return keep[rows, cols].astype(F32) + recv[rows, cols].astype(F32)

    first, second = slice(0, half), slice(half, 2 * half)

    def odd(cols, k):
        return jnp.concatenate([pair(slice(k * b, k * b + b), cols), pair(slice((k + 2) * b, (k + 3) * b), cols)], axis=0)

    got_a = swap(later(pair(slice(2 * b, 4 * b), first).astype(BF), *tokens), "ta")
    got_b = swap(later(odd(second, 1).astype(BF), *tokens), "zl")
    tokens = yield [got_a, got_b]
    sum_a = pair(slice(0, 2 * b), first) + got_a.astype(F32)
    sum_b = odd(second, 0) + got_b.astype(F32)
    last_a = swap(later(sum_a[b:].astype(BF), *tokens), "zl")
    last_b = swap(later(sum_b[b:].astype(BF), *tokens), "ta")
    yield [last_a, last_b]
    return jnp.concatenate([sum_a[:b] + last_a.astype(F32), sum_b[:b] + last_b.astype(F32)], axis=1)


def scatter_tokens(keep, send):
    return Stages(scatter_stages(keep, send)).finish()


class Stages:
    def __init__(self, chain):
        self.chain, self.begun, self.result = chain, False, None

    def start(self, *tokens):
        try:
            if self.begun:
                return self.chain.send(tokens)
            self.begun = True
            return next(self.chain)
        except StopIteration as end:
            self.result = end.value
            return None

    def finish(self):
        while self.start() is not None:
            pass
        return self.result


def later(value, *tokens):
    return tied(value, *tokens)[0] if tokens else value


def tied(*values):
    return lax.optimization_barrier(values)


def blocks_of(me_ref, parts, rows):
    out, j = [], 0
    for part in parts:
        for k in range(part.shape[0] // rows):
            at = pl.multiple_of((j ^ me_ref[0]) * rows, rows)
            out.append((part.at[pl.ds(k * rows, rows), :], pl.ds(at, rows)))
            j += 1
    return out


def weight_copies(me_ref, parts, held, sem):
    rows = held.shape[0] // sem.shape[0]
    return [
        pltpu.make_async_copy(block, held.at[at, :], sem.at[j]) for j, (block, at) in enumerate(blocks_of(me_ref, parts, rows))
    ]


def at_first(do, copies):
    @pl.when(pl.program_id(0) == 0)
    def _():
        for copy in copies():
            getattr(copy, do)()


def mixer_copies(me_ref, parts, far_kv, far_bc, held, sem):
    rows = held.shape[0] // sem.shape[1]
    states = far_bc.shape[1]
    inner = (held.shape[1] - 3 * HD - 2 * states - 128) // 2
    core = me_ref[3]

    def key(which):
        return pl.ds(pl.multiple_of(2 * inner + HD + which * HD, HD), HD)

    def state(which):
        return pl.ds(pl.multiple_of(2 * inner + 3 * HD + 128 + which * states, HD), states)

    first, second, third = (blocks_of(me_ref, part, rows) for part in parts)
    copies = []
    for j, ((one, at), (two, _), (three, _)) in enumerate(zip(first, second, third)):
        here = pl.ds(j * rows, rows)
        for k, (source, cols) in enumerate(
            (
                (one.at[:, pl.ds(0, inner)], pl.ds(0, inner)),
                (one.at[:, pl.ds(inner, HD)], pl.ds(2 * inner, HD)),
                (two.at[:, pl.ds(0, inner)], pl.ds(inner, inner)),
                (two.at[:, pl.ds(inner, HD)], key(core)),
                (three.at[:, pl.ds(0, states)], state(core)),
                (three.at[:, pl.ds(states, 128)], pl.ds(2 * inner + 3 * HD, 128)),
                (far_kv.at[here, :], key(1 - core)),
                (far_bc.at[here, :], state(1 - core)),
            )
        ):
            copies.append(pltpu.make_async_copy(source, held.at[at, cols], sem.at[k, j]))
    return copies


def turned_rows(me_ref, size):
    b = size // 4
    out = []
    for core in (me_ref[3], 1 - me_ref[3]):
        for z in range(2):
            out.append(pl.ds(pl.multiple_of(((z ^ me_ref[2]) * 2 + core) * b, b), b))
    return out


def emit(keep_ref, send_ref, cols, value):
    half = value.shape[0] // 2
    low = value.astype(BF)
    keep_ref[:, cols] = low[:half]
    send_ref[:, cols] = low[half:]


def in_kernel(me_ref, h_ref, shrink_ref, expand_ref, cos_ref, sin_ref, far_kv, far_bc, *rest):
    parts, rest = (rest[0:2], rest[2:4], rest[4:6]), rest[6:]
    zx_ref, bc_ref, qkv_ref, step_ref, rank_ref, held, sem = rest
    inner = zx_ref.shape[1]
    states = bc_ref.shape[1]

    def copies(wide):
        return lambda: [
            copy
            for k, copy in enumerate(mixer_copies(me_ref, parts, far_kv, far_bc, held, sem))
            if (k % sem.shape[0] in (0, 2)) == wide
        ]

    at_first("start", copies(True))
    h = h_ref[...]
    rank = dot_nt(h, shrink_ref[...]).astype(BF)
    rank_ref[...] = rank
    at_first("wait", copies(True))
    at_first("start", copies(False))

    def part(at, width):
        cols = slice(at, at + width)
        return dot(h, held[:, cols]) + dot(rank, expand_ref[:, cols])

    for at in range(0, inner, 256):
        zx_ref[:, at : at + 256] = part(at, 256).astype(BF)
    at_first("wait", copies(False))
    qk = part(inner, 2 * HD)
    cos, sin = cos_ref[...], sin_ref[...]
    for k in range(2):
        head = qk[:, k * HD : (k + 1) * HD]
        turned = head * cos + pltpu.roll(head, HD // 2, 1) * sin
        qkv_ref[:, k * HD : (k + 1) * HD] = turned.astype(BF)
    last = part(inner + 2 * HD, HD + 128)
    qkv_ref[:, 2 * HD :] = last[:, :HD].astype(BF)
    step_ref[...] = last[:, HD:]
    for at in range(0, states, 256):
        bc_ref[:, at : at + 256] = part(inner + 3 * HD + 128 + at, 256).astype(BF)


def in_back_kernel(
    me_ref, dzx_ref, dbc_ref, dqkv_ref, dstep_ref, h_ref, rank_ref, shrink_ref, expand_ref, far_kv, far_bc, *rest
):
    parts, rest = (rest[0:2], rest[2:4], rest[4:6]), rest[6:]
    keep_ref, send_ref, gexpand_ref, gshrink_ref, held, du, low, sem = rest
    inner = dzx_ref.shape[1]

    def copies():
        return mixer_copies(me_ref, parts, far_kv, far_bc, held, sem)

    at_first("start", copies)

    @pl.when(pl.program_id(0) == 0)
    def _():
        gexpand_ref[...] = jnp.zeros_like(gexpand_ref)
        gshrink_ref[...] = jnp.zeros_like(gshrink_ref)

    size = du.shape[0]
    b = size // 4
    rank = rank_ref[...]
    where = turned_rows(me_ref, size)
    at = 0
    for source in (dzx_ref, dqkv_ref, dstep_ref, dbc_ref):
        wide = source.shape[1]
        gexpand_ref[:, at : at + wide] += dot_tn(rank, source[...])
        for k in range(4):
            du[k * b : (k + 1) * b, at : at + wide] = source[where[k], :]
        at += wide
    drank = dot_nt(du[...], expand_ref[...]).astype(BF)
    for k in range(4):
        low[where[k], :] = drank[k * b : (k + 1) * b]
    natural = low[...]
    for at in range(0, h_ref.shape[1], 256):
        cols = slice(at, at + 256)
        gshrink_ref[:, cols] += dot_tn(natural, h_ref[:, cols])
    at_first("wait", copies)
    for at in range(0, h_ref.shape[1], 256):
        cols = slice(at, at + 256)
        emit(keep_ref, send_ref, cols, dot_nt(du[...], held[cols, :]) + dot(drank, shrink_ref[:, cols]))


def out_kernel(me_ref, g_ref, o_ref, shrink_ref, expand_ref, *rest):
    pieces, rest = rest[:2], rest[2:]
    keep_ref, send_ref, rank_ref, held, go, sem = rest

    def copies():
        return weight_copies(me_ref, pieces, held, sem)

    at_first("start", copies)
    inner = g_ref.shape[1]
    size = go.shape[0]
    b = size // 4
    where = turned_rows(me_ref, size)
    for k in range(4):
        go[k * b : (k + 1) * b, :inner] = g_ref[where[k], :]
        go[k * b : (k + 1) * b, inner:] = o_ref[where[k], :]
    rank = dot_nt(go[...], shrink_ref[...]).astype(BF)
    for k in range(4):
        rank_ref[where[k], :] = rank[k * b : (k + 1) * b]
    at_first("wait", copies)
    for at in range(0, expand_ref.shape[1], 256):
        cols = slice(at, at + 256)
        emit(keep_ref, send_ref, cols, dot_nt(go[...], held[cols, :]) + dot(rank, expand_ref[:, cols]))


def out_back_kernel(me_ref, ml_ref, g_ref, o_ref, rank_ref, shrink_ref, expand_ref, *rest):
    pieces, rest = rest[:2], rest[2:]
    dg_ref, do_ref, gexpand_ref, gshrink_ref, held, sem = rest

    def copies():
        return weight_copies(me_ref, pieces, held, sem)

    at_first("start", copies)

    @pl.when(pl.program_id(0) == 0)
    def _():
        gexpand_ref[...] = jnp.zeros_like(gexpand_ref)
        gshrink_ref[...] = jnp.zeros_like(gshrink_ref)

    inner = g_ref.shape[1]
    ml = ml_ref[...]
    drank = dot_nt(ml, expand_ref[...]).astype(BF)
    rank = rank_ref[...]
    for at in range(0, ml.shape[1], 256):
        cols = slice(at, at + 256)
        gexpand_ref[:, cols] += dot_tn(rank, ml_ref[:, cols])
    gshrink_ref[:, :inner] += dot_tn(drank, g_ref[...])
    gshrink_ref[:, inner:] += dot_tn(drank, o_ref[...])
    at_first("wait", copies)
    for at in range(0, held.shape[1], 256):
        cols = slice(at, at + 256)
        got = (dot(ml, held[:, cols]) + dot(drank, shrink_ref[:, cols])).astype(BF)
        for to in (at, at + 128):
            if to < inner:
                dg_ref[:, to : to + 128] = got[:, to - at : to - at + 128]
            else:
                do_ref[:, to - inner : to - inner + 128] = got[:, to - at : to - at + 128]


def ffn_kernel(me_ref, h_ref, shrink_ref, expand_ref, dshrink_ref, dexpand_ref, *rest):
    (gates, ups, downs), rest = (rest[0:2], rest[2:4], rest[4:6]), rest[6:]
    keep_ref, send_ref, gu_ref, q_ref, rank_ref, drank_ref, held, dheld, qt, sem = rest
    half = dheld.shape[1]

    def both():
        return weight_copies(me_ref, gates, held.at[:, pl.ds(0, half)], sem.at[0]) + weight_copies(
            me_ref, ups, held.at[:, pl.ds(half, half)], sem.at[1]
        )

    def down():
        return weight_copies(me_ref, downs, dheld, sem.at[2])

    at_first("start", lambda: both() + down())
    h = h_ref[...]
    rank = dot_nt(h, shrink_ref[...]).astype(BF)
    rank_ref[...] = rank
    at_first("wait", both)
    for at in range(0, half, 256):
        one = slice(at, at + 256)
        two = slice(half + at, half + at + 256)
        gate = dot(h, held[:, one]) + dot(rank, expand_ref[:, one])
        up = dot(h, held[:, two]) + dot(rank, expand_ref[:, two])
        gu_ref[:, one] = gate.astype(BF)
        gu_ref[:, two] = up.astype(BF)
        q_ref[:, one] = (gate * sigmoid(gate) * up).astype(BF)
    size = qt.shape[0]
    b = size // 4
    where = turned_rows(me_ref, size)
    for k in range(4):
        qt[k * b : (k + 1) * b, :] = q_ref[where[k], :]
    drank = dot_nt(qt[...], dshrink_ref[...]).astype(BF)
    for k in range(4):
        drank_ref[where[k], :] = drank[k * b : (k + 1) * b]
    at_first("wait", down)
    for at in range(0, dexpand_ref.shape[1], 256):
        cols = slice(at, at + 256)
        emit(keep_ref, send_ref, cols, dot_nt(qt[...], dheld[cols, :]) + dot(drank, dexpand_ref[:, cols]))


def ffn_back_kernel(
    me_ref, dl_ref, h_ref, gu_ref, q_ref, rank_ref, drank_ref, shrink_ref, expand_ref, dshrink_ref, dexpand_ref, *rest
):
    (gates, ups, downs), rest = (rest[0:2], rest[2:4], rest[4:6]), rest[6:]
    keep_ref, send_ref, gshrink_ref, gexpand_ref, gdshrink_ref, gdexpand_ref, held, dheld, dgu, turned, low, sem = rest
    half = dheld.shape[1]

    def both():
        return weight_copies(me_ref, gates, held.at[:, pl.ds(0, half)], sem.at[0]) + weight_copies(
            me_ref, ups, held.at[:, pl.ds(half, half)], sem.at[1]
        )

    def down():
        return weight_copies(me_ref, downs, dheld, sem.at[2])

    at_first("start", lambda: down() + both())

    @pl.when(pl.program_id(0) == 0)
    def _():
        for ref in (gshrink_ref, gexpand_ref, gdshrink_ref, gdexpand_ref):
            ref[...] = jnp.zeros_like(ref)

    dl = dl_ref[...]
    ddrank = dot_nt(dl, dexpand_ref[...]).astype(BF)
    down_rank = drank_ref[...]
    for at in range(0, dl.shape[1], 256):
        cols = slice(at, at + 256)
        gdexpand_ref[:, cols] += dot_tn(down_rank, dl_ref[:, cols])
    gdshrink_ref[...] += dot_tn(ddrank, q_ref[...])
    rank = rank_ref[...]
    at_first("wait", down)
    for at in range(0, half, 256):
        one = slice(at, at + 256)
        two = slice(half + at, half + at + 256)
        dq = dot(dl, dheld[:, one]) + dot(ddrank, dshrink_ref[:, one])
        gate = gu_ref[:, one].astype(F32)
        up = gu_ref[:, two].astype(F32)
        sig = sigmoid(gate)
        dgu[:, one] = (dq * up * sig * (1.0 + gate * (1.0 - sig))).astype(BF)
        dgu[:, two] = (dq * gate * sig).astype(BF)
    gexpand_ref[...] += dot_tn(rank, dgu[...])
    size = dgu.shape[0]
    b = size // 4
    where = turned_rows(me_ref, size)
    for k in range(4):
        turned[k * b : (k + 1) * b, :] = dgu[where[k], :]
    drank = dot_nt(turned[...], expand_ref[...]).astype(BF)
    for k in range(4):
        low[where[k], :] = drank[k * b : (k + 1) * b]
    natural = low[...]
    for at in range(0, h_ref.shape[1], 256):
        cols = slice(at, at + 256)
        gshrink_ref[:, cols] += dot_tn(natural, h_ref[:, cols])
    at_first("wait", both)
    for at in range(0, h_ref.shape[1], 256):
        cols = slice(at, at + 256)
        emit(keep_ref, send_ref, cols, dot_nt(turned[...], held[cols, :]) + dot(drank, shrink_ref[:, cols]))


def attend(q, k, v, place_q, seg_q, place_k, seg_k):
    scores = dot_nt(q, k) * HD ** (-0.5)
    seen = (place_q >= place_k) & (seg_q == seg_k)
    masked = jnp.where(seen, scores, -1e30)
    top = jnp.max(masked, axis=-1, keepdims=True)
    raised = jnp.exp(masked - top)
    probs = raised * (1.0 / jnp.sum(raised, axis=-1, keepdims=True))
    low = probs.astype(BF)
    return probs, low, dot(low, v)


def attn_kernel(qkv_ref, col_ref, row_ref, o_ref):
    for start in range(0, o_ref.shape[0], TILE):
        at, seen = slice(start, start + TILE), slice(0, start + TILE)
        _, _, out = attend(
            qkv_ref[at, :HD], qkv_ref[seen, HD : 2 * HD], qkv_ref[seen, 2 * HD :],
            col_ref[at, 6:7], col_ref[at, 5:6], row_ref[1:2, seen], row_ref[0:1, seen],
        )
        o_ref[at, :] = out.astype(BF)


def attn_back_kernel(qkv_ref, col_ref, row_ref, do_ref, cos_ref, sin_ref, dqkv_ref, dk_sum, dv_sum):
    def back(turned, cos, sin):
        return ((turned * cos - pltpu.roll(turned, HD // 2, 1) * sin) * HD ** (-0.5)).astype(BF)

    dk_sum[...] = jnp.zeros_like(dk_sum)
    dv_sum[...] = jnp.zeros_like(dv_sum)
    for start in range(0, do_ref.shape[0], TILE):
        at, seen = slice(start, start + TILE), slice(0, start + TILE)
        q, k, v, do = qkv_ref[at, :HD], qkv_ref[seen, HD : 2 * HD], qkv_ref[seen, 2 * HD :], do_ref[at, :]
        probs, low, out = attend(
            q, k, v, col_ref[at, 6:7], col_ref[at, 5:6], row_ref[1:2, seen], row_ref[0:1, seen]
        )
        delta = jnp.sum(do.astype(F32) * out, axis=-1, keepdims=True)
        ds = (probs * (dot_nt(do, v) - delta)).astype(BF)
        dqkv_ref[at, :HD] = back(dot(ds, k), cos_ref[at, :], sin_ref[at, :])
        dk_sum[seen, :] += dot_tn(ds, q)
        dv_sum[seen, :] += dot_tn(low, do)
    dqkv_ref[:, HD : 2 * HD] = back(dk_sum[...], cos_ref[...], sin_ref[...])
    dqkv_ref[:, 2 * HD :] = dv_sum[...].astype(BF)


def spread(cols, first, pairs):
    rows = cols.shape[0]
    low = lax.broadcasted_iota(jnp.int32, (rows, 128), 1) < 64
    return jnp.concatenate(
        [
            jnp.where(low, cols[:, first + 2 * p : first + 2 * p + 1], cols[:, first + 2 * p + 1 : first + 2 * p + 2])
            for p in range(pairs)
        ],
        axis=1,
    )


def exact(ones, value):
    high = value.astype(BF)
    return dot(ones, high) + dot(ones, (value - high.astype(F32)).astype(BF))


def collected(value, ones):
    high = value.astype(BF)
    return dot(high, ones) + dot((value - high.astype(F32)).astype(BF), ones)


def span(pre, step, col_ref, row_ref, tri_ref, heads_ref, inner):
    count = pre.shape[0]
    states = pre.shape[1] - inner
    pairs = inner // 128
    sig = sigmoid(pre)
    conv = pre * sig
    x = conv[:, :inner]
    b = conv[:, inner : inner + states // 2].astype(BF)
    c = conv[:, inner + states // 2 :].astype(BF)
    raw = step + heads_ref[0:1, :]
    dt = jnp.maximum(raw, 0.0) + jnp.log1p(jnp.exp(-jnp.abs(raw)))
    tri = tri_ref[0]
    cum = exact(tri, -heads_ref[1:2, :] * dt)
    keep = (col_ref[:, 5:6] == row_ref[...]) & (tri > 0)
    carry, tail = col_ref[:, 4:5], col_ref[:, 0:1]
    ecum = jnp.exp(cum) * carry
    weight = jnp.exp(cum[count - 1 :, :] - cum) * tail
    turned = jnp.transpose(cum)
    decays = [
        jnp.where(keep, jnp.exp(cum[:, h : h + 1] - turned[h : h + 1, :]), 0.0) for h in range(2 * pairs)
    ]
    scores = dot_nt(c, b)
    mixing = [(scores * decay).astype(BF) for decay in decays]
    xdt = x * spread(dt, 0, pairs)
    return sig, x, b, c, raw, dt, ecum, weight, decays, mixing, xdt, pairs


def halves(value):
    low = lax.broadcasted_iota(jnp.int32, value.shape, 1) < 64
    zero = jnp.zeros_like(value)
    return jnp.concatenate([jnp.where(low, value, zero), jnp.where(low, zero, value)], axis=0)


def mamba_kernel(
    me_ref, zx_ref, zxp_ref, bc_ref, bcp_ref, step_ref, col_ref, row_ref, taps_ref, heads_ref, skip_ref, tri_ref,
    g_ref, hs_ref, pre_ref, state, ext,
):
    @pl.when(pl.program_id(0) == 0)
    def _():
        state[...] = jnp.zeros_like(state)

    count, inner = zx_ref.shape[0], zx_ref.shape[1] // 2
    ext[0:8, :inner] = zxp_ref[8:16, inner:].astype(F32)
    ext[0:8, inner:] = bcp_ref[8:16, :].astype(F32)
    ext[8:, :inner] = zx_ref[:, inner:].astype(F32)
    ext[8:, inner:] = bc_ref[...].astype(F32)
    chunk = tri_ref.shape[1]
    for k in range(count // chunk):
        at = slice(k * chunk, (k + 1) * chunk)
        pre = taps_ref[0:1, :] * ext[8 + k * chunk : 8 + (k + 1) * chunk, :]
        for tap in range(1, CONV):
            first = 8 - tap + k * chunk
            pre = pre + taps_ref[tap : tap + 1, :] * (ext[first : first + chunk, :] * col_ref[at, tap : tap + 1])
        pre_ref[at, :] = pre.astype(BF)
        _, x, b, c, _, _, ecum, weight, _, mixing, xdt, pairs = span(
            pre, step_ref[at, :], col_ref.at[at, :], row_ref.at[k], tri_ref, heads_ref, inner
        )
        old = state[...]
        held = old.astype(BF)
        hs_ref[k] = held
        low = xdt.astype(BF)
        direct = jnp.concatenate(
            [
                dot(jnp.concatenate(mixing[2 * p : 2 * p + 2], axis=1), halves(low[:, 128 * p : 128 * p + 128]))
                for p in range(pairs)
            ],
            axis=1,
        )
        wide = spread(ecum, 0, pairs)
        y = direct + dot(c, held) * wide + skip_ref[...] * x
        z = zx_ref[at, :inner].astype(F32)
        g_ref[at, :] = (y * z * sigmoid(z)).astype(BF)
        state[...] = old * wide[chunk - 1 :, :] + dot_tn(b, (xdt * spread(weight, 0, pairs)).astype(BF))


def mamba_back_kernel(
    me_ref, z_ref, pre_ref, step_ref, col_ref, row_ref, taps_ref, heads_ref, skip_ref, tri_ref, collect_ref, hs_ref, dg_ref,
    dzx_ref, dbc_ref, dstep_ref, dstate, ext, later_rows, cross,
):
    @pl.when(pl.program_id(0) == 0)
    def _():
        dstate[...] = jnp.zeros_like(dstate)
        later_rows[...] = jnp.zeros_like(later_rows)
        cross[...] = jnp.zeros_like(cross)

    chunk = tri_ref.shape[1]
    for k in reversed(range(z_ref.shape[0] // chunk)):
        at = pl.ds(k * chunk, chunk)
        mamba_back_chunk(
            z_ref.at[at, :], pre_ref.at[at, :], step_ref.at[at, :], col_ref.at[at, :], row_ref.at[k], taps_ref, heads_ref, skip_ref,
            tri_ref, collect_ref, hs_ref.at[k], dg_ref.at[at, :], dzx_ref.at[at, :], dbc_ref.at[at, :], dstep_ref.at[at, :],
            dstate, ext, later_rows, cross,
        )


def mamba_back_chunk(
    z_ref, pre_ref, step_ref, col_ref, row_ref, taps_ref, heads_ref, skip_ref, tri_ref, collect_ref, hs_ref, dg_ref,
    dzx_ref, dbc_ref, dstep_ref, dstate, ext, later_rows, cross,
):
    pre = pre_ref[...].astype(F32)
    sig, x, b, c, raw, dt, ecum, weight, decays, mixing, xdt, pairs = span(
        pre, step_ref[...], col_ref, row_ref, tri_ref, heads_ref, z_ref.shape[1]
    )
    count, inner = x.shape
    state = hs_ref[...]
    z = z_ref[...].astype(F32)
    dg = dg_ref[...].astype(F32)
    sig_z = sigmoid(z)
    dy = dg * z * sig_z
    dyl = dy.astype(BF)
    low = xdt.astype(BF)
    dst = dstate[...]
    dsl = dst.astype(BF)
    directs, dxdts = [], []
    dscores = jnp.zeros((count, count), F32)
    for p in range(pairs):
        lanes = slice(128 * p, 128 * p + 128)
        dy_two = halves(dyl[:, lanes])
        x_two = halves(low[:, lanes])
        directs.append(dot(jnp.concatenate(mixing[2 * p : 2 * p + 2], axis=1), x_two))
        dxdts.append(dot_tn(jnp.concatenate(mixing[2 * p : 2 * p + 2], axis=0), dy_two))
        dmix = dot_nt(dy_two, low[:, lanes])
        dscores = dscores + decays[2 * p] * dmix[:count] + decays[2 * p + 1] * dmix[count:]
    wide = spread(ecum, 0, pairs)
    tails = spread(weight, 0, pairs)
    core = jnp.concatenate(directs, axis=1) + dot(c, state) * wide
    dxdt = jnp.concatenate(dxdts, axis=1) + dot(b, dsl) * tails
    y = core + skip_ref[...] * x
    dz = dg * y * (sig_z * (1.0 + z * (1.0 - sig_z)))
    dsc = dscores.astype(BF)
    into = (dy * wide).astype(BF)
    dc = dot(dsc, b) + dot_nt(into, state)
    db = dot_tn(dsc, c) + dot_nt((xdt * tails).astype(BF), dsl)
    wide_dt = spread(dt, 0, pairs)
    dx = dxdt * wide_dt + skip_ref[...] * dy
    collect = collect_ref[...]
    flow = dyl.astype(F32) * core - low.astype(F32) * dxdt
    dcum = collected(flow, collect)
    rows = lax.broadcasted_iota(jnp.int32, (count, 128), 0)
    dcum = dcum + jnp.where(rows == count - 1, cross[0:1, :], 0.0)
    da = exact(tri_ref[1], dcum)
    ddt = collected(x * dxdt, collect) - heads_ref[1:2, :] * da
    lanes = lax.broadcasted_iota(jnp.int32, (count, 128), 1)
    dstep_ref[...] = jnp.where(lanes < 2 * pairs, ddt * sigmoid(raw), 0.0).astype(BF)
    dnew = dst * wide[count - 1 :, :] + dot_tn(c, into)
    dstate[...] = dnew
    held = jnp.sum(dnew * state.astype(F32), axis=0, keepdims=True)
    cross[...] = collected(jnp.broadcast_to(held, (8, inner)), collect)
    dzx_ref[:, :inner] = dz.astype(BF)
    dpre = jnp.concatenate([dx, db, dc], axis=1) * (sig * (1.0 + pre * (1.0 - sig)))
    total = taps_ref[0:1, :] * dpre
    for k in range(1, CONV):
        masked = dpre * col_ref[:, k : k + 1]
        ext[0:count, :] = masked
        ext[count:, :] = later_rows[k - 1]
        total = total + taps_ref[k : k + 1, :] * ext[k : k + count, :]
        later_rows[k - 1] = masked[0:8, :]
    dzx_ref[:, inner:] = total[:, :inner].astype(BF)
    dbc_ref[...] = total[:, inner:].astype(BF)


def whole(shape):
    return pl.BlockSpec(shape, lambda i, me: (0,) * len(shape))


def rows_of(width, rows=ROWS):
    return pl.BlockSpec((rows, width), lambda i, me: (i, 0))


ANY = pl.BlockSpec(memory_space=pl.ANY)


def params():
    return pltpu.CompilerParams(vmem_limit_bytes=VMEM)


def sds(shape, dtype):
    return jax.ShapeDtypeStruct(shape, dtype)


def half_rows(width):
    return pl.BlockSpec((ROWS // 2, width), lambda i, me: (i ^ me[1], 0))


def sems(count):
    return pltpu.SemaphoreType.DMA((count,))


def cost(macs, size):
    return pl.CostEstimate(flops=2 * macs // COST, bytes_accessed=size // COST, transcendentals=0)


def call_in(me, h, shrink, expand, cos, sin, far_kv, far_bc, parts, blocks, inner, states):
    n, d = h.shape
    r = shrink.shape[0]
    width = expand.shape[1]
    return pl.pallas_call(
        in_kernel,
        grid_spec=pltpu.PrefetchScalarGridSpec(
            num_scalar_prefetch=1,
            grid=(n // ROWS,),
            in_specs=[rows_of(d), whole((r, d)), whole((r, width)), rows_of(HD), rows_of(HD)]
            + [ANY] * (2 + len(parts)),
            out_specs=[rows_of(2 * inner), rows_of(states), rows_of(3 * HD), rows_of(128), rows_of(r)],
            scratch_shapes=[pltpu.VMEM((d, width), BF), pltpu.SemaphoreType.DMA((8, blocks))],
        ),
        out_shape=[sds((n, 2 * inner), BF), sds((n, states), BF), sds((n, 3 * HD), BF), sds((n, 128), F32), sds((n, r), BF)],
        compiler_params=params(),
        cost_estimate=cost(n * d * width, 2 * (n * d + d * width + n * width)),
        name="mixer_in",
    )(me, h, shrink, expand, cos, sin, far_kv, far_bc, *parts)


def call_in_back(me, dzx, dbc, dqkv, dstep, h, rank, shrink, expand, far_kv, far_bc, parts, blocks):
    n, d = h.shape
    r, width = expand.shape
    return pl.pallas_call(
        in_back_kernel,
        grid_spec=pltpu.PrefetchScalarGridSpec(
            num_scalar_prefetch=1,
            grid=(n // ROWS,),
            in_specs=[
                rows_of(dzx.shape[1]), rows_of(dbc.shape[1]), rows_of(3 * HD), rows_of(128), rows_of(d), rows_of(r),
                whole((r, d)), whole((r, width)),
            ]
            + [ANY] * (2 + len(parts)),
            out_specs=[half_rows(d), half_rows(d), whole((r, width)), whole((r, d))],
            scratch_shapes=[
                pltpu.VMEM((d, width), BF), pltpu.VMEM((ROWS, width), BF), pltpu.VMEM((ROWS, r), BF),
                pltpu.SemaphoreType.DMA((8, blocks)),
            ],
        ),
        out_shape=[sds((n // 2, d), BF)] * 2 + [sds((r, width), F32), sds((r, d), F32)],
        compiler_params=params(),
        cost_estimate=cost(n * d * width, 2 * (2 * n * d + d * width + n * width)),
        name="mixer_in_back",
    )(me, dzx, dbc, dqkv, dstep, h, rank, shrink, expand, far_kv, far_bc, *parts)


def call_out(me, g, o, shrink, expand, pieces, blocks):
    n, inner = g.shape
    r, d = expand.shape
    width = shrink.shape[1]
    return pl.pallas_call(
        out_kernel,
        grid_spec=pltpu.PrefetchScalarGridSpec(
            num_scalar_prefetch=1,
            grid=(n // ROWS,),
            in_specs=[rows_of(inner), rows_of(HD), whole((r, width)), whole((r, d))] + [ANY] * len(pieces),
            out_specs=[half_rows(d), half_rows(d), rows_of(r)],
            scratch_shapes=[pltpu.VMEM((d, width), BF), pltpu.VMEM((ROWS, width), BF), sems(blocks)],
        ),
        out_shape=[sds((n // 2, d), BF)] * 2 + [sds((n, r), BF)],
        compiler_params=params(),
        cost_estimate=cost(n * d * width, 2 * (n * d + d * width + n * width)),
        name="mixer_out",
    )(me, g, o, shrink, expand, *pieces)


def call_out_back(me, ml, g, o, rank, shrink, expand, pieces, blocks):
    n, inner = g.shape
    r, d = expand.shape
    width = shrink.shape[1]
    return pl.pallas_call(
        out_back_kernel,
        grid_spec=pltpu.PrefetchScalarGridSpec(
            num_scalar_prefetch=1,
            grid=(n // ROWS,),
            in_specs=[rows_of(d), rows_of(inner), rows_of(HD), rows_of(r), whole((r, width)), whole((r, d))] + [ANY] * len(pieces),
            out_specs=[rows_of(inner), rows_of(HD), whole((r, d)), whole((r, width))],
            scratch_shapes=[pltpu.VMEM((d, width), BF), sems(blocks)],
        ),
        out_shape=[sds((n, inner), BF), sds((n, HD), BF), sds((r, d), F32), sds((r, width), F32)],
        compiler_params=params(),
        cost_estimate=cost(n * d * width, 2 * (n * d + d * width + n * width)),
        name="mixer_out_back",
    )(me, ml, g, o, rank, shrink, expand, *pieces)


def call_ffn(me, h, shrink, expand, dshrink, dexpand, parts, blocks):
    n, d = h.shape
    r, both = expand.shape
    half = both // 2
    return pl.pallas_call(
        ffn_kernel,
        grid_spec=pltpu.PrefetchScalarGridSpec(
            num_scalar_prefetch=1,
            grid=(n // ROWS,),
            in_specs=[rows_of(d), whole((r, d)), whole((r, both)), whole((r, half)), whole((r, d))] + [ANY] * len(parts),
            out_specs=[half_rows(d), half_rows(d), rows_of(both), rows_of(half), rows_of(r), rows_of(r)],
            scratch_shapes=[
                pltpu.VMEM((d, both), BF), pltpu.VMEM((d, half), BF), pltpu.VMEM((ROWS, half), BF), pltpu.SemaphoreType.DMA((3, blocks))
            ],
        ),
        out_shape=[sds((n // 2, d), BF)] * 2 + [sds((n, both), BF), sds((n, half), BF), sds((n, r), BF), sds((n, r), BF)],
        compiler_params=params(),
        cost_estimate=cost(3 * n * d * half, 2 * (2 * n * d + 3 * d * half + 3 * n * half)),
        name="ffn",
    )(me, h, shrink, expand, dshrink, dexpand, *parts)


def call_ffn_back(me, dl, h, gu, q, rank, drank, shrink, expand, dshrink, dexpand, parts, blocks):
    n, d = h.shape
    r, both = expand.shape
    half = both // 2
    return pl.pallas_call(
        ffn_back_kernel,
        grid_spec=pltpu.PrefetchScalarGridSpec(
            num_scalar_prefetch=1,
            grid=(n // ROWS,),
            in_specs=[
                rows_of(d), rows_of(d), rows_of(both), rows_of(half), rows_of(r), rows_of(r),
                whole((r, d)), whole((r, both)), whole((r, half)), whole((r, d)),
            ]
            + [ANY] * len(parts),
            out_specs=[half_rows(d), half_rows(d), whole((r, d)), whole((r, both)), whole((r, half)), whole((r, d))],
            scratch_shapes=[
                pltpu.VMEM((d, both), BF), pltpu.VMEM((d, half), BF), pltpu.VMEM((ROWS, both), BF), pltpu.VMEM((ROWS, both), BF),
                pltpu.VMEM((ROWS, r), BF), pltpu.SemaphoreType.DMA((3, blocks)),
            ],
        ),
        out_shape=[sds((n // 2, d), BF)] * 2 + [sds((r, d), F32), sds((r, both), F32), sds((r, half), F32), sds((r, d), F32)],
        compiler_params=params(),
        cost_estimate=cost(3 * n * d * half, 2 * (3 * n * d + 3 * d * half + 3 * n * half)),
        name="ffn_back",
    )(me, dl, h, gu, q, rank, drank, shrink, expand, dshrink, dexpand, *parts)


def call_attn(qkv, cols, places):
    n = qkv.shape[0]
    return pl.pallas_call(
        attn_kernel,
        in_specs=[pl.BlockSpec(memory_space=pltpu.VMEM)] * 3,
        out_specs=pl.BlockSpec(memory_space=pltpu.VMEM),
        out_shape=sds((n, HD), BF),
        compiler_params=params(),
        cost_estimate=cost(2 * n * n * HD, 8 * n * HD),
        name="attend",
    )(qkv, cols, places)


def call_attn_back(qkv, cols, places, do, cos, sin):
    n = qkv.shape[0]
    return pl.pallas_call(
        attn_back_kernel,
        in_specs=[pl.BlockSpec(memory_space=pltpu.VMEM)] * 6,
        out_specs=pl.BlockSpec(memory_space=pltpu.VMEM),
        out_shape=sds((n, 3 * HD), BF),
        scratch_shapes=[pltpu.VMEM((n, HD), F32)] * 2,
        compiler_params=params(),
        cost_estimate=cost(7 * n * n * HD, 16 * n * HD),
        name="attend_back",
    )(qkv, cols, places, do, cos, sin)


def triangles(chunk):
    rows = jnp.arange(chunk, dtype=jnp.int32)
    lower = rows[:, None] >= rows[None, :]
    return jnp.stack([lower, lower.T]).astype(BF)


def call_mamba(me, zx, bc, step, cols, rows, taps, heads, skip, chunk):
    n = zx.shape[0]
    inner, states = zx.shape[1] // 2, bc.shape[1] // 2
    width = inner + 2 * states
    wide = AHEAD * chunk
    tail = wide // 16

    def here(i, me):
        return (i, 0)

    def before(i, me):
        return (jnp.maximum(i - 1, 0) * tail + tail - 1, 0)

    return pl.pallas_call(
        mamba_kernel,
        grid_spec=pltpu.PrefetchScalarGridSpec(
            num_scalar_prefetch=1,
            grid=(n // wide,),
            in_specs=[
                pl.BlockSpec((wide, 2 * inner), here),
                pl.BlockSpec((16, 2 * inner), before),
                pl.BlockSpec((wide, 2 * states), here),
                pl.BlockSpec((16, 2 * states), before),
                pl.BlockSpec((wide, 128), here),
                pl.BlockSpec((wide, 128), here),
                pl.BlockSpec((AHEAD, 1, chunk), lambda i, me: (i, 0, 0)),
                whole((8, width)),
                whole((8, 128)),
                whole((1, inner)),
                whole((2, chunk, chunk)),
            ],
            out_specs=[
                pl.BlockSpec((wide, inner), here),
                pl.BlockSpec((AHEAD, states, inner), lambda i, me: (i, 0, 0)),
                pl.BlockSpec((wide, width), here),
            ],
            scratch_shapes=[pltpu.VMEM((states, inner), F32), pltpu.VMEM((wide + 8, width), F32)],
        ),
        out_shape=[sds((n, inner), BF), sds((n // chunk, states, inner), BF), sds((n, width), BF)],
        compiler_params=params(),
        cost_estimate=cost(3 * n * inner * states, 4 * n * width),
        name="mamba",
    )(me, zx, zx, bc, bc, step, cols, rows, taps, heads, skip, triangles(chunk))


def call_mamba_back(me, zx, pre, step, cols, rows, taps, heads, skip, hs, dg, chunk):
    n = zx.shape[0]
    inner = zx.shape[1] // 2
    width = pre.shape[1]
    states = (width - inner) // 2
    wide = BACK * chunk
    count = n // wide
    collect = (jnp.arange(inner, dtype=jnp.int32)[:, None] // 64 == jnp.arange(128, dtype=jnp.int32)[None, :]).astype(BF)

    def here(i, me):
        return (count - 1 - i, 0)

    def deep(i, me):
        return (count - 1 - i, 0, 0)

    return pl.pallas_call(
        mamba_back_kernel,
        grid_spec=pltpu.PrefetchScalarGridSpec(
            num_scalar_prefetch=1,
            grid=(count,),
            in_specs=[
                pl.BlockSpec((wide, inner), here),
                pl.BlockSpec((wide, width), here),
                pl.BlockSpec((wide, 128), here),
                pl.BlockSpec((wide, 128), here),
                pl.BlockSpec((BACK, 1, chunk), deep),
                whole((8, width)),
                whole((8, 128)),
                whole((1, inner)),
                whole((2, chunk, chunk)),
                whole((inner, 128)),
                pl.BlockSpec((BACK, states, inner), deep),
                pl.BlockSpec((wide, inner), here),
            ],
            out_specs=[
                pl.BlockSpec((wide, 2 * inner), here),
                pl.BlockSpec((wide, 2 * states), here),
                pl.BlockSpec((wide, 128), here),
            ],
            scratch_shapes=[
                pltpu.VMEM((states, inner), F32),
                pltpu.VMEM((chunk + 8, width), F32),
                pltpu.VMEM((CONV - 1, 8, width), F32),
                pltpu.VMEM((8, 128), F32),
            ],
        ),
        out_shape=[sds((n, 2 * inner), BF), sds((n, 2 * states), BF), sds((n, 128), BF)],
        compiler_params=params(),
        cost_estimate=cost(10 * n * inner * states, 8 * n * width),
        name="mamba_back",
    )(me, zx, pre, step, cols, rows, taps, heads, skip, triangles(chunk), collect, hs, dg)


def place_kernel(pieces, parts, *outs):
    adapter = pl.program_id(0)
    seqs, _, width = parts[0].shape
    lane = lax.broadcasted_iota(jnp.int32, (1, 128), 1)
    hot = [
        jnp.sum(jnp.where(lane == adapter, parts[0][s, 0:1, width - 128 :].astype(F32), 0.0), axis=1, keepdims=True)
        for s in range(seqs)
    ]
    for out, rows in zip(outs, pieces):
        for k, sources in enumerate(rows):
            to = 0
            for which, start, size in sources:
                value = hot[0] * parts[which][0, :, start : start + size].astype(F32)
                for s in range(1, seqs):
                    value = value + hot[s] * parts[which][s, :, start : start + size].astype(F32)
                if len(rows) > 1:
                    out[0, 0, :, k, to : to + size] = value
                else:
                    out[0, 0, :, to : to + size] = value
                to += size


def call_place(l, layers, group, before, adapters, rank, width, inner, ff, states, kv_width):
    kv = 2 * width + states
    of = len(group) - 1
    first, second = inner + HD + 2 * inner + HD + 128, 3 * ff
    sums = kv + kv_width + (0 if of else 2 * width)
    owned = first + (0 if of else second)
    ffn = 0 if of else kv + kv_width

    def both(at, size):
        return ((0, sums + at, size), (0, sums + owned + at, size))

    def ffn_both(at, size):
        if of:
            return ((1, 2 * width + at, size), (1, 2 * width + second + at, size))
        return both(first + at, size)

    zx = inner + HD
    pieces = (
        (((0, width, width),),),
        (both(zx, inner), both(zx + inner, inner)),
        (both(zx + 2 * inner, HD),),
        (((0, 2 * width, states // 2),), ((0, 2 * width + states // 2, states // 2),)),
        (((0, kv, kv_width // 2),), ((0, kv + kv_width // 2, kv_width // 2),)),
        (both(0, inner),),
        (both(inner, HD),),
        (((0, 0, width),),),
        (((of, ffn, width),),),
        (ffn_both(0, ff), ffn_both(ff, ff)),
        (ffn_both(2 * ff, ff),),
        (((of, ffn + width, width),),),
        (((0, sums + zx + 2 * inner + HD, 128),),),
        (((0, sums + owned + zx + 2 * inner + HD, 128),),),
    )
    shapes = []
    for rows in pieces:
        size = sum(size for _, _, size in rows[0])
        shapes.append((rank, len(rows), size) if len(rows) > 1 else (rank, size))

    def block(shape):
        zeros = (0,) * len(shape)
        return pl.BlockSpec((1, 1) + shape, lambda a: (l, a) + zeros)

    def body(*refs):
        place_kernel(pieces, refs[: len(group)], *refs[len(group) + len(before) :])

    return pl.pallas_call(
        body,
        grid=(adapters,),
        in_specs=[pl.BlockSpec(array.shape, lambda a: (0, 0, 0)) for array in group] + [ANY] * len(before),
        out_specs=[block(shape) for shape in shapes],
        out_shape=[sds((layers, adapters) + shape, F32) for shape in shapes],
        input_output_aliases={len(group) + k: k for k in range(len(before))},
        compiler_params=params(),
        name="place",
    )(*group, *before)


def half_of(array, which, axis):
    size = array.shape[axis] // 2
    return lax.dynamic_slice_in_dim(array, which * size, size, axis)


def on_device(
    dp_axes,
    tokens,
    out_grad,
    doc_lengths,
    adapter_ids,
    mixer_gain,
    ffn_gain,
    ssm_in,
    step_proj,
    query_proj,
    state_proj,
    keyval_proj,
    conv_inner,
    conv_state,
    decay_log,
    step_bias,
    skip_gain,
    ssm_out,
    attn_out,
    gate_up,
    down_proj,
    mixer_shrink,
    inner_expand,
    step_expand,
    query_expand,
    state_expand,
    keyval_expand,
    ssmout_shrink,
    attnout_shrink,
    mixer_expand,
    ffn_shrink,
    gateup_expand,
    down_shrink,
    down_expand,
):
    layers = ssm_in.shape[0]
    zh, zl, ta, tb = (lax.axis_index(a) for a in ("zh", "zl", "ta", "tb"))
    me_w = zh * 2 + zl
    for k, axis in enumerate(dp_axes):
        me_w = me_w + lax.axis_index(axis) * (4 << k)
    me = jnp.stack([me_w, ta, zl, tb]).astype(jnp.int32)
    block, width = tokens.shape[1:]
    n = block * 4
    share = n // 8
    chunk = share
    heads = step_proj.shape[2] // 2
    inner = ssm_in.shape[3] // 2
    states = 2 * state_proj.shape[3]
    rank = mixer_shrink.shape[3]
    local = ssm_in.shape[1]
    ff = gate_up.shape[3] // 2

    def own_stages(array, *tokens):
        mine = half_of(array, tb, 1)
        keep = lax.dynamic_index_in_dim(mine, zh, 0, False)
        away = lax.dynamic_index_in_dim(mine, 1 - zh, 0, False)
        rows = away.shape[0] // 2
        got = swap(later(jnp.where(zh == ta, away[:rows], away[rows:]), *tokens), "zh")
        tokens = yield [got]
        beside = swap(later(got, *tokens), "ta")
        yield [beside]
        return jnp.where(zh == ta, keep, jnp.concatenate([got, beside], axis=0))

    def all_stages(own, dtype, *tokens):
        own = later(own, *tokens)
        got = lax.ppermute(own, ("zh", "ta"), [(2, 0), (1, 3)])
        near = swap(own, "ta")
        tokens = yield [got, near]
        same = jnp.where(zh == ta, own, near)
        got = later(got, *tokens)
        across = swap(got, "ta")
        tokens = yield [across]
        other = jnp.where(zh == ta, got, across)
        pair = later(jnp.where(zh == 0, jnp.stack([same, other]), jnp.stack([other, same])), *tokens)
        far = swap(pair, "tb")
        yield [far]
        full = jnp.where(tb == 0, jnp.concatenate([pair, far], axis=1), jnp.concatenate([far, pair], axis=1))
        return full.astype(dtype)

    def ordered(axis, own, got, along):
        here = lax.axis_index(axis) == 0
        return jnp.where(here, jnp.concatenate([own, got], axis=along), jnp.concatenate([got, own], axis=along))


    def takes(name, l, tie):
        def cut(array, starts, sizes):
            return lax.dynamic_slice(array, (l,) + starts, (1,) + sizes).reshape(tuple(k for k in sizes if k > 1))

        def pick(which):
            if name in ("a", "b"):
                k = 0 if name == "a" else 1
                left = cut(arrays[0], (0, k, which * inner), (local, 1, inner))
                if name == "a":
                    return [left, cut(arrays[1], (0, which * HD), (local, HD))]
                return [left, cut(arrays[1], (0, tb, ta * HD), (local, 1, HD))]
            if name == "c":
                step = cut(arrays[1], (0, which * heads), (local, heads))
                return [cut(arrays[0], (0, tb, 0), (local, 1, states // 2)), jnp.pad(step, ((0, 0), (0, 128 - heads)))]
            if name == "out":
                return [cut(arrays[0], (which * inner, 0), (inner, local)).T, cut(arrays[1], (which * HD, 0), (HD, local)).T]
            if name == "down":
                return [cut(arrays[0], (which * ff, 0), (ff, local)).T]
            return [cut(arrays[0], (0, 0 if name == "gate" else 1, which * ff), (local, 1, ff))]

        sources = {
            "a": (ssm_in, query_proj), "b": (ssm_in, keyval_proj), "c": (state_proj, step_proj), "out": (ssm_out, attn_out),
            "gate": (gate_up,), "up": (gate_up,), "down": (down_proj,),
        }
        arrays = tie(*sources[name])
        return pick

    own, sent, near, pair, far_z, got = ({} for _ in range(6))
    last = {}

    def gathered(keys, *tokens):
        def tie(*values):
            return tied(*values, *tokens)[: len(values)] if tokens else values

        picks = [takes(*key, tie) for key in keys]
        mine, away = (jnp.concatenate([c for pick in picks for c in pick(which)], axis=1) for which in (zl, 1 - zl))
        return keys, mine, away

    def exchange(group, *tokens):
        keys, mine, away = group
        moved = swap(later(away, *tokens), "zl")
        at = 0
        for key in keys:
            size = widths[key[0]]
            own[key], near[key] = mine[:, at : at + size], moved[:, at : at + size]
            at += size
        return moved

    def prepare(keys, *tokens):
        return exchange(gathered(keys, *tokens))

    def order(way):
        return (last[way],) if way in last else ()

    def send_zh(key, *tokens, parts=1):
        pair[key] = later(jnp.concatenate([own[key], near[key]], axis=0), *order("zh"), *tokens)
        if parts == 1:
            far_z[key] = last["zh"] = swap(pair[key], "zh")
            return
        moved = []
        for part in jnp.split(pair[key], parts, axis=0):
            moved.append(swap(later(part, *moved[-1:]), "zh"))
        far_z[key] = jnp.concatenate(moved, axis=0)
        last["zh"] = moved[-1]

    def send_dp(key, *tokens):
        held, moved = pair[key], far_z[key]
        for axis in dp_axes:
            held = later(jnp.concatenate([held, moved], axis=0), *order("dp"), *tokens)
            moved = last["dp"] = swap(held, axis)
        got[key] = (held, moved)

    blocks = 4 << len(dp_axes)
    chain = [(name, 0) for name in ("a", "b", "c", "out", "gate", "up", "down")]
    for l in range(1, layers):
        chain += [(name, l) for name in ("a", "c", "b", "out", "gate", "up", "down")]
    widths = {
        "a": inner + HD, "b": inner + HD, "c": states // 2 + 128, "out": inner + HD, "gate": ff, "up": ff, "down": ff
    }
    first = prepare(chain[:1])
    second = prepare(chain[1:3], first)
    for key in chain[:3]:
        send_zh(key)
    for key in chain[:3]:
        send_dp(key)
    third = prepare(chain[3:5], far_z[chain[0]])
    send_zh(chain[3])
    late = gathered(chain[5:7], far_z[chain[1]], third)
    moved = [5]
    arrived = [far_z[chain[3]], *late[1:]]
    ahead = {1: (0, 3), 4: (3, 7)}
    groups = {}

    def ready_for(l, w, *tokens):
        if l + 1 < layers:
            start, end = ahead[w]
            groups[l, w] = gathered(chain[7 * l + 7 + start : 7 * l + 7 + end], *tokens)
            arrived.extend(groups[l, w][1:])

    def window(value, *tokens, parts=1, early=False):
        out = later(value, *arrived, *tokens)
        before = tuple(a for group in groups.values() for a in group[1:] if any(a is b for b in arrived)) if early else tokens
        arrived.clear()
        k = moved[0]
        moved[0] += 1
        if k - 1 < len(chain):
            send_zh(chain[k - 1], *tokens, parts=parts)
            arrived.append(last["zh"])
        if k - 2 < len(chain):
            send_dp(chain[k - 2], *before)
            arrived.append(got[chain[k - 2]][1])
        if k == 5:
            arrived.append(exchange(late, *tokens))
        for w in ahead:
            l, rest = divmod(k - 5 - w, 7)
            if not rest and (l, w) in groups:
                arrived.append(exchange(groups[l, w], *tokens))
        return out

    def step_window(value, tokens, *stages):
        out = later(value, *arrived, *tokens)
        arrived.clear()
        for stage in stages:
            arrived.extend(stage.start(*tokens) or ())
        return out


    def mixer_weights(l):
        def both(key, start, size):
            return swap(jnp.concatenate([part[:, start : start + size] for part in got[key]], axis=0), "tb")

        parts = got["a", l] + got["b", l] + got["c", l]
        return both(("b", l), inner, HD), both(("c", l), 0, states // 2), parts, blocks

    lengths = lax.dynamic_index_in_dim(doc_lengths, zh, 0, False)
    aid = lax.dynamic_index_in_dim(adapter_ids, zh, 0, False)
    lengths, positions = tied(lengths, jnp.arange(n, dtype=jnp.int32), far_z["a", 0])[:2]
    seg = segment_of(positions, lengths)
    seg_back = [segment_of(positions - k, lengths) for k in range(1, CONV)]
    starts = (positions // chunk) * chunk
    seg_start = segment_of(starts - 1, lengths)
    seg_end = segment_of(starts + chunk - 1, lengths)
    cols = jnp.stack(
        [(seg == seg_end).astype(F32)]
        + [(seg == s).astype(F32) for s in seg_back]
        + [(seg == seg_start).astype(F32), seg.astype(F32), positions.astype(F32)],
        axis=1,
    )
    cols = jnp.pad(cols, ((0, 0), (0, 128 - cols.shape[1])))
    rows = seg.astype(F32).reshape(n // chunk, 1, chunk)
    places = jnp.pad(jnp.stack([seg.astype(F32), positions.astype(F32)]), ((0, 6), (0, 0)))
    freqs = ROPE_BASE ** (-jnp.arange(HD // 2, dtype=F32) / (HD // 2))
    angles = positions.astype(F32)[:, None] * freqs[None, :]
    cos = jnp.tile(jnp.cos(angles), (1, 2))
    sin = jnp.sin(angles)
    sin = jnp.concatenate([-sin, sin], axis=1)

    def small_of(l, token):
        aid_now = tied(aid, token)[0]

        def pick(table):
            zeros = (0,) * (table.ndim - 2)
            return lax.dynamic_slice(table, (l, aid_now) + zeros, (1, 1) + table.shape[2:]).reshape(table.shape[2:])

        def flat(table):
            return pick(table).T

        inner_e, keyval_e = pick(inner_expand), pick(keyval_expand)
        expand_in = jnp.concatenate(
            [
                half_of(inner_e[:, 0], zl, 1),
                half_of(inner_e[:, 1], zl, 1),
                half_of(pick(query_expand), zl, 1),
                lax.dynamic_slice_in_dim(keyval_e[:, 0], ta * HD, HD, 1),
                lax.dynamic_slice_in_dim(keyval_e[:, 1], ta * HD, HD, 1),
                jnp.pad(half_of(pick(step_expand), zl, 1), ((0, 0), (0, 128 - heads))),
                pick(state_expand).reshape(rank, -1),
            ],
            axis=1,
        )
        shrink_out = jnp.concatenate([half_of(flat(ssmout_shrink), zl, 1), half_of(flat(attnout_shrink), zl, 1)], axis=1)
        gate_e = pick(gateup_expand)
        expand_gu = jnp.concatenate([half_of(gate_e[:, 0], zl, 1), half_of(gate_e[:, 1], zl, 1)], axis=1)
        shrink_down = half_of(flat(down_shrink), zl, 1)
        taps = jnp.pad(
            jnp.concatenate([half_of(conv_inner[l], zl, 1), conv_state[l].reshape(CONV, -1)], axis=1), ((0, 8 - CONV), (0, 0))
        )
        head_rows = jnp.pad(
            jnp.stack([half_of(step_bias[l], zl, 0), jnp.exp(half_of(decay_log[l], zl, 0))]), ((0, 6), (0, 128 - heads))
        )
        skip = jnp.repeat(half_of(skip_gain[l], zl, 0), inner // heads)[None, :]
        return (
            flat(mixer_shrink), expand_in, shrink_out, pick(mixer_expand), flat(ffn_shrink), expand_gu, shrink_down,
            pick(down_expand), taps, head_rows, skip,
        )

    weights, small, saved = [], [], []
    resid = Stages(own_stages(tied(tokens, near["a", 0])[0])).finish().astype(F32)
    grad_stages = None
    token = far_z["a", 0]
    for l in range(layers):
        small.append(small_of(l, token))
        shrink_in, expand_in, shrink_out, expand_out, shrink_gu, expand_gu, shrink_down, expand_down, taps, head_rows, skip = small[l]
        if l:
            gain = window(mixer_gain[l], resid)
            if grad_stages is not None and l + 1 == layers:
                arrived.extend(grad_stages.start(resid))
        else:
            gain = later(mixer_gain[l], far_z["c", l], got["b", l][1], third, cols, cos, sin, places, rows, *small[l])
        h = gather_tokens(rms_norm(resid, gain).astype(BF))
        w_in = mixer_weights(l)
        if not l:
            ready_for(l, 1, far_z["c", l])
        zx, bc, qkv, step, rank_in = call_in(window(me, h, early=bool(l)), h, shrink_in, expand_in, cos, sin, *w_in, inner, states)
        if l + 1 == layers:
            grad = (grad_stages or Stages(own_stages(out_grad))).finish().astype(F32)
            top_grad = gather_tokens(grad.astype(BF))
        g, hs, pre = call_mamba(window(me, rank_in), zx, bc, step, cols, rows, taps, head_rows, skip, chunk)
        o = call_attn(qkv, cols, places)
        w_out = (got["out", l], blocks)
        keep, send, rank_out = call_out(me, g, o, shrink_out, expand_out, *w_out)
        mid = resid + scatter_tokens(keep, window(send, rank_out, parts=2))
        if l + 1 == layers:
            arrived.append(top_grad)
        token = mid
        h2 = gather_tokens(rms_norm(mid, window(ffn_gain[l], mid)).astype(BF))
        ready_for(l, 4, mid)
        w_ffn = (got["gate", l] + got["up", l] + got["down", l], blocks)
        keep, send, gu, q, rank_gu, rank_down = call_ffn(window(me, h2, early=True), h2, shrink_gu, expand_gu, shrink_down, expand_down, *w_ffn)
        if l + 1 < layers:
            send = window(send, rank_down, parts=2)
            if l + 2 == layers:
                grad_stages = Stages(own_stages(out_grad, last["zh"]))
                arrived.extend(grad_stages.start())
            resid_next = mid + scatter_tokens(keep, send)
        else:
            final = Stages(scatter_stages(keep, send))
        weights.append((w_in, w_out, w_ffn))
        saved.append((resid, mid, h, zx, pre, qkv, step, rank_in, g, hs, o, rank_out, h2, gu, q, rank_gu, rank_down))
        resid = resid_next

    seq_axes = tuple(reversed(dp_axes)) + ("zh",)
    adapters = mixer_shrink.shape[1]
    hot = jnp.pad((aid == jnp.arange(adapters, dtype=jnp.int32)).astype(BF), (0, 128 - adapters))
    hot = jnp.broadcast_to(hot[None], (rank, 128))

    def sum_stages(partial, owned, *tokens):
        mine = jnp.concatenate(partial, axis=1).astype(BF)
        size = mine.shape[1]
        for axis in ("tb", "ta"):
            mine = later(mine, *tokens)
            moved = swap(mine, axis)
            tokens = yield [moved]
            mine = (mine.astype(F32) + moved.astype(F32)).astype(BF)
        mine = later(jnp.concatenate([mine] + [value.astype(BF) for value in owned], axis=1), *tokens)
        moved = swap(mine, "zl")
        tokens = yield [moved]
        total = (mine[:, :size].astype(F32) + moved[:, :size].astype(F32)).astype(BF)
        held = jnp.concatenate([total, ordered("zl", mine[:, size:], moved[:, size:], 1), hot], axis=1)[None]
        for axis in ("zh",) + dp_axes:
            held = later(held, *tokens)
            moved = swap(held, axis)
            tokens = yield [moved]
            held = jnp.concatenate([held, moved], axis=0)
        return (held,)

    def place(l, group, tables):
        return call_place(l, layers, group, tables, adapters, rank, width, inner, ff, states, 2 * keyval_proj.shape[3])

    sums = [None] * layers
    at = 2 * inner
    out_stages, older = None, None
    for l in reversed(range(layers)):
        shrink_in, expand_in, shrink_out, expand_out, shrink_gu, expand_gu, shrink_down, expand_down, taps, head_rows, skip = small[l]
        w_in, w_out, w_ffn = weights[l]
        resid, mid, h, zx, pre, qkv, step, rank_in, g, hs, o, rank_out, h2, gu, q, rank_gu, rank_down = saved[l]
        top = l == layers - 1
        dl = top_grad if top else gather_tokens(grad.astype(BF))
        if top:
            now = step_window(me, (dl, rank_down), final)
        else:
            now = step_window(me, (dl,), out_stages, older)
        keep, send, g_shrink_gu, g_expand_gu, g_shrink_down, g_expand_down = call_ffn_back(
            now, dl, h2, gu, q, rank_gu, rank_down, shrink_gu, expand_gu, shrink_down, expand_down, *w_ffn
        )
        of_ffn = [g_shrink_gu, g_expand_down], [g_expand_gu, g_shrink_down]
        if not l:
            rest = Stages(sum_stages(*of_ffn))
        send = step_window(send, (g_expand_gu,), *(() if top else (older,)), *(() if l else (rest,)))
        d_mid = scatter_tokens(keep, send)
        grad = grad + norm_back(mid, step_window(ffn_gain[l], (d_mid,), *(() if l else (rest, rest))), d_mid)
        ml = gather_tokens(grad.astype(BF))
        now = step_window(me, (ml,), *((final,) if top else (out_stages,)), *(() if l else (rest,)))
        dg, do, g_expand_out, g_shrink_out = call_out_back(now, ml, g, o, rank_out, shrink_out, expand_out, *w_out)
        dqkv = call_attn_back(qkv, cols, places, do, cos, sin)
        now = step_window(me, (dqkv,), *((final,) if top else ()), *(() if l else (rest,)))
        dzx, dbc, dstep = call_mamba_back(now, zx, pre, step, cols, rows, taps, head_rows, skip, hs, dg, chunk)
        if top:
            output = mid + final.finish()
            out_stages = Stages(all_stages(output.astype(BF), BF, dstep))
            now = step_window(me, (dstep,), out_stages)
        else:
            now = step_window(me, (dstep,))
        keep, send, g_expand_in, g_shrink_in = call_in_back(
            now, dzx, dbc, dqkv, dstep, h, rank_in, shrink_in, expand_in, *w_in
        )
        send = step_window(send, (g_expand_in,))
        kv = jnp.zeros((rank, 2, keyval_proj.shape[3]), F32)
        own_kv = jnp.stack([g_expand_in[:, at + HD : at + 2 * HD], g_expand_in[:, at + 2 * HD : at + 3 * HD]], axis=1)
        kv = lax.dynamic_update_slice_in_dim(kv, own_kv, ta * HD, 2).reshape(rank, -1)
        partial = [g_expand_out, g_shrink_in, g_expand_in[:, at + 3 * HD + 128 :], kv]
        owned = [g_shrink_out, g_expand_in[:, : at + HD], g_expand_in[:, at + 3 * HD : at + 3 * HD + 128]]
        last_sum = Stages(scatter_stages(keep, send))
        for _ in range(3):
            summed = last_sum.start()
        d_resid = last_sum.finish()
        grad = grad + norm_back(resid, mixer_gain[l], d_resid)
        if l:
            older = sums[l] = Stages(sum_stages(partial + of_ffn[0], owned + of_ffn[1], d_resid))
            for _ in range(3):
                arrived[:] = older.start()
        else:
            sums[l] = Stages(sum_stages(partial, owned))
            for _ in range(4):
                moving = sums[l].start()
    output = out_stages.finish()
    last_grad = Stages(all_stages(grad.astype(BF), F32, *moving))
    last_grad.start()
    tables = ()
    for k in reversed(range(1, layers)):
        tables = place(k, tied(*sums[k].finish(), *summed)[:-2], tables)
    last_grad.start(*tables[-1:])

    tables = place(0, sums[0].finish() + rest.finish(), tables)
    last_grad.start(*tables[-1:])
    input_grad = last_grad.finish()

    def turned(value):
        return jnp.swapaxes(value, 2, 3)

    (
        mixshrink, innerexpand, queryexpand, stateexpand, keyvalexpand, ssmshrink, attnshrink, mixexpand, ffnshrink, gateexpand,
        downshrink, downexpand, step_low, step_high,
    ) = tables
    return (
        output,
        input_grad,
        turned(mixshrink),
        innerexpand,
        jnp.concatenate([step_low[..., :heads], step_high[..., :heads]], axis=-1),
        queryexpand,
        stateexpand,
        keyvalexpand,
        turned(ssmshrink),
        turned(attnshrink),
        mixexpand,
        turned(ffnshrink),
        gateexpand,
        turned(downshrink),
        downexpand,
    )


def solution(mesh):
    dp, ctx, tensor = (mesh.shape[a] for a in ("dp", "ctx", "tensor"))
    bits = dp.bit_length() - 1
    dp_names = tuple("d%d" % k for k in reversed(range(bits)))
    inside = Mesh(
        mesh.devices.reshape((2,) * bits + (2, ctx // 2, 2, tensor // 2)), dp_names + ("zh", "zl", "ta", "tb")
    )
    dp_axes = tuple(reversed(dp_names))
    d, c, t = dp_names, ("zh", "zl"), ("ta", "tb")
    dc = dp_names + c
    return jax.shard_map(
        functools.partial(on_device, dp_axes),
        mesh=inside,
        in_specs=(
            P(d, c, None),
            P(d, c, None),
            P(d, None),
            P(d),
            P(),
            P(),
            P(None, dc, None, t),
            P(None, dc, t),
            P(None, dc, t),
            P(None, dc, None, None),
            P(None, dc, None, None),
            P(None, None, t),
            P(),
            P(None, t),
            P(None, t),
            P(None, t),
            P(None, t, dc),
            P(None, t, dc),
            P(None, dc, None, t),
            P(None, t, dc),
            P(),
            P(None, None, None, None, t),
            P(None, None, None, t),
            P(None, None, None, t),
            P(),
            P(),
            P(None, None, t, None),
            P(None, None, t, None),
            P(),
            P(),
            P(None, None, None, None, t),
            P(None, None, t, None),
            P(),
        ),
        out_specs=(
            P(d, c, None),
            P(d, c, None),
            P(),
            P(None, None, None, None, t),
            P(None, None, None, t),
            P(None, None, None, t),
            P(),
            P(),
            P(None, None, t, None),
            P(None, None, t, None),
            P(),
            P(),
            P(None, None, None, None, t),
            P(None, None, t, None),
            P(),
        ),
        check_vma=False,
    )
```
